128 devices in a mesh: seq: 2 (over z_hi), dp: 64 (over y, x, z_lo, core).
Axes of the slice: x: 4, y: 4, z: 4 (z_hi: 2, z_lo: 2; z = z_hi * 2 + z_lo), core: 2. Of those that a mesh axis runs over, the one named last changes fastest.
Arguments:
- inputs: bfloat16 [64, 1536, 768], P('dp', 'seq'), may hold values from -6 to 6
- segments: int32 [64, 1536], P('dp', 'seq'), may hold values from 0 to 3, as said below
- w_query: bfloat16 [768, 768], P(('seq', 'dp')), may hold values from -0.21875 to 0.21875
- w_key: bfloat16 [768, 768], P(('seq', 'dp')), may hold values from -0.21875 to 0.21875
- w_value: bfloat16 [768, 768], P(('seq', 'dp')), may hold values from -0.21875 to 0.21875
- w_output: bfloat16 [768, 768], P(('seq', 'dp')), may hold values from -6 to 6
- b_query: bfloat16 [768], P(('seq', 'dp')), may hold values from -3 to 3
- b_value: bfloat16 [768], P(('seq', 'dp')), may hold values from -0.15625 to 0.15625
- b_output: bfloat16 [768], P(('seq', 'dp')), may hold values from -3 to 3
- gain_attn: bfloat16 [768], P(('seq', 'dp')), may hold values from 0.099609375 to 1.8984375
- bias_attn: bfloat16 [768], P(('seq', 'dp')), may hold values from -3 to 3
- w_inner: bfloat16 [768, 3072], P(('seq', 'dp')), may hold values from -0.21875 to 0.21875
- b_inner: bfloat16 [3072], P(('seq', 'dp')), may hold values from -3 to 3
- w_outer: bfloat16 [3072, 768], P(('seq', 'dp')), may hold values from -0.109375 to 0.109375
- b_outer: bfloat16 [768], P(('seq', 'dp')), may hold values from -3 to 3
- gain_out: bfloat16 [768], P(('seq', 'dp')), may hold values from 0.099609375 to 1.8984375
- bias_out: bfloat16 [768], P(('seq', 'dp')), may hold values from -3 to 3
- cotangent: bfloat16 [64, 1536, 768], P('dp', 'seq'), may hold values from -6 to 6
Outputs:
- output: bfloat16 [64, 1536, 768], P('dp', 'seq')
- grad_input: float32 [64, 1536, 768], P('dp', 'seq')
- grad_w_query: float32 [768, 768], P(('seq', 'dp'))
- grad_w_key: float32 [768, 768], P(('seq', 'dp'))
- grad_w_value: float32 [768, 768], P(('seq', 'dp'))
- grad_w_output: float32 [768, 768], P(('seq', 'dp'))
- grad_b_query: float32 [768], P(('seq', 'dp'))
- grad_b_value: float32 [768], P(('seq', 'dp'))
- grad_b_output: float32 [768], P(('seq', 'dp'))
- grad_gain_attn: float32 [768], P(('seq', 'dp'))
- grad_bias_attn: float32 [768], P(('seq', 'dp'))
- grad_w_inner: float32 [768, 3072], P(('seq', 'dp'))
- grad_b_inner: float32 [3072], P(('seq', 'dp'))
- grad_w_outer: float32 [3072, 768], P(('seq', 'dp'))
- grad_b_outer: float32 [768], P(('seq', 'dp'))
- grad_gain_out: float32 [768], P(('seq', 'dp'))
- grad_bias_out: float32 [768], P(('seq', 'dp'))
The draws below stay inside these ranges and needn't reach their ends.
Inputs may be any that keep to these rules, and one draw needn't show every extreme that they name: `segments`: in each sequence the numbers never fall, begin at 0 and end at 3; one document covers at least positions 384 to 1151.
All inputs are finite; a program needn't handle non-finite values.
Results may differ from the reference program's by a relative error of at most 0.019.
Values may be sent and summed in bfloat16 or wider, within the bound.
A program may use at most 256 MiB of HBM per device.

```python
import math
import jax
import jax.numpy as jnp
from jax import lax

D = 768
HEADS = 12
FF = 3072
HALF_WIN = 512
TOK_DEV = 768
SEQ_LEN = 1536
SEQS = 64


def draw_segments(key, part):
    key = jax.random.fold_in(key, 11)
    key_early = jax.random.fold_in(key, 1)
    key_late = jax.random.fold_in(key, 2)
    early_cut = jax.random.randint(key_early, (SEQS, 2), 1, TOK_DEV // 2 + 1)
    late_cut = jax.random.randint(key_late, (SEQS, 1), TOK_DEV + TOK_DEV // 2, SEQ_LEN)
    cut_points = jnp.concatenate([early_cut, late_cut], axis=1).astype(jnp.int32)
    positions = jnp.arange(SEQ_LEN, dtype=jnp.int32)
    passed = (positions[None, :, None] >= cut_points[:, None, :]).astype(jnp.int32)
    return jnp.sum(passed, axis=2).astype(jnp.int32)


def shard_levels(own_key, dims, cuts, least, high):
    gain = 1.0
    for position, parts in cuts:
        steps = jax.random.uniform(jax.random.fold_in(jax.random.fold_in(own_key, 6), position), (parts,), jnp.float32, least / len(cuts), high / len(cuts))
        gain = gain * jnp.repeat(jnp.exp(steps), dims[position] // parts).reshape((-1,) + (1,) * (len(dims) - 1 - position))
    return gain


def noise(key, shape, scale, most, shards=(), held_as=jnp.bfloat16):
    drawn = scale * jax.random.normal(key, shape, jnp.float32)
    if shards:
        drawn = drawn * shard_levels(key, shape, shards, -0.22, 0.18)
    return jnp.clip(drawn, -most, most).astype(held_as)


def setup_inputs(seed: int = 0) -> dict:
    streams_of = jax.random.split(jax.random.key(seed), 19)
    inputs = noise(streams_of[0], (SEQS, SEQ_LEN, D), 1.0, 6.0, ((0, 64), (1, 2)))
    segments = draw_segments(jax.random.fold_in(streams_of[18], 71), 0)
    w_query = noise(streams_of[2], (D, D), D ** -0.5, 0.21875, ((0, 128),))
    w_key = noise(streams_of[3], (D, D), D ** -0.5, 0.21875, ((0, 128),))
    w_value = noise(streams_of[4], (D, D), D ** -0.5, 0.21875, ((0, 128),))
    w_output = noise(streams_of[5], (D, D), (max(1, D // (2 * HALF_WIN))) ** -0.5, 6.0, ((0, 128),))
    b_query = noise(streams_of[6], (D,), 0.5, 3.0, ((0, 128),))
    b_value = noise(streams_of[7], (D,), (0.7 * max(1, D // (2 * HALF_WIN)) ** 0.5 * D ** -0.5), 0.15625, ((0, 128),))
    b_output = noise(streams_of[8], (D,), 0.5, 3.0, ((0, 128),))
    gain_attn = jnp.clip(1.0 + 0.18 * jax.random.normal(streams_of[9], (D,), jnp.float32), 0.099609375, 1.8984375).astype(jnp.bfloat16)
    bias_attn = noise(streams_of[10], (D,), 0.5, 3.0, ((0, 128),))
    w_inner = noise(streams_of[11], (D, FF), D ** -0.5, 0.21875, ((0, 128),))
    b_inner = noise(streams_of[12], (FF,), 0.5, 3.0, ((0, 128),))
    w_outer = noise(streams_of[13], (FF, D), FF ** -0.5, 0.109375, ((0, 128),))
    b_outer = noise(streams_of[14], (D,), 0.5, 3.0, ((0, 128),))
    gain_out = jnp.clip(1.0 + 0.18 * jax.random.normal(streams_of[15], (D,), jnp.float32), 0.099609375, 1.8984375).astype(jnp.bfloat16)
    bias_out = noise(streams_of[16], (D,), 0.5, 3.0, ((0, 128),))
    cotangent = noise(streams_of[17], (SEQS, SEQ_LEN, D), 1.0, 6.0, ((0, 64), (1, 2)))
    return {"inputs": inputs, "segments": segments, "w_query": w_query, "w_key": w_key, "w_value": w_value, "w_output": w_output, "b_query": b_query, "b_value": b_value, "b_output": b_output, "gain_attn": gain_attn, "bias_attn": bias_attn, "w_inner": w_inner, "b_inner": b_inner, "w_outer": w_outer, "b_outer": b_outer, "gain_out": gain_out, "bias_out": bias_out, "cotangent": cotangent}


EPS = 1e-12
NEG_FILL = -1e+30

@jax.custom_vjp
def low(v):
    return lax.optimization_barrier(v.astype(jnp.bfloat16)).astype(jnp.float32)

@jax.custom_vjp
def low_back(v):
    return v

def low_keep(v):
    return (low(v), None)

def low_pass(kept, grad):
    return (grad,)

def back_keep(v):
    return (v, None)

def back_low(kept, grad):
    return (low(grad),)
low.defvjp(low_keep, low_pass)
low_back.defvjp(back_keep, back_low)

def both_ways(tensor):
    return low_back(low(tensor))

def high_dot(mat_one, mat_two):
    return jnp.dot(mat_one, mat_two, precision=lax.Precision.HIGHEST)

def layer_norm(hidden, scales, offset):
    average = lax.optimization_barrier(jnp.mean(hidden, axis=-1, keepdims=True))
    centred = hidden - average
    variance = lax.optimization_barrier(jnp.mean(centred * centred, axis=-1, keepdims=True))
    return centred * lax.rsqrt(variance + EPS) * scales + offset

def attend_sequence(query_rows, key_rows, value_rows, seg_rows):
    seq_len = query_rows.shape[0]
    head_size = query_rows.shape[2]
    block_rows = math.gcd(seq_len, 512)
    blocks = seq_len // block_rows
    places = jnp.arange(seq_len, dtype=jnp.int32)
    scaling = head_size ** (-0.5)

    def one_block(pieces):
        query_blk, pos_blk, seg_blk = pieces
        scores = jnp.einsum('qhd,khd->hqk', query_blk, key_rows, precision=lax.Precision.HIGHEST) * scaling
        scores = low_back(scores)
        same_doc = seg_blk[:, None] == seg_rows[None, :]
        within_reach = jnp.abs(pos_blk[:, None] - places[None, :]) <= HALF_WIN
        scores = jnp.where((same_doc & within_reach)[None], scores, NEG_FILL)
        probs = jax.nn.softmax(scores, axis=-1)
        return jnp.einsum('hqk,khd->qhd', low(probs), value_rows, precision=lax.Precision.HIGHEST)
    block_out = lax.map(jax.checkpoint(one_block), (query_rows.reshape(blocks, block_rows, HEADS, head_size), places.reshape(blocks, block_rows), seg_rows.reshape(blocks, block_rows)))
    return block_out.reshape(seq_len, HEADS, head_size)

def layer_group(x_group, seg_group, params):
    w_query, w_key, w_value, w_output, b_query, b_value, b_output, gain_attn, bias_attn, w_inner, b_inner, w_outer, b_outer, gain_out, bias_out = params
    seq_count, seq_len, model_width = x_group.shape
    head_size = model_width // HEADS
    tokens = x_group.reshape(seq_count * seq_len, model_width)
    query = both_ways(high_dot(tokens, w_query) + b_query)
    key_vals = both_ways(high_dot(tokens, w_key))
    value_vals = both_ways(high_dot(tokens, w_value) + b_value)

    def to_heads(matrix):
        return matrix.reshape(seq_count, seq_len, HEADS, head_size)
    attended = jax.vmap(attend_sequence)(to_heads(query), to_heads(key_vals), to_heads(value_vals), seg_group)
    mixed = both_ways(attended.reshape(seq_count * seq_len, model_width))
    branch = low_back(high_dot(mixed, w_output) + b_output)
    first = layer_norm(tokens + branch, gain_attn, bias_attn)
    inner = low_back(high_dot(low(first), w_inner) + b_inner)
    active = jax.nn.gelu(inner, approximate=True)
    outer = low_back(high_dot(low(active), w_outer) + b_outer)
    result = layer_norm(first + outer, gain_out, bias_out)
    return result.reshape(seq_count, seq_len, model_width)

def reference(inputs, segments, w_query, w_key, w_value, w_output, b_query, b_value, b_output, gain_attn, bias_attn, w_inner, b_inner, w_outer, b_outer, gain_out, bias_out, cotangent):
    params = tuple((weight_arr.astype(jnp.float32) for weight_arr in (w_query, w_key, w_value, w_output, b_query, b_value, b_output, gain_attn, bias_attn, w_inner, b_inner, w_outer, b_outer, gain_out, bias_out)))
    limit = min(SEQS, max(1, 4096 // SEQ_LEN))
    per_step = max((count for count in range(1, limit + 1) if SEQS % count == 0))
    step_count = SEQS // per_step
    seg_steps = segments.reshape(step_count, per_step, SEQ_LEN)

    def forward(x_all, weight_set):
        x_steps = x_all.reshape(step_count, per_step, SEQ_LEN, D)

        def step_fn(carry, pieces):
            return (carry, layer_group(pieces[0], pieces[1], weight_set))
        _, results = lax.scan(jax.checkpoint(step_fn), jnp.zeros((), jnp.float32), (x_steps, seg_steps))
        return results.reshape(SEQS, SEQ_LEN, D)
    result, pullback = jax.vjp(forward, inputs.astype(jnp.float32), params)
    grad_x, grad_params = pullback(cotangent.astype(jnp.float32))
    return (result.astype(jnp.bfloat16), grad_x, grad_params[0], grad_params[1], grad_params[2], grad_params[3], grad_params[4], grad_params[5], grad_params[6], grad_params[7], grad_params[8], grad_params[9], grad_params[10], grad_params[11], grad_params[12], grad_params[13], grad_params[14])
```

```python
import math

import jax
import jax.numpy as jnp
import numpy as np
from jax import lax
from jax.experimental import pallas as pl
from jax.experimental.pallas import tpu as pltpu
from jax.sharding import PartitionSpec as P

HALF_WIN = 512
EPS = 1e-12
NEG_FILL = -1e30


MESH = pl.DeviceIdType.MESH
BF, F32 = jnp.bfloat16, jnp.float32
WIDTH = 768
PART = 256
PARTS = 3
BLOCK = 256
ATTN_ROWS, MLP_ROWS = 32, 48
ORDER = (("x", "y", "z"), ("y", "z", "x"), ("z", "x", "y"))
SHIFTS = (1, 3, 2)
VMEM_BYTES = 62 * 2**20
NN = (((1,), (0,)), ((), ()))
NT = (((1,), (1,)), ((), ()))
TN = (((0,), (0,)), ((), ()))


def dot(one, two, dims=NN):
    return lax.dot_general(one, two, dims, preferred_element_type=F32)


def coords():
    seq, dp = lax.axis_index("seq"), lax.axis_index("dp")
    return {"x": (dp // 4) % 4, "y": dp // 16, "z": seq * 2 + (dp // 2) % 2, "c": dp % 2}


def device(place):
    return {
        "seq": place["z"] // 2,
        "dp": place["y"] * 16 + place["x"] * 4 + (place["z"] % 2) * 2 + place["c"],
    }


def shifted(place, axis, by):
    moved = dict(place)
    moved[axis] = (place[axis] + by) % (2 if axis == "c" else 4)
    return device(moved)


def greet(place):
    barrier = pltpu.get_barrier_semaphore()
    others = [shifted(place, axis, by) for axis in "xyz" for by in SHIFTS] + [shifted(place, "c", 1)]
    for other in others:
        pl.semaphore_signal(barrier, inc=1, device_id=other, device_id_type=MESH)
    pl.semaphore_wait(barrier, len(others))


def slab_place(group, member):
    return {
        "x": (group % 2) * 2 + member // 4,
        "y": (group // 2) % 4,
        "z": (group // 8) * 2 + (member // 2) % 2,
        "c": member % 2,
    }


def slab_index(part, place):
    first, second, third = (place[axis] for axis in ORDER[part])
    return (part, place["c"], third, second, first)


class Copies:
    def __init__(self, send_sem, recv_sem, anyone):
        self.send_sem, self.recv_sem, self.anyone = send_sem, recv_sem, anyone
        self.started = []

    def describe(self, part, number, source, target, to):
        return pltpu.make_async_remote_copy(
            src_ref=source, dst_ref=target,
            send_sem=self.send_sem.at[part, number], recv_sem=self.recv_sem.at[part, number],
            device_id=to, device_id_type=MESH,
        )

    def send(self, part, number, source, target, to):
        one = self.describe(part, number, source, target, to)
        one.start()
        self.started.append(one)

    def arrived(self, part, number, target):
        self.describe(part, number, target, target, self.anyone).wait_recv()

    def finish(self):
        for one in self.started:
            one.wait_send()
        self.started = []


class Gather:
    COUNT = 18

    def __init__(self, me, held, send_sem, recv_sem):
        self.me, self.held, self.core = me, held, me["c"]
        self.other = shifted(me, "c", 1)
        self.copies = Copies(send_sem, recv_sem, self.other)
        self.mine = [tuple(me[axis] for axis in ORDER[part]) for part in range(PARTS)]

    def first(self):
        for part in range(PARTS):
            m1, m2, m3 = self.mine[part]
            block = self.held.at[part, self.core, m3, m2, m1]
            for k, by in enumerate(SHIFTS):
                self.copies.send(part, k, block, block, shifted(self.me, ORDER[part][0], by))

    def second(self):
        for part in range(PARTS):
            m1, m2, m3 = self.mine[part]
            block = self.held.at[part, self.core, m3, m2]
            for k, by in enumerate(SHIFTS):
                self.copies.arrived(part, k, block.at[(m1 - by + 4) % 4])
            for k, by in enumerate(SHIFTS):
                self.copies.send(part, 3 + k, block, block, shifted(self.me, ORDER[part][1], by))
            self.copies.send(part, 10, block, block, self.other)

    def third(self):
        for part in range(PARTS):
            m1, m2, m3 = self.mine[part]
            block = self.held.at[part, self.core, m3]
            for k, by in enumerate(SHIFTS):
                self.copies.arrived(part, 3 + k, block.at[(m2 - by + 4) % 4])
            for k, by in enumerate((1, 3)):
                self.copies.send(part, 6 + k, block, block, shifted(self.me, ORDER[part][2], by))
            for k, by in enumerate(SHIFTS):
                there = block.at[(m2 - by + 4) % 4]
                self.copies.send(part, 11 + k, there, there, self.other)

    def fourth(self):
        for part in range(PARTS):
            m3 = self.mine[part][2]
            for k, by in enumerate((1, 3)):
                block = self.held.at[part, self.core, (m3 - by + 4) % 4]
                self.copies.arrived(part, 6 + k, block)
                half = block.at[pl.ds(2 * k, 2)]
                self.copies.send(part, 8 + k, half, half, shifted(self.me, ORDER[part][2], by))
                self.copies.send(part, 14 + k, block, block, self.other)

    def fifth(self):
        for part in range(PARTS):
            m3 = self.mine[part][2]
            for k in range(2):
                block = self.held.at[part, self.core, (m3 + 2) % 4, pl.ds(2 * k, 2)]
                self.copies.arrived(part, 8 + k, block)
                self.copies.send(part, 16 + k, block, block, self.other)

    def last(self):
        for part in range(PARTS):
            m1, m2, m3 = self.mine[part]
            there = self.held.at[part, 1 - self.core]
            self.copies.arrived(part, 10, there.at[m3, m2])
            for k, by in enumerate(SHIFTS):
                self.copies.arrived(part, 11 + k, there.at[m3, (m2 - by + 4) % 4])
            for k, by in enumerate((1, 3)):
                self.copies.arrived(part, 14 + k, there.at[(m3 - by + 4) % 4])
            for k in range(2):
                self.copies.arrived(part, 16 + k, there.at[(m3 + 2) % 4, pl.ds(2 * k, 2)])
        self.copies.finish()


def tables():
    attn = np.zeros((208, 256), np.float32)
    mlp = np.zeros((384, 384), np.float32)
    for i in range(8):
        attn[192 + i, 32 * i + 24] = 1
        for t in range(6):
            for w in range(4):
                attn[48 * w + 6 * i + t, 32 * i + 6 * w + t] = 1
                mlp[48 * w + 6 * i + t, 48 * i + 6 * w + t] = 1
        for t in range(24):
            mlp[192 + 24 * i + t, 48 * i + 24 + t] = 1
    lane, column = np.arange(128)[:, None], np.arange(WIDTH)[None]
    short = (lane % 8 == column % 6).astype(np.float32)
    short_owner = (lane == column // 6).astype(np.float32)
    inner = (lane - 64 == column % 24).astype(np.float32)
    inner_owner = (lane[:32] == column // 24).astype(np.float32)
    return attn, mlp, short, short_owner, inner, inner_owner


def block_bias(query_pos, query_seg, key_pos, key_seg):
    allowed = (query_seg == key_seg) & (jnp.abs(query_pos - key_pos) <= HALF_WIN)
    return jnp.where(allowed, 0.0, NEG_FILL)


def forward_kernel(
    wq_part, wk_part, wv_part, wo_part, win_part, wout_part, row_part, x_ref, seg_ref,
    pick_attn_ref, pick_mlp_ref, short_ref, short_owner_ref, inner_ref, inner_owner_ref,
    wq_ref, wk_ref, wv_ref, wo_ref, win_ref, wout_ref, vec_ref,
    q_ref, qh_ref, k_ref, v_ref, mixed_ref, lse_ref, segs_ref,
    held_a, held_m, rows, xh, bias, lse_cols,
    send_a, recv_a, send_m, recv_m, send_h, recv_h,
):
    me = coords()
    side = lax.axis_index("seq")
    attn_row = jnp.concatenate(
        [ref[...].astype(F32) for ref in (wq_part, wk_part, wv_part, wo_part)]
        + [row_part[...].astype(F32), jnp.zeros((7, WIDTH), F32)], axis=0,
    ).astype(BF)
    mlp_row = jnp.concatenate(
        [win_part[:, WIDTH * k : WIDTH * (k + 1)].astype(F32) for k in range(4)]
        + [wout_part[...].astype(F32)], axis=0,
    ).astype(BF)
    for part in range(PARTS):
        held_a[slab_index(part, me)] = attn_row[:, PART * part : PART * (part + 1)]
        held_m[slab_index(part, me)] = mlp_row[:, PART * part : PART * (part + 1)]
    for k in range(3):
        segs_ref[k] = jnp.broadcast_to(seg_ref[:, BLOCK * k : BLOCK * (k + 1)].astype(F32), (8, BLOCK))
    greet(me)
    attn = Gather(me, held_a, send_a, recv_a)
    mlp = Gather(me, held_m, send_m, recv_m)
    partner = shifted(me, "z", 2)
    halo = Copies(send_h, recv_h, partner)
    attn.first()
    attn.second()
    mlp.first()
    attn.third()
    attn.fourth()
    for k in range(2):
        block = jnp.where(side == 1, k, 2 - k)
        rows_out = x_ref.at[pl.ds(pl.multiple_of(block * BLOCK, BLOCK), BLOCK)]
        halo.send(0, k, rows_out, xh.at[pl.ds(k * BLOCK, BLOCK)], partner)
        halo.send(1, k, segs_ref.at[block], segs_ref.at[3 + k], partner)
    mlp.second()
    attn.fifth()
    attn.last()

    def unpack_attn(group, _):
        at = pl.ds(pl.multiple_of(group * 48, 16), 48)
        for part in range(PARTS):
            slabs = [held_a[slab_index(part, slab_place(group, member))] for member in range(8)]
            picked = dot(pick_attn_ref[...], jnp.concatenate(slabs, axis=0))
            for k, ref in enumerate((wq_ref, wk_ref, wv_ref, wo_ref)):
                ref[at, pl.ds(part * PART, PART)] = picked[48 * k : 48 * k + 48].astype(BF)
            if part == 0:
                rows[pl.ds(pl.multiple_of(group * 8, 8), 8), :] = picked[192:200, :128]
        return 0

    lax.fori_loop(0, 16, unpack_attn, 0)
    lane = lax.broadcasted_iota(jnp.int32, (1, 128), 1)
    for k in range(8):
        chosen = jnp.where(lane // 8 == k, rows[...], 0.0).astype(BF)
        vec_ref[pl.ds(k, 1), :] = jnp.sum(
            dot(chosen, short_ref[...]) * short_owner_ref[...], axis=0, keepdims=True
        )
    for k in range(4):
        chosen = rows[pl.ds(32 * k, 32), :].astype(BF)
        vec_ref[pl.ds(8 + k, 1), :] = jnp.sum(
            dot(chosen, inner_ref[...]) * inner_owner_ref[...], axis=0, keepdims=True
        )

    def project(tokens, q_out, rows_at):
        q_out[...] = (dot(tokens[...], wq_ref[...]) + vec_ref[0:1, :]).astype(BF) * jnp.asarray(0.125, BF)
        k_ref[rows_at, :] = dot(tokens[...], wk_ref[...]).astype(BF)
        v_ref[rows_at, :] = (dot(tokens[...], wv_ref[...]) + vec_ref[1:2, :]).astype(BF)

    project(x_ref, q_ref, pl.ds(0, 768))
    mlp.third()
    for k in range(2):
        halo.arrived(0, k, xh.at[pl.ds(k * BLOCK, BLOCK)])
        halo.arrived(1, k, segs_ref.at[3 + k])
    project(xh, qh_ref, pl.ds(768, 512))

    across = lax.broadcasted_iota(jnp.int32, (1, BLOCK), 1)
    down = lax.broadcasted_iota(jnp.int32, (BLOCK, 1), 0)
    starts = [BLOCK * k for k in range(3)] + [
        jnp.where(side == 0, 768 + BLOCK * k, -BLOCK * (k + 1)) for k in range(2)
    ]
    blocks = [jnp.where(side == 0, b, 2 - b) for b in range(3)]
    for b in range(3):
        seg_here = segs_ref[blocks[b], 0:1, :]
        seg_down = jnp.broadcast_to(seg_here, (128, BLOCK)).T[:, 0:1]
        for k in range(3 + b):
            bias[b, :, pl.ds(k * BLOCK, BLOCK)] = block_bias(
                blocks[b] * BLOCK + down, seg_down, starts[k] + across, segs_ref[k, 0:1, :]
            )

    low = lane < 64

    def attend(pair, _):
        columns = pl.ds(pl.multiple_of(pair * 128, 128), 128)
        for b in range(3):
            count = 768 + BLOCK * b
            at = pl.ds(pl.multiple_of(blocks[b] * BLOCK, BLOCK), BLOCK)
            queries = q_ref[at, columns]
            keys, values = k_ref[pl.ds(0, count), columns], v_ref[pl.ds(0, count), columns]
            outs = []
            for e in range(2):
                keep = low if e == 0 else ~low
                scores = dot(jnp.where(keep, queries, jnp.zeros((), BF)), keys, NT)
                scores = scores + bias[b, :, pl.ds(0, count)]
                top = jnp.max(scores, axis=1, keepdims=True)
                weights = jnp.exp(scores - top).astype(BF)
                out = dot(weights, jnp.where(keep, values, jnp.ones((), BF)))
                outs.append(out)
                total = out[:, 64:65] if e == 0 else out[:, 0:1]
                lse_cols[at, :] = jnp.where(lane == 2 * pair + e, top + jnp.log(total), lse_cols[at, :])
            sums = pltpu.roll(jnp.where(low, outs[1], outs[0]), 64, 1)
            mixed_ref[at, columns] = (jnp.where(low, outs[0], outs[1]) / sums).astype(BF)
        return 0

    lax.fori_loop(0, 2, attend, 0)
    mlp.fourth()
    lax.fori_loop(2, 4, attend, 0)
    mlp.fifth()
    lax.fori_loop(4, 6, attend, 0)
    lse_ref[...] = lse_cols[...].T[:16]
    mlp.last()
    halo.finish()

    def unpack_mlp(group, _):
        at = pl.ds(pl.multiple_of(group * 48, 16), 48)
        at_outer = pl.ds(pl.multiple_of(group * 192, 64), 192)
        for part in range(PARTS):
            slabs = [held_m[slab_index(part, slab_place(group, member))] for member in range(8)]
            picked = dot(pick_mlp_ref[...], jnp.concatenate(slabs, axis=0)).astype(BF)
            for k in range(4):
                win_ref[at, pl.ds(k * WIDTH + part * PART, PART)] = picked[48 * k : 48 * k + 48]
            wout_ref[at_outer, pl.ds(part * PART, PART)] = picked[192:]
        return 0

    lax.fori_loop(0, 16, unpack_mlp, 0)


def run_forward(parts, row, tokens, seg_row):
    attn, mlp, short, short_owner, inner, inner_owner = tables()
    fixed = (
        jnp.asarray(attn, BF), jnp.asarray(mlp, BF), jnp.asarray(short, BF),
        jnp.asarray(short_owner), jnp.asarray(inner, BF), jnp.asarray(inner_owner),
    )
    vmem = pl.BlockSpec(memory_space=pltpu.VMEM)
    shapes = (
        [((768, 768), BF)] * 4
        + [((768, 3072), BF), ((3072, 768), BF), ((16, 768), F32)]
        + [((768, 768), BF), ((512, 768), BF), ((1280, 768), BF), ((1280, 768), BF)]
        + [((768, 768), BF), ((16, 768), F32), ((5, 8, BLOCK), F32)]
    )
    sems = pltpu.SemaphoreType.DMA
    return pl.pallas_call(
        forward_kernel,
        out_shape=tuple(jax.ShapeDtypeStruct(*shape) for shape in shapes),
        in_specs=[vmem] * 15,
        out_specs=(vmem,) * len(shapes),
        scratch_shapes=[
            pltpu.VMEM((PARTS, 2, 4, 4, 4, ATTN_ROWS, PART), BF),
            pltpu.VMEM((PARTS, 2, 4, 4, 4, MLP_ROWS, PART), BF),
            pltpu.VMEM((128, 128), F32),
            pltpu.VMEM((512, 768), BF),
            pltpu.VMEM((3, BLOCK, 1280), F32),
            pltpu.VMEM((768, 128), F32),
            sems((PARTS, 18)), sems((PARTS, 18)), sems((PARTS, 18)), sems((PARTS, 18)),
            sems((2, 2)), sems((2, 2)),
        ],
        compiler_params=pltpu.CompilerParams(
            collective_id=0, has_side_effects=True, vmem_limit_bytes=VMEM_BYTES
        ),
        name="gather_and_attend",
    )(*parts, row, tokens, seg_row, *fixed)


class Scatter:
    COUNT = 14

    def __init__(self, me, parts, own, near, halves, blocks, second, first, send_sem, recv_sem):
        self.me, self.core = me, me["c"]
        self.parts, self.own, self.near, self.halves = parts, own, near, halves
        self.blocks, self.second, self.first = blocks, second, first
        self.other = shifted(me, "c", 1)
        self.copies = Copies(send_sem, recv_sem, self.other)
        self.mine = [tuple(me[axis] for axis in ORDER[part]) for part in range(PARTS)]

    def add(self, target, sources, count):
        def body(index, _):
            at = (index // 4, index % 4)
            total = target[at].astype(F32)
            for source in sources:
                total = total + source[at].astype(F32)
            target[at] = total.astype(BF)
            return 0

        lax.fori_loop(0, 4 * count, body, 0)

    def to_sibling(self):
        for k, by in enumerate((2, 1, 3, 0)):
            for part in range(PARTS):
                at = (self.mine[part][2] + by) % 4
                self.copies.send(
                    part, k, self.parts.at[part, 1 - self.core, at], self.near.at[part, at], self.other
                )

    def near_sum(self, part, k, by):
        at = (self.mine[part][2] + by) % 4
        self.copies.arrived(part, k, self.near.at[part, at])
        self.add(self.near.at[part, at], [self.own(part, at)], 4)

    def opposite(self):
        for part in range(PARTS):
            m3 = self.mine[part][2]
            self.near_sum(part, 0, 2)
            for k, by in enumerate((1, 3)):
                half = self.near.at[part, (m3 + 2) % 4, pl.ds(2 * k, 2)]
                self.copies.send(
                    part, 4 + k, half, self.halves.at[part, k], shifted(self.me, ORDER[part][2], by)
                )

    def neighbours(self):
        for part in range(PARTS):
            self.near_sum(part, 1, 1)
            self.near_sum(part, 2, 3)
        for part in range(PARTS):
            m3 = self.mine[part][2]
            for k, by in enumerate((1, 3)):
                self.copies.arrived(part, 4 + k, self.halves.at[part, k])
                block = self.near.at[part, (m3 + by) % 4]
                self.add(block.at[pl.ds(2 * k, 2)], [self.halves.at[part, k]], 2)
                self.copies.send(
                    part, 6 + k, block, self.blocks.at[part, k], shifted(self.me, ORDER[part][2], by)
                )
        for part in range(PARTS):
            self.near_sum(part, 3, 0)

    def middle(self):
        for part in range(PARTS):
            m1, m2, m3 = self.mine[part]
            for k in range(2):
                self.copies.arrived(part, 6 + k, self.blocks.at[part, k])
            block = self.near.at[part, m3]
            self.add(block, [self.blocks.at[part, 0], self.blocks.at[part, 1]], 4)
            for k, by in enumerate(SHIFTS):
                self.copies.send(
                    part, 8 + k, block.at[(m2 + by) % 4], self.second.at[part, k],
                    shifted(self.me, ORDER[part][1], by),
                )

    def final(self):
        for part in range(PARTS):
            m1, m2, m3 = self.mine[part]
            for k in range(3):
                self.copies.arrived(part, 8 + k, self.second.at[part, k])
            block = self.near.at[part, m3, pl.ds(m2, 1)]
            self.add(block, [self.second.at[part, pl.ds(k, 1)] for k in range(3)], 1)
            for k, by in enumerate(SHIFTS):
                self.copies.send(
                    part, 11 + k, block.at[0, (m1 + by) % 4], self.first.at[part, k],
                    shifted(self.me, ORDER[part][0], by),
                )

    def result(self, out_ref):
        for part in range(PARTS):
            m1, m2, m3 = self.mine[part]
            for k in range(3):
                self.copies.arrived(part, 11 + k, self.first.at[part, k])
            total = self.near[part, m3, m2, m1].astype(F32)
            for k in range(3):
                total = total + self.first[part, k].astype(F32)
            out_ref[part] = total
        self.copies.finish()


def row_sum(block):
    return jnp.sum(block, axis=0, keepdims=True)


def normed_of(hidden):
    centred = hidden - jnp.mean(hidden, axis=1, keepdims=True)
    inverse = lax.rsqrt(jnp.mean(centred * centred, axis=1, keepdims=True) + EPS)
    return centred * inverse, inverse


def dense_kernel(
    x_ref, mixed_ref, cot_ref, wo_ref, win_ref, wout_ref, vec_ref, put_mlp_ref, heads_ref,
    out_ref, dwo_ref, hidden_ref, gmix_ref, delta_ref, sums_ref, parts_ref,
    active, slope, normed, inverse, first_bf, total, grad_bf,
):
    sums_ref[...] = jnp.zeros_like(sums_ref)

    def add_sum(row, block):
        sums_ref[pl.ds(row, 1), :] += row_sum(block)

    def row_block(index):
        return pl.ds(pl.multiple_of(index * BLOCK, BLOCK), BLOCK)

    def norm_one(index, _):
        at = row_block(index)
        hidden = x_ref[at, :].astype(F32) + (dot(mixed_ref[at, :], wo_ref[...]) + vec_ref[2:3, :])
        normed[at, :], spread = normed_of(hidden)
        inverse[at, :] = jnp.broadcast_to(spread, (BLOCK, 128))
        first_bf[at, :] = (normed[at, :] * vec_ref[3:4, :] + vec_ref[4:5, :]).astype(BF)
        return 0

    lax.fori_loop(0, 3, norm_one, 0)
    total[...] = jnp.zeros_like(total)
    rate, bend = math.sqrt(2 / math.pi), 0.044715

    def inner_block(index, _):
        columns = pl.ds(pl.multiple_of(index * WIDTH, WIDTH), WIDTH)
        u = dot(first_bf[...], win_ref[:, columns]) + vec_ref[pl.ds(8 + index, 1), :]
        square = u * u
        bent = jnp.tanh(rate * u * (1 + bend * square))
        half = 0.5 * (1 + bent)
        active[:, columns] = (u * half).astype(BF)
        slope[:, columns] = (
            half + u * half * (1 - bent) * (rate + (3 * rate * bend) * square)
        ).astype(BF)
        total[...] += dot(active[:, columns], wout_ref[columns, :])
        return 0

    lax.fori_loop(0, 4, inner_block, 0)

    def norm_two(index, _):
        at = row_block(index)
        first = normed[at, :] * vec_ref[3:4, :] + vec_ref[4:5, :]
        normed_two, spread = normed_of(first + (total[at, :] + vec_ref[5:6, :]))
        out_ref[at, :] = (normed_two * vec_ref[6:7, :] + vec_ref[7:8, :]).astype(BF)
        grad = cot_ref[at, :].astype(F32)
        add_sum(6, grad * normed_two)
        add_sum(7, grad)
        scaled = grad * vec_ref[6:7, :]
        mean_grad = jnp.mean(scaled, axis=1, keepdims=True)
        mean_cross = jnp.mean(scaled * normed_two, axis=1, keepdims=True)
        back = spread * (scaled - mean_grad - normed_two * mean_cross)
        total[at, :] = back
        grad_bf[at, :] = back.astype(BF)
        add_sum(5, grad_bf[at, :].astype(F32))
        return 0

    lax.fori_loop(0, 3, norm_two, 0)

    def outer_block(index, _):
        columns = pl.ds(pl.multiple_of(index * WIDTH, WIDTH), WIDTH)
        grad_inner = (dot(grad_bf[...], wout_ref[columns, :], NT) * slope[:, columns].astype(F32)).astype(BF)
        add_sum(8 + index, grad_inner.astype(F32))
        total[...] += dot(grad_inner, win_ref[:, columns], NT)
        active[:, columns] = dot(active[:, columns], grad_bf[...], TN).astype(BF)
        slope[:, columns] = dot(first_bf[...], grad_inner, TN).astype(BF)
        return 0

    lax.fori_loop(0, 4, outer_block, 0)

    def back_one(index, _):
        at = row_block(index)
        grad, normed_one = total[at, :], normed[at, :]
        add_sum(3, grad * normed_one)
        add_sum(4, grad)
        scaled = grad * vec_ref[3:4, :]
        mean_grad = jnp.mean(scaled, axis=1, keepdims=True)
        mean_cross = jnp.mean(scaled * normed_one, axis=1, keepdims=True)
        back = inverse[at, 0:1] * (scaled - mean_grad - normed_one * mean_cross)
        hidden_ref[at, :] = back
        grad_bf[at, :] = back.astype(BF)
        add_sum(2, grad_bf[at, :].astype(F32))
        return 0

    lax.fori_loop(0, 3, back_one, 0)
    dwo_ref[...] = dot(mixed_ref[...], grad_bf[...], TN).astype(BF)
    gmix_ref[...] = dot(grad_bf[...], wo_ref[...], NT).astype(BF)
    for k in range(3):
        at = pl.ds(BLOCK * k, BLOCK)
        product = mixed_ref[at, :].astype(F32) * gmix_ref[at, :].astype(F32)
        delta_ref[k] = lax.dot_general(
            heads_ref[...], product, NT, precision=lax.Precision.HIGHEST, preferred_element_type=F32
        )

    def pack(group, _):
        at = pl.ds(pl.multiple_of(group * 48, 16), 48)
        at_outer = pl.ds(pl.multiple_of((group % 4) * 192, 64), 192)
        for part in range(PARTS):
            pieces = [slope[at, pl.ds(k * WIDTH + part * PART, PART)] for k in range(4)]
            outer_columns = pl.ds(pl.multiple_of((group // 4) * WIDTH + part * PART, PART), PART)
            pieces.append(active[at_outer, outer_columns])
            placed = dot(put_mlp_ref[...], jnp.concatenate(pieces, axis=0)).astype(BF)
            for member in range(8):
                parts_ref[slab_index(part, slab_place(group, member))] = placed[48 * member : 48 * member + 48]
        return 0

    lax.fori_loop(0, 16, pack, 0)


def run_dense(tokens, mixed, cot, wo, win, wout, vec):
    mlp = tables()[1]
    heads = (np.arange(16)[:, None] == np.arange(WIDTH)[None] // 64).astype(np.float32)
    vmem = pl.BlockSpec(memory_space=pltpu.VMEM)
    shapes = (
        ((768, 768), BF), ((768, 768), BF), ((768, 768), F32), ((768, 768), BF), ((3, 16, BLOCK), F32),
        ((16, 768), F32), ((PARTS, 2, 4, 4, 4, MLP_ROWS, PART), BF),
    )
    return pl.pallas_call(
        dense_kernel,
        out_shape=tuple(jax.ShapeDtypeStruct(*shape) for shape in shapes),
        in_specs=[vmem] * 9,
        out_specs=(vmem,) * len(shapes),
        scratch_shapes=[
            pltpu.VMEM((768, 3072), BF), pltpu.VMEM((768, 3072), BF), pltpu.VMEM((768, 768), F32),
            pltpu.VMEM((768, 128), F32), pltpu.VMEM((768, 768), BF), pltpu.VMEM((768, 768), F32),
            pltpu.VMEM((768, 768), BF),
        ],
        compiler_params=pltpu.CompilerParams(vmem_limit_bytes=VMEM_BYTES),
        name="feed_forward",
    )(tokens, mixed, cot, wo, win, wout, vec, jnp.asarray(mlp.T, BF), jnp.asarray(heads))


def backward_kernel(
    q_any, qh_any, k_any, v_any, g_any, x_any, wq_any, wk_any, wv_any, hidden_any, mlp_any,
    lse_ref, delta_ref, segs_ref, dwo_ref, sums_ref, put_attn_ref, short_ref, short_owner_ref,
    inner_ref, inner_owner_ref,
    grad_any, attn_out, mlp_out,
    q, qh, k, v, g, gh, stats, own_m, bias, bias_h, dq, dk, dv, dw, rows, hidden,
    parts_a, near_a, halves_a, blocks_a, second_a, first_a,
    near_m, halves_m, blocks_m, second_m, first_m,
    load_sem, send_a, recv_a, send_m, recv_m, send_h, recv_h,
):
    me = coords()
    core = me["c"]
    side = lax.axis_index("seq")
    partner = shifted(me, "z", 2)
    loads = {}

    def load(number, source, target):
        loads[number] = pltpu.make_async_copy(source, target, load_sem.at[number])
        loads[number].start()

    for number, (source, target) in enumerate(
        ((q_any, q), (k_any, k), (v_any, v), (g_any, g), (qh_any, qh), (mlp_any.at[:, core], own_m))
    ):
        load(number, source, target)
    load(6, hidden_any, hidden)
    for b in range(3):
        stats[b, 0:16, :] = lse_ref[b]
        stats[b, 16:32, :] = delta_ref[b]
    greet(me)
    mlp = Scatter(
        me, mlp_any, lambda part, at: own_m.at[part, at], near_m, halves_m, blocks_m, second_m, first_m,
        send_m, recv_m,
    )
    attn = Scatter(
        me, parts_a, lambda part, at: parts_a.at[part, core, at], near_a, halves_a, blocks_a, second_a,
        first_a, send_a, recv_a,
    )
    halo = Copies(send_h, recv_h, partner)
    loads[3].wait()
    for n in range(2):
        block = jnp.where(side == 1, n, 2 - n)
        rows_out = g.at[pl.ds(pl.multiple_of(block * BLOCK, BLOCK), BLOCK)]
        halo.send(0, n, rows_out, gh.at[pl.ds(n * BLOCK, BLOCK)], partner)
        halo.send(1, n, stats.at[block], stats.at[3 + n], partner)
    mlp.to_sibling()

    across = lax.broadcasted_iota(jnp.int32, (1, BLOCK), 1)
    down = lax.broadcasted_iota(jnp.int32, (BLOCK, 1), 0)
    starts = [BLOCK * n for n in range(3)] + [
        jnp.where(side == 0, 768 + BLOCK * n, -BLOCK * (n + 1)) for n in range(2)
    ]
    blocks = [jnp.where(side == 0, b, 2 - b) for b in range(3)]

    def seg_down(block):
        return jnp.broadcast_to(segs_ref[block, 0:1, :], (128, BLOCK)).T[:, 0:1]

    for n in range(5):
        seg_key, key_pos = seg_down(n), starts[n] + down
        for b in range(max(0, n - 2), 3):
            bias[b, pl.ds(n * BLOCK, BLOCK), :] = block_bias(
                blocks[b] * BLOCK + across, segs_ref[blocks[b], 0:1, :], key_pos, seg_key
            )
    reach = [
        (jnp.where(side == 0, BLOCK * (1 + n), 0), BLOCK * (2 - n)) for n in range(2)
    ]
    for n in range(2):
        for m in range(2 - n):
            block = jnp.where(side == 0, 1 + n + m, m)
            bias_h[n, pl.ds(m * BLOCK, BLOCK), :] = block_bias(
                starts[3 + n] + across, segs_ref[3 + n, 0:1, :], block * BLOCK + down, seg_down(block)
            )
    dk[...] = jnp.zeros_like(dk)
    dv[...] = jnp.zeros_like(dv)
    low = lax.broadcasted_iota(jnp.int32, (1, 128), 1) < 64
    nothing = jnp.zeros((), BF)

    def weights_back(keys, values, queries, grads, shift, stat, head):
        scores = dot(keys, queries, NT) + shift
        probs = jnp.exp(scores - stats[stat, pl.ds(head, 1), :])
        grad_probs = dot(values, grads, NT)
        grad_scores = probs * (grad_probs - stats[stat, pl.ds(16 + head, 1), :])
        return probs.astype(BF), grad_scores.astype(BF)

    def own_pair(pair, _):
        columns = pl.ds(pl.multiple_of(pair * 128, 128), 128)
        for b in range(3):
            count = 768 + BLOCK * b
            at = pl.ds(pl.multiple_of(blocks[b] * BLOCK, BLOCK), BLOCK)
            queries, grads = q[at, columns], g[at, columns]
            keys, values = k[pl.ds(0, count), columns], v[pl.ds(0, count), columns]
            grad_query = jnp.zeros((BLOCK, 128), F32)
            for e in range(2):
                keep = low if e == 0 else ~low
                queries_e, grads_e = jnp.where(keep, queries, nothing), jnp.where(keep, grads, nothing)
                probs, grad_scores = weights_back(
                    keys, values, queries_e, grads_e, bias[b, pl.ds(0, count), :], blocks[b], 2 * pair + e
                )
                dk[:, columns] += dot(grad_scores[:768], queries_e)
                dv[:, columns] += dot(probs[:768], grads_e)
                grad_query += dot(grad_scores, jnp.where(keep, keys, nothing), TN)
            dq[at, columns] = (grad_query * 0.125).astype(BF)
        return 0

    def halo_pair(pair, _):
        columns = pl.ds(pl.multiple_of(pair * 128, 128), 128)
        for n in range(2):
            start, count = reach[n]
            at = pl.ds(pl.multiple_of(start, BLOCK), count)
            here = pl.ds(n * BLOCK, BLOCK)
            queries, grads = qh[here, columns], gh[here, columns]
            keys, values = k[at, columns], v[at, columns]
            for e in range(2):
                keep = low if e == 0 else ~low
                queries_e, grads_e = jnp.where(keep, queries, nothing), jnp.where(keep, grads, nothing)
                probs, grad_scores = weights_back(
                    keys, values, queries_e, grads_e, bias_h[n, pl.ds(0, count), :], 3 + n, 2 * pair + e
                )
                dk[at, columns] += dot(grad_scores, queries_e)
                dv[at, columns] += dot(probs, grads_e)
        return 0

    for number in (0, 1, 2, 4, 5):
        loads[number].wait()
    lax.fori_loop(0, 2, own_pair, 0)
    mlp.opposite()
    lax.fori_loop(2, 3, own_pair, 0)
    mlp.neighbours()
    lax.fori_loop(3, 6, own_pair, 0)
    mlp.middle()
    for n in range(2):
        halo.arrived(0, n, gh.at[pl.ds(n * BLOCK, BLOCK)])
        halo.arrived(1, n, stats.at[3 + n])
    lax.fori_loop(0, 6, halo_pair, 0)
    mlp.final()
    halo.finish()
    for number, (source, target) in enumerate(
        ((x_any, g), (wq_any, q), (wk_any, k.at[pl.ds(0, 768)]), (wv_any, v.at[pl.ds(0, 768)]))
    ):
        load(7 + number, source, target)

    rows[...] = jnp.zeros_like(rows)
    lane = lax.broadcasted_iota(jnp.int32, (1, 128), 1)
    for n in range(8):
        if n == 0:
            vec = row_sum(dq[...].astype(F32))
        elif n == 1:
            vec = row_sum(dv[...].astype(BF).astype(F32))
        else:
            vec = sums_ref[n : n + 1, :]
        spread = dot((short_owner_ref[...] * vec).astype(BF), short_ref[...], NT)
        rows[...] = jnp.where(lane // 8 == n, spread, rows[...])
    for n in range(4):
        spread = dot((inner_owner_ref[...] * sums_ref[8 + n : 9 + n, :]).astype(BF), inner_ref[...], NT)
        at = pl.ds(32 * n, 32)
        rows[at, :] = jnp.where((lane >= 64) & (lane < 88), spread, rows[at, :])
    loads[7].wait()
    for part in range(PARTS):
        columns = slice(PART * part, PART * (part + 1))
        for n, grad in enumerate((dq, dk, dv)):
            dw[n] = dot(g[...], grad[:, columns].astype(BF), TN).astype(BF)

        def pack(group, _):
            at = pl.ds(pl.multiple_of(group * 48, 16), 48)
            pieces = [dw[n, at, :] for n in range(3)] + [dwo_ref[at, columns]]
            if part == 0:
                vec = rows[pl.ds(pl.multiple_of(group * 8, 8), 8), :]
                vec = jnp.concatenate([vec, jnp.zeros_like(vec)], axis=1)
                vec = jnp.concatenate([vec, jnp.zeros_like(vec)], axis=0).astype(BF)
            else:
                vec = jnp.zeros((16, PART), BF)
            placed = dot(put_attn_ref[...], jnp.concatenate(pieces + [vec], axis=0)).astype(BF)
            for member in range(8):
                parts_a[slab_index(part, slab_place(group, member))] = placed[32 * member : 32 * member + 32]
            return 0

        lax.fori_loop(0, 16, pack, 0)
    attn.to_sibling()
    mlp.result(mlp_out)
    for number in (6, 8, 9, 10):
        loads[number].wait()
    hidden[...] += dot(dq[...], q[...], NT)
    attn.opposite()
    hidden[...] += dot(dk[...].astype(BF), k[pl.ds(0, 768), :], NT)
    attn.neighbours()
    hidden[...] += dot(dv[...].astype(BF), v[pl.ds(0, 768), :], NT)
    store = pltpu.make_async_copy(hidden, grad_any, load_sem.at[11])
    store.start()
    attn.middle()
    attn.final()
    attn.result(attn_out)
    store.wait()


def run_backward(q, qh, k, v, g, x, wq, wk, wv, hidden, mlp, lse, delta, segs, dwo, sums):
    attn_table, _, short, short_owner, inner, inner_owner = tables()
    fixed = (
        jnp.asarray(attn_table.T, BF), jnp.asarray(short, BF), jnp.asarray(short_owner),
        jnp.asarray(inner, BF), jnp.asarray(inner_owner),
    )
    vmem, anywhere = pl.BlockSpec(memory_space=pltpu.VMEM), pl.BlockSpec(memory_space=pl.ANY)
    sems = pltpu.SemaphoreType.DMA

    def steps(rows):
        return [
            pltpu.VMEM((PARTS, 4, 4, 4, rows, PART), BF),
            pltpu.VMEM((PARTS, 2, 2, 4, rows, PART), BF),
            pltpu.VMEM((PARTS, 2, 4, 4, rows, PART), BF),
            pltpu.VMEM((PARTS, 3, 4, rows, PART), BF),
            pltpu.VMEM((PARTS, 3, rows, PART), BF),
        ]

    return pl.pallas_call(
        backward_kernel,
        out_shape=(
            jax.ShapeDtypeStruct((768, 768), F32),
            jax.ShapeDtypeStruct((PARTS, ATTN_ROWS, PART), F32),
            jax.ShapeDtypeStruct((PARTS, MLP_ROWS, PART), F32),
        ),
        in_specs=[anywhere] * 11 + [vmem] * 10,
        out_specs=(anywhere, vmem, vmem),
        scratch_shapes=[
            pltpu.VMEM((768, 768), BF), pltpu.VMEM((512, 768), BF),
            pltpu.VMEM((1280, 768), BF), pltpu.VMEM((1280, 768), BF),
            pltpu.VMEM((768, 768), BF), pltpu.VMEM((512, 768), BF),
            pltpu.VMEM((5, 32, BLOCK), F32),
            pltpu.VMEM((PARTS, 4, 4, 4, MLP_ROWS, PART), BF),
            pltpu.VMEM((3, 1280, BLOCK), F32), pltpu.VMEM((2, 512, BLOCK), F32),
            pltpu.VMEM((768, 768), BF), pltpu.VMEM((768, 768), F32), pltpu.VMEM((768, 768), F32),
            pltpu.VMEM((3, 768, PART), BF), pltpu.VMEM((128, 128), F32), pltpu.VMEM((768, 768), F32),
            pltpu.VMEM((PARTS, 2, 4, 4, 4, ATTN_ROWS, PART), BF),
            *steps(ATTN_ROWS), *steps(MLP_ROWS),
            sems((12,)), sems((PARTS, 14)), sems((PARTS, 14)), sems((PARTS, 14)), sems((PARTS, 14)),
            sems((2, 2)), sems((2, 2)),
        ],
        compiler_params=pltpu.CompilerParams(
            collective_id=1, has_side_effects=True, vmem_limit_bytes=VMEM_BYTES
        ),
        name="attend_back_and_scatter",
    )(q, qh, k, v, g, x, wq, wk, wv, hidden, mlp, lse, delta, segs, dwo, sums, *fixed)


def split_kernel(attn_ref, mlp_ref, *outs):
    wq, wk, wv, wo, win, wout, inner, short = outs
    for part in range(PARTS):
        columns = pl.ds(PART * part, PART)
        for k, ref in enumerate((wq, wk, wv, wo)):
            ref[:, columns] = attn_ref[part, 6 * k : 6 * k + 6, :]
        for k in range(4):
            win[:, pl.ds(WIDTH * k + PART * part, PART)] = mlp_ref[part, 6 * k : 6 * k + 6, :]
        wout[:, columns] = mlp_ref[part, 24:48, :]
    inner[...] = attn_ref[0, 24:25, 64:88]
    for k in range(8):
        short[k : k + 1, :] = attn_ref[0, 24:25, 8 * k : 8 * k + 6]


def split_results(attn, mlp):
    vmem = pl.BlockSpec(memory_space=pltpu.VMEM)
    shapes = ((6, 768),) * 4 + ((6, 3072), (24, 768), (1, 24), (8, 6))
    return pl.pallas_call(
        split_kernel,
        out_shape=tuple(jax.ShapeDtypeStruct(shape, F32) for shape in shapes),
        in_specs=[vmem] * 2,
        out_specs=(vmem,) * len(shapes),
        name="split_gradients",
    )(attn, mlp)


def per_device(
    inputs,
    segments,
    w_query,
    w_key,
    w_value,
    w_output,
    b_query,
    b_value,
    b_output,
    gain_attn,
    bias_attn,
    w_inner,
    b_inner,
    w_outer,
    b_outer,
    gain_out,
    bias_out,
    cotangent,
):
    tokens = inputs.reshape(768, 768)
    short = (b_query, b_value, b_output, gain_attn, bias_attn, b_outer, gain_out, bias_out)
    row = jnp.concatenate([jnp.pad(vec, (0, 2)) for vec in short] + [b_inner])
    row = jnp.pad(row, (0, WIDTH - row.shape[0]))[None]
    parts = (w_query, w_key, w_value, w_output, w_inner, w_outer)
    wq, wk, wv, wo, win, wout, vec, q, qh, k, v, mixed, lse, segs = run_forward(parts, row, tokens, segments)
    out, dwo, hidden, gmix, delta, sums, mlp = run_dense(
        tokens, mixed, cotangent.reshape(768, 768), wo, win, wout, vec
    )
    lse = lse.reshape(16, 3, BLOCK).transpose(1, 0, 2)
    grad_input, attn_sum, mlp_sum = run_backward(
        q, qh, k, v, gmix, tokens, wq, wk, wv, hidden, mlp, lse, delta, segs, dwo, sums
    )
    dwq, dwk, dwv, dwo, dwin, dwout, inner, short = split_results(attn_sum, mlp_sum)
    return (
        out.reshape(1, 768, 768),
        grad_input.reshape(1, 768, 768),
        dwq,
        dwk,
        dwv,
        dwo,
        *(short[k] for k in range(5)),
        dwin,
        inner.reshape(24),
        dwout,
        *(short[k] for k in range(5, 8)),
    )


def solution(mesh):
    return jax.shard_map(
        per_device,
        mesh=mesh,
        in_specs=(
            P("dp", "seq", None),
            P("dp", "seq"),
            P(("seq", "dp"), None),
            P(("seq", "dp"), None),
            P(("seq", "dp"), None),
            P(("seq", "dp"), None),
            P(("seq", "dp")),
            P(("seq", "dp")),
            P(("seq", "dp")),
            P(("seq", "dp")),
            P(("seq", "dp")),
            P(("seq", "dp"), None),
            P(("seq", "dp")),
            P(("seq", "dp"), None),
            P(("seq", "dp")),
            P(("seq", "dp")),
            P(("seq", "dp")),
            P("dp", "seq", None),
        ),
        out_specs=(
            P("dp", "seq", None),
            P("dp", "seq", None),
            P(("seq", "dp"), None),
            P(("seq", "dp"), None),
            P(("seq", "dp"), None),
            P(("seq", "dp"), None),
            P(("seq", "dp")),
            P(("seq", "dp")),
            P(("seq", "dp")),
            P(("seq", "dp")),
            P(("seq", "dp")),
            P(("seq", "dp"), None),
            P(("seq", "dp")),
            P(("seq", "dp"), None),
            P(("seq", "dp")),
            P(("seq", "dp")),
            P(("seq", "dp")),
        ),
        check_vma=False,
    )
```

```python
import math

import jax
import jax.numpy as jnp
import numpy as np
from jax import lax
from jax.experimental import pallas as pl
from jax.experimental.pallas import tpu as pltpu
from jax.sharding import PartitionSpec as P

HALF_WIN = 512
EPS = 1e-12
NEG_FILL = -1e30


MESH = pl.DeviceIdType.MESH
BF, F32 = jnp.bfloat16, jnp.float32
WIDTH = 768
PART, PARTS = 256, 3
WIDE, WIDES = 384, 2
BLOCK = 256
ATTN_ROWS, MLP_ROWS = 16, 48
ORDER = (("x", "y", "z"), ("y", "z", "x"), ("z", "x", "y"))
WIDE_ORDER = (("z", "x", "y"), ("z", "y", "x"))
SHIFTS = (1, 3, 2)
VMEM_BYTES = 62 * 2**20
NN = (((1,), (0,)), ((), ()))
NT = (((1,), (1,)), ((), ()))
TN = (((0,), (0,)), ((), ()))


def dot(one, two, dims=NN):
    return lax.dot_general(one, two, dims, preferred_element_type=F32)


def coords():
    seq, dp = lax.axis_index("seq"), lax.axis_index("dp")
    return {"x": (dp // 4) % 4, "y": dp // 16, "z": seq * 2 + (dp // 2) % 2, "c": dp % 2}


def device(place):
    return {
        "seq": place["z"] // 2,
        "dp": place["y"] * 16 + place["x"] * 4 + (place["z"] % 2) * 2 + place["c"],
    }


def shifted(place, axis, by):
    moved = dict(place)
    moved[axis] = (place[axis] + by) % (2 if axis == "c" else 4)
    return device(moved)


def greet(place):
    barrier = pltpu.get_barrier_semaphore()
    others = [shifted(place, axis, by) for axis in "xyz" for by in SHIFTS] + [shifted(place, "c", 1)]
    for other in others:
        pl.semaphore_signal(barrier, inc=1, device_id=other, device_id_type=MESH)
    pl.semaphore_wait(barrier, len(others))


def slab_place(group, member):
    return {
        "x": (group % 2) * 2 + member // 4,
        "y": (group // 2) % 4,
        "z": (group // 8) * 2 + (member // 2) % 2,
        "c": member % 2,
    }


def slab_index(order, part, place):
    first, second, third = (place[axis] for axis in order[part])
    return (part, place["c"], third, second, first)


class Copies:
    def __init__(self, sems, sizes, anyone):
        self.sems, self.sizes, self.anyone = sems, sizes, anyone
        self.kinds = set()

    def describe(self, kind, source, target, to):
        return pltpu.make_async_remote_copy(
            src_ref=source, dst_ref=target, send_sem=self.sems.at[0, kind], recv_sem=self.sems.at[1, kind],
            device_id=to, device_id_type=MESH,
        )

    def send(self, kind, source, target, to):
        self.describe(kind, source, target, to).start()
        self.kinds.add(kind)

    def arrived(self, kind):
        self.describe(kind, self.sizes[kind], self.sizes[kind], self.anyone).wait_recv()

    def finish(self):
        for kind in sorted(self.kinds):
            self.describe(kind, self.sizes[kind], self.sizes[kind], self.anyone).wait_send()


class Gather:
    KINDS = 10

    def __init__(self, me, held, sems, order):
        self.order, self.parts = order, range(len(order))
        self.me, self.held, self.core = me, held, me["c"]
        self.other = shifted(me, "c", 1)
        all_parts = held.at[:, self.core]
        three, two = pl.ds(0, 3), pl.ds(0, 2)
        sizes = (
            all_parts.at[:, 0, 0, three], all_parts.at[:, 0, three], all_parts.at[:, two, two],
            all_parts.at[:, two, two], all_parts.at[:, two, two], all_parts.at[:, 0, 0],
            all_parts.at[:, 0, three], all_parts.at[:, two, two], all_parts.at[:, two, two],
            all_parts.at[:, two, two],
        )
        self.copies = Copies(sems, sizes, self.other)
        self.mine = [tuple(me[axis] for axis in order[part]) for part in self.parts]

    def send(self, kind, block, to):
        self.copies.send(kind, block, block, to)

    def first(self):
        for part in self.parts:
            m1, m2, m3 = self.mine[part]
            for by in SHIFTS:
                self.send(0, self.held.at[part, self.core, m3, m2, m1], shifted(self.me, self.order[part][0], by))

    def second(self):
        self.copies.arrived(0)
        for part in self.parts:
            m1, m2, m3 = self.mine[part]
            for by in SHIFTS:
                self.send(1, self.held.at[part, self.core, m3, m2], shifted(self.me, self.order[part][1], by))
        for part in self.parts:
            m1, m2, m3 = self.mine[part]
            self.send(5, self.held.at[part, self.core, m3, m2], self.other)

    def third(self):
        self.copies.arrived(1)
        for late in range(2):
            for part in self.parts:
                m3 = self.mine[part][2]
                for k, by in enumerate((1, 3)):
                    half = self.held.at[part, self.core, m3, pl.ds(2 * (k ^ late), 2)]
                    self.send(2 + late, half, shifted(self.me, self.order[part][2], by))
        for part in self.parts:
            m1, m2, m3 = self.mine[part]
            for by in SHIFTS:
                self.send(6, self.held.at[part, self.core, m3, (m2 - by + 4) % 4], self.other)

    def fourth(self):
        self.copies.arrived(2)
        halves = []
        for part in self.parts:
            m3 = self.mine[part][2]
            for k, by in enumerate((1, 3)):
                half = self.held.at[part, self.core, (m3 - by + 4) % 4, pl.ds(2 * k, 2)]
                self.send(4, half, shifted(self.me, self.order[part][2], by))
                halves.append(half)
        for half in halves:
            self.send(7, half, self.other)

    def fifth(self):
        self.copies.arrived(3)
        for part in self.parts:
            m3 = self.mine[part][2]
            for k, by in enumerate((1, 3)):
                self.send(8, self.held.at[part, self.core, (m3 - by + 4) % 4, pl.ds(2 - 2 * k, 2)], self.other)
        self.copies.arrived(4)
        for part in self.parts:
            for k in range(2):
                half = self.held.at[part, self.core, (self.mine[part][2] + 2) % 4, pl.ds(2 * k, 2)]
                self.send(9, half, self.other)

    def last(self):
        for kind in range(5, 10):
            self.copies.arrived(kind)
        self.copies.finish()


def tables():
    early = np.zeros((112, 128), np.float32)
    late = np.zeros((96, 128), np.float32)
    mlp = np.zeros((192, 192), np.float32)
    for i in range(8):
        early[96 + i, 16 * i + 12] = 1
        for t in range(6):
            for w in range(2):
                early[48 * w + 6 * i + t, 16 * i + 6 * w + t] = 1
                late[48 * w + 6 * i + t, 16 * i + 6 * w + t] = 1
            for w in range(4):
                mlp[48 * w + 6 * i + t, 24 * i + 6 * w + t] = 1
    lane, column = np.arange(128)[:, None], np.arange(WIDTH)[None]
    short = ((lane < 48) & (lane % 6 == column % 6)).astype(np.float32)
    short_owner = (lane == column // 6).astype(np.float32)
    inner = (lane - 48 == column % 24).astype(np.float32)
    inner_owner = (lane[:32] == column // 24).astype(np.float32)
    return early, late, mlp, short, short_owner, inner, inner_owner


def block_bias(query_pos, query_seg, key_pos, key_seg):
    allowed = (query_seg == key_seg) & (jnp.abs(query_pos - key_pos) <= HALF_WIN)
    return jnp.where(allowed, 0.0, NEG_FILL)


class Local:
    def __init__(self, sems):
        self.sems, self.started = sems, {}

    def start(self, number, source, target):
        self.started[number] = pltpu.make_async_copy(source, target, self.sems.at[number])
        self.started[number].start()

    def wait(self, *numbers):
        for number in numbers or list(self.started):
            self.started.pop(number).wait()


def eight(held, order, part, group):
    return [held[slab_index(order, part, slab_place(group, member))] for member in range(8)]


def forward_kernel(
    wq_part, wk_part, wv_part, wo_part, win_part, wout_part,
    bq_part, bv_part, bo_part, ga_part, ba_part, bout_part, go_part, bo2_part, binner_part, x_ref, seg_ref,
    early_ref, late_ref, pick_mlp_ref, short_ref, short_owner_ref, inner_ref, inner_owner_ref,
    wq_any, wk_any, wv_any, wo_any, win_any, wout_any, q_any, qh_any, k_any, v_any,
    vec_ref, mixed_ref, lse_ref, segs_ref,
    wq, wk, wv, wo, win, wout, q, qh, k, v,
    held_e, held_l, held_m, rows, xh, bias, lse_cols,
    sems_e, sems_l, sems_m, sems_h, out_sem,
):
    me = coords()
    side = lax.axis_index("seq")
    short = (bq_part, bv_part, bo_part, ga_part, ba_part, bout_part, go_part, bo2_part)
    row = jnp.concatenate(
        [ref[...].astype(F32).reshape(1, 6) for ref in short]
        + [binner_part[...].astype(F32).reshape(1, 24), jnp.zeros((1, WIDTH - 72), F32)], axis=1,
    )
    early_rows = jnp.concatenate(
        [wk_part[...].astype(F32), wv_part[...].astype(F32), row, jnp.zeros((3, WIDTH), F32)], axis=0
    ).astype(BF)
    late_rows = jnp.concatenate(
        [wq_part[...].astype(F32), wo_part[...].astype(F32), jnp.zeros((4, WIDTH), F32)], axis=0
    ).astype(BF)
    for part in range(WIDES):
        held_e[slab_index(WIDE_ORDER, part, me)] = early_rows[:, WIDE * part : WIDE * (part + 1)]
        held_l[slab_index(WIDE_ORDER, part, me)] = late_rows[:, WIDE * part : WIDE * (part + 1)]
    greet(me)
    early = Gather(me, held_e, sems_e, WIDE_ORDER)
    late = Gather(me, held_l, sems_l, WIDE_ORDER)
    mlp = Gather(me, held_m, sems_m, ORDER)
    outs = Local(out_sem)
    partner = shifted(me, "z", 2)
    halo = Copies(sems_h, (xh, segs_ref.at[pl.ds(3, 2)]), partner)
    early.first()
    late.first()
    for n in range(3):
        segs_ref[n] = jnp.broadcast_to(seg_ref[:, BLOCK * n : BLOCK * (n + 1)].astype(F32), (8, BLOCK))
    mlp_rows = jnp.concatenate(
        [win_part[:, WIDTH * n : WIDTH * (n + 1)].astype(F32) for n in range(4)]
        + [wout_part[...].astype(F32)], axis=0,
    ).astype(BF)
    for part in range(PARTS):
        held_m[slab_index(ORDER, part, me)] = mlp_rows[:, PART * part : PART * (part + 1)]
    early.second()
    late.second()
    for n in range(2):
        block = jnp.where(side == 1, n, 2 - n)
        rows_out = x_ref.at[pl.ds(pl.multiple_of(block * BLOCK, BLOCK), BLOCK)]
        halo.send(0, rows_out, xh.at[pl.ds(n * BLOCK, BLOCK)], partner)
        halo.send(1, segs_ref.at[block], segs_ref.at[3 + n], partner)
    early.third()
    late.third()
    across = lax.broadcasted_iota(jnp.int32, (1, BLOCK), 1)
    down = lax.broadcasted_iota(jnp.int32, (BLOCK, 1), 0)
    starts = [BLOCK * n for n in range(3)] + [
        jnp.where(side == 0, 768 + BLOCK * n, -BLOCK * (n + 1)) for n in range(2)
    ]
    blocks = [jnp.where(side == 0, b, 2 - b) for b in range(3)]

    def fill_bias(b, key_blocks):
        seg_here = segs_ref[blocks[b], 0:1, :]
        seg_down = jnp.broadcast_to(seg_here, (128, BLOCK)).T[:, 0:1]
        for n in key_blocks:
            bias[b, :, pl.ds(n * BLOCK, BLOCK)] = block_bias(
                blocks[b] * BLOCK + down, seg_down, starts[n] + across, segs_ref[n, 0:1, :]
            )

    for b in range(3):
        fill_bias(b, range(3))
    mlp.first()
    early.fourth()
    late.fourth()
    early.fifth()
    late.fifth()
    early.last()
    mlp.second()

    def unpack_early(group, _):
        at = pl.ds(pl.multiple_of(group * 48, 16), 48)
        for part in range(WIDES):
            picked = dot(early_ref[...], jnp.concatenate(eight(held_e, WIDE_ORDER, part, group), axis=0))
            for n, ref in enumerate((wk, wv)):
                ref[at, pl.ds(part * WIDE, WIDE)] = picked[48 * n : 48 * n + 48].astype(BF)
            if part == 0:
                rows[pl.ds(pl.multiple_of(group * 8, 8), 8), :] = picked[96:104, :128]
        return 0

    lax.fori_loop(0, 16, unpack_early, 0, unroll=4)
    outs.start(0, wk, wk_any)
    outs.start(1, wv, wv_any)
    lane = lax.broadcasted_iota(jnp.int32, (1, 128), 1)
    for n in range(2):
        chosen = jnp.where((lane >= 6 * n) & (lane < 6 * n + 6), rows[...], 0.0).astype(BF)
        vec_ref[n : n + 1, :] = jnp.sum(
            dot(chosen, short_ref[...]) * short_owner_ref[...], axis=0, keepdims=True
        )
    def project_key(tokens, at):
        k[at, :] = dot(tokens[...], wk[...]).astype(BF)
        v[at, :] = (dot(tokens[...], wv[...]) + vec_ref[1:2, :]).astype(BF)

    def project_query(tokens, target):
        target[...] = (dot(tokens[...], wq[...]) + vec_ref[0:1, :]).astype(BF) * jnp.asarray(0.125, BF)

    project_key(x_ref, pl.ds(0, 768))
    late.last()
    for n in range(2, 8):
        chosen = jnp.where((lane >= 6 * n) & (lane < 6 * n + 6), rows[...], 0.0).astype(BF)
        vec_ref[n : n + 1, :] = jnp.sum(
            dot(chosen, short_ref[...]) * short_owner_ref[...], axis=0, keepdims=True
        )
    for n in range(4):
        chosen = rows[pl.ds(32 * n, 32), :].astype(BF)
        vec_ref[8 + n : 9 + n, :] = jnp.sum(
            dot(chosen, inner_ref[...]) * inner_owner_ref[...], axis=0, keepdims=True
        )

    mlp.third()

    def unpack_late(group, _):
        at = pl.ds(pl.multiple_of(group * 48, 16), 48)
        for part in range(WIDES):
            picked = dot(late_ref[...], jnp.concatenate(eight(held_l, WIDE_ORDER, part, group), axis=0))
            for n, ref in enumerate((wq, wo)):
                ref[at, pl.ds(part * WIDE, WIDE)] = picked[48 * n : 48 * n + 48].astype(BF)
        return 0

    lax.fori_loop(0, 16, unpack_late, 0, unroll=4)
    outs.start(2, wq, wq_any)
    outs.start(3, wo, wo_any)
    project_query(x_ref, q)
    outs.start(4, q, q_any)

    low = lane < 64

    def attend(pair, those):
        columns = pl.ds(pl.multiple_of(pair * 128, 128), 128)
        items = [(b, e) for b in those for e in range(2)]

        def place(b):
            return pl.ds(pl.multiple_of(blocks[b] * BLOCK, BLOCK), BLOCK)

        def scores_of(b, e):
            count = 768 + BLOCK * b
            queries = jnp.where(low if e == 0 else ~low, q[place(b), columns], jnp.zeros((), BF))
            return dot(queries, k[pl.ds(0, count), columns], NT) + bias[b, :, pl.ds(0, count)]

        scores, outs_of = scores_of(*items[0]), []
        for n, (b, e) in enumerate(items):
            later = scores_of(*items[n + 1]) if n + 1 < len(items) else None
            top = jnp.max(scores, axis=1, keepdims=True)
            weights = jnp.exp(scores - top).astype(BF)
            values = v[pl.ds(0, 768 + BLOCK * b), columns]
            out = dot(weights, jnp.where(low if e == 0 else ~low, values, jnp.ones((), BF)))
            outs_of.append(out)
            total = out[:, 64:65] if e == 0 else out[:, 0:1]
            lse_cols[place(b), :] = jnp.where(
                lane == 2 * pair + e, top + jnp.log(total), lse_cols[place(b), :]
            )
            scores = later
            if e == 1:
                sums = pltpu.roll(jnp.where(low, outs_of[1], outs_of[0]), 64, 1)
                mixed_ref[place(b), columns] = (jnp.where(low, outs_of[0], outs_of[1]) / sums).astype(BF)
                outs_of = []

    def attend_near(pair, _):
        attend(pair, (0,))
        return 0

    def attend_far(pair, _):
        attend(pair, (1, 2))
        return 0

    lax.fori_loop(0, 6, attend_near, 0, unroll=2)
    halo.arrived(0)
    halo.arrived(1)
    for b in range(1, 3):
        fill_bias(b, range(3, 3 + b))
    project_key(xh, pl.ds(768, 512))
    project_query(xh, qh)
    outs.start(5, qh, qh_any)
    outs.start(6, k, k_any)
    outs.start(7, v, v_any)
    mlp.fourth()
    lax.fori_loop(0, 3, attend_far, 0)
    mlp.fifth()
    lax.fori_loop(3, 5, attend_far, 0)
    mlp.last()

    def unpack_mlp(group, _):
        at = pl.ds(pl.multiple_of(group * 48, 16), 48)
        at_outer = pl.ds(pl.multiple_of(group * 192, 64), 192)
        for part in range(PARTS):
            slabs = eight(held_m, ORDER, part, group)
            picked = dot(pick_mlp_ref[...], jnp.concatenate([slab[:24] for slab in slabs], axis=0)).astype(BF)
            for n in range(4):
                win[at, pl.ds(n * WIDTH + part * PART, PART)] = picked[48 * n : 48 * n + 48]
            wout[at_outer, pl.ds(part * PART, PART)] = jnp.concatenate([slab[24:] for slab in slabs], axis=0)
        return 0

    lax.fori_loop(0, 16, unpack_mlp, 0, unroll=4)
    outs.start(8, win, win_any)
    outs.start(9, wout, wout_any)
    lax.fori_loop(5, 6, attend_far, 0)
    for b in range(3):
        lse_ref[b] = lse_cols[pl.ds(b * BLOCK, BLOCK), :].T[:16]
    halo.finish()
    outs.wait()


def run_forward(parts, tokens, seg_row):
    early, late, mlp, short, short_owner, inner, inner_owner = tables()
    fixed = (
        jnp.asarray(early, BF), jnp.asarray(late, BF), jnp.asarray(mlp, BF), jnp.asarray(short, BF),
        jnp.asarray(short_owner), jnp.asarray(inner, BF), jnp.asarray(inner_owner),
    )
    vmem, anywhere = pl.BlockSpec(memory_space=pltpu.VMEM), pl.BlockSpec(memory_space=pl.ANY)
    large = (
        [(768, 768)] * 4 + [(768, 3072), (3072, 768), (768, 768), (512, 768), (1280, 768), (1280, 768)]
    )
    small = [((16, 768), F32), ((768, 768), BF), ((3, 16, BLOCK), F32), ((5, 8, BLOCK), F32)]
    sems = pltpu.SemaphoreType.DMA
    return pl.pallas_call(
        forward_kernel,
        out_shape=tuple(jax.ShapeDtypeStruct(shape, BF) for shape in large)
        + tuple(jax.ShapeDtypeStruct(*shape) for shape in small),
        in_specs=[vmem] * 24,
        out_specs=(anywhere,) * len(large) + (vmem,) * len(small),
        scratch_shapes=[
            *(pltpu.VMEM(shape, BF) for shape in large),
            pltpu.VMEM((WIDES, 2, 4, 4, 4, ATTN_ROWS, WIDE), BF),
            pltpu.VMEM((WIDES, 2, 4, 4, 4, ATTN_ROWS, WIDE), BF),
            pltpu.VMEM((PARTS, 2, 4, 4, 4, MLP_ROWS, PART), BF),
            pltpu.VMEM((128, 128), F32),
            pltpu.VMEM((512, 768), BF),
            pltpu.VMEM((3, BLOCK, 1280), F32),
            pltpu.VMEM((768, 128), F32),
            *(sems((2, Gather.KINDS)) for _ in range(3)), sems((2, 2)), sems((10,)),
        ],
        compiler_params=pltpu.CompilerParams(
            collective_id=0, has_side_effects=True, vmem_limit_bytes=VMEM_BYTES
        ),
        name="gather_and_attend",
    )(*parts, tokens, seg_row, *fixed)


class Scatter:
    KINDS = 8

    def __init__(self, me, parts, own, near, halves, blocks, second, first, sems, order):
        self.order, self.every = order, range(len(order))
        self.me, self.core = me, me["c"]
        self.parts, self.own, self.near, self.halves = parts, own, near, halves
        self.blocks, self.second, self.first = blocks, second, first
        self.other = shifted(me, "c", 1)
        sizes = (near.at[:, 0],) * 4 + (halves, blocks, second, first)
        self.copies = Copies(sems, sizes, self.other)
        self.mine = [tuple(me[axis] for axis in order[part]) for part in self.every]

    def add(self, target, sources, count):
        def body(index, _):
            if len(sources) == 1:
                target[index] = target[index] + sources[0][index]
            else:
                total = target[index].astype(F32)
                for source in sources:
                    total = total + source[index].astype(F32)
                target[index] = total.astype(BF)
            return 0

        lax.fori_loop(0, count, body, 0)

    def to_sibling(self):
        for k, by in enumerate((2, 1, 3, 0)):
            for part in self.every:
                at = (self.mine[part][2] + by) % 4
                self.copies.send(k, self.parts.at[part, 1 - self.core, at], self.near.at[part, at], self.other)

    def near_sum(self, k, by):
        self.copies.arrived(k)
        for part in self.every:
            at = (self.mine[part][2] + by) % 4
            self.add(self.near.at[part, at], [self.own(part, at)], 4)

    def opposite(self):
        self.near_sum(0, 2)
        for part in self.every:
            m3 = self.mine[part][2]
            for k, by in enumerate((1, 3)):
                half = self.near.at[part, (m3 + 2) % 4, pl.ds(2 * k, 2)]
                self.copies.send(4, half, self.halves.at[part, k], shifted(self.me, self.order[part][2], by))

    def nearest(self):
        self.near_sum(1, 1)
        self.near_sum(2, 3)
        self.near_sum(3, 0)

    def neighbours(self):
        self.copies.arrived(4)
        for part in self.every:
            m3 = self.mine[part][2]
            for k, by in enumerate((1, 3)):
                block = self.near.at[part, (m3 + by) % 4]
                self.add(block.at[pl.ds(2 * k, 2)], [self.halves.at[part, k]], 2)
                self.copies.send(5, block, self.blocks.at[part, k], shifted(self.me, self.order[part][2], by))

    def middle(self):
        self.copies.arrived(5)
        for part in self.every:
            m1, m2, m3 = self.mine[part]
            block = self.near.at[part, m3]
            self.add(block, [self.blocks.at[part, 0], self.blocks.at[part, 1]], 4)
            for k, by in enumerate(SHIFTS):
                self.copies.send(
                    6, block.at[(m2 + by) % 4], self.second.at[part, k], shifted(self.me, self.order[part][1], by)
                )

    def final(self):
        self.copies.arrived(6)
        for part in self.every:
            m1, m2, m3 = self.mine[part]
            block = self.near.at[part, m3, pl.ds(m2, 1)]
            self.add(block, [self.second.at[part, pl.ds(k, 1)] for k in range(3)], 1)
            for k, by in enumerate(SHIFTS):
                self.copies.send(
                    7, block.at[0, (m1 + by) % 4], self.first.at[part, k], shifted(self.me, self.order[part][0], by)
                )

    def result(self, out_ref):
        self.copies.arrived(7)
        for part in self.every:
            m1, m2, m3 = self.mine[part]
            total = self.near[part, m3, m2, m1].astype(F32)
            for k in range(3):
                total = total + self.first[part, k].astype(F32)
            out_ref[part] = total
        self.copies.finish()


def row_sum(block):
    return jnp.sum(block, axis=0, keepdims=True)


def normed_of(hidden):
    centred = hidden - jnp.mean(hidden, axis=1, keepdims=True)
    inverse = lax.rsqrt(jnp.mean(centred * centred, axis=1, keepdims=True) + EPS)
    return centred * inverse, inverse


def dense_kernel(
    x_any, mixed_any, cot_any, wo_any, win_any, wout_any, vec_ref, put_mlp_ref, heads_ref,
    out_any, dwo_any, hidden_any, gmix_any, parts_any, delta_ref, sums_ref,
    x, mixed, cot, wo, win, wout, out, gmix, parts,
    active, slope, normed, inverse, first_bf, total, grad_bf, load_sem, store_sem, chunk_sem,
):
    loads, stores = Local(load_sem), Local(store_sem)
    for n, (source, target) in enumerate(((mixed_any, mixed), (wo_any, wo), (x_any, x))):
        loads.start(n, source, target)

    def chunk_loads(index):
        columns = pl.ds(pl.multiple_of(index * WIDTH, WIDTH), WIDTH)
        return (
            pltpu.make_async_copy(win_any.at[:, columns], win.at[:, columns], chunk_sem.at[0, index]),
            pltpu.make_async_copy(wout_any.at[columns], wout.at[columns], chunk_sem.at[1, index]),
        )

    sums_ref[...] = jnp.zeros_like(sums_ref)

    def add_sum(row, block):
        sums_ref[pl.ds(row, 1), :] += row_sum(block)

    def row_block(index):
        return pl.ds(pl.multiple_of(index * BLOCK, BLOCK), BLOCK)

    def norm_one(index, _):
        at = row_block(index)
        hidden = x[at, :].astype(F32) + (dot(mixed[at, :], wo[...]) + vec_ref[2:3, :])
        normed[at, :], spread = normed_of(hidden)
        inverse[at, :] = jnp.broadcast_to(spread, (BLOCK, 128))
        first_bf[at, :] = (normed[at, :] * vec_ref[3:4, :] + vec_ref[4:5, :]).astype(BF)
        return 0

    loads.wait(0, 1, 2)
    for n in range(4):
        for one in chunk_loads(n):
            one.start()
    loads.start(3, cot_any, cot)
    lax.fori_loop(0, 3, norm_one, 0)
    total[...] = jnp.zeros_like(total)
    rate, bend = math.sqrt(2 / math.pi), 0.044715

    def inner_block(index, _):
        columns = pl.ds(pl.multiple_of(index * WIDTH, WIDTH), WIDTH)
        for one in chunk_loads(index):
            one.wait()
        u = dot(first_bf[...], win[:, columns]) + vec_ref[pl.ds(8 + index, 1), :]
        square = u * u
        bent = jnp.tanh(rate * u * (1 + bend * square))
        half = 0.5 * (1 + bent)
        active[:, columns] = (u * half).astype(BF)
        slope[:, columns] = (
            half + u * half * (1 - bent) * (rate + (3 * rate * bend) * square)
        ).astype(BF)
        total[...] += dot(active[:, columns], wout[columns, :])
        return 0

    lax.fori_loop(0, 4, inner_block, 0)
    loads.wait(3)

    def norm_two(index, _):
        at = row_block(index)
        first = normed[at, :] * vec_ref[3:4, :] + vec_ref[4:5, :]
        normed_two, spread = normed_of(first + (total[at, :] + vec_ref[5:6, :]))
        out[at, :] = (normed_two * vec_ref[6:7, :] + vec_ref[7:8, :]).astype(BF)
        grad = cot[at, :].astype(F32)
        add_sum(6, grad * normed_two)
        add_sum(7, grad)
        scaled = grad * vec_ref[6:7, :]
        mean_grad = jnp.mean(scaled, axis=1, keepdims=True)
        mean_cross = jnp.mean(scaled * normed_two, axis=1, keepdims=True)
        back = spread * (scaled - mean_grad - normed_two * mean_cross)
        total[at, :] = back
        grad_bf[at, :] = back.astype(BF)
        add_sum(5, grad_bf[at, :].astype(F32))
        return 0

    lax.fori_loop(0, 3, norm_two, 0)
    stores.start(0, out, out_any)

    def outer_block(index, _):
        columns = pl.ds(pl.multiple_of(index * WIDTH, WIDTH), WIDTH)
        grad_inner = (dot(grad_bf[...], wout[columns, :], NT) * slope[:, columns].astype(F32)).astype(BF)
        add_sum(8 + index, grad_inner.astype(F32))
        total[...] += dot(grad_inner, win[:, columns], NT)
        active[:, columns] = dot(active[:, columns], grad_bf[...], TN).astype(BF)
        slope[:, columns] = dot(first_bf[...], grad_inner, TN).astype(BF)
        return 0

    lax.fori_loop(0, 4, outer_block, 0)

    def back_one(index, _):
        at = row_block(index)
        grad, normed_one = total[at, :], normed[at, :]
        add_sum(3, grad * normed_one)
        add_sum(4, grad)
        scaled = grad * vec_ref[3:4, :]
        mean_grad = jnp.mean(scaled, axis=1, keepdims=True)
        mean_cross = jnp.mean(scaled * normed_one, axis=1, keepdims=True)
        back = inverse[at, 0:1] * (scaled - mean_grad - normed_one * mean_cross)
        total[at, :] = back
        grad_bf[at, :] = back.astype(BF)
        add_sum(2, grad_bf[at, :].astype(F32))
        return 0

    lax.fori_loop(0, 3, back_one, 0)
    stores.start(1, total, hidden_any)
    gmix[...] = dot(grad_bf[...], wo[...], NT).astype(BF)
    stores.start(2, gmix, gmix_any)
    first_bf[...] = dot(mixed[...], grad_bf[...], TN).astype(BF)
    stores.start(3, first_bf, dwo_any)

    for part in range(WIDES):

        def pack(group, _):
            at = pl.ds(pl.multiple_of(group * 48, 16), 48)
            at_outer = pl.ds(pl.multiple_of((group % 4) * 192, 64), 192)
            pieces = [slope[at, pl.ds(k * WIDTH + part * WIDE, WIDE)] for k in range(4)]
            placed = dot(put_mlp_ref[...], jnp.concatenate(pieces, axis=0)).astype(BF)
            outer_columns = pl.ds(pl.multiple_of((group // 4) * WIDTH + part * WIDE, 128), WIDE)
            outer = active[at_outer, outer_columns]
            for member in range(8):
                these = slice(24 * member, 24 * member + 24)
                parts[slab_index(WIDE_ORDER, part, slab_place(group, member))] = jnp.concatenate(
                    [placed[these], outer[these]], axis=0
                )
            return 0

        lax.fori_loop(0, 16, pack, 0, unroll=4)
        stores.start(4 + part, parts.at[part], parts_any.at[part])
    for k in range(3):
        at = pl.ds(BLOCK * k, BLOCK)
        product = mixed[at, :].astype(F32) * gmix[at, :].astype(F32)
        high = product.astype(BF)
        rest = (product - high.astype(F32)).astype(BF)
        delta_ref[k] = dot(heads_ref[...], high, NT) + dot(heads_ref[...], rest, NT)
    stores.wait()


def run_dense(tokens, mixed, cot, wo, win, wout, vec):
    mlp = tables()[2]
    heads = (np.arange(16)[:, None] == np.arange(WIDTH)[None] // 64).astype(np.float32)
    vmem, anywhere = pl.BlockSpec(memory_space=pltpu.VMEM), pl.BlockSpec(memory_space=pl.ANY)
    parts_shape = (WIDES, 2, 4, 4, 4, MLP_ROWS, WIDE)
    shapes = (
        ((768, 768), BF), ((768, 768), BF), ((768, 768), F32), ((768, 768), BF), (parts_shape, BF),
        ((3, 16, BLOCK), F32), ((16, 768), F32),
    )
    sems = pltpu.SemaphoreType.DMA
    return pl.pallas_call(
        dense_kernel,
        out_shape=tuple(jax.ShapeDtypeStruct(*shape) for shape in shapes),
        in_specs=[anywhere] * 6 + [vmem] * 3,
        out_specs=(anywhere,) * 5 + (vmem,) * 2,
        scratch_shapes=[
            *(pltpu.VMEM((768, 768), BF) for _ in range(4)),
            pltpu.VMEM((768, 3072), BF), pltpu.VMEM((3072, 768), BF),
            pltpu.VMEM((768, 768), BF), pltpu.VMEM((768, 768), BF), pltpu.VMEM(parts_shape, BF),
            pltpu.VMEM((768, 3072), BF), pltpu.VMEM((768, 3072), BF), pltpu.VMEM((768, 768), F32),
            pltpu.VMEM((768, 128), F32), pltpu.VMEM((768, 768), BF), pltpu.VMEM((768, 768), F32),
            pltpu.VMEM((768, 768), BF), sems((4,)), sems((7,)), sems((2, 4)),
        ],
        compiler_params=pltpu.CompilerParams(vmem_limit_bytes=VMEM_BYTES),
        name="feed_forward",
    )(tokens, mixed, cot, wo, win, wout, vec, jnp.asarray(mlp.T, BF), jnp.asarray(heads, BF))


def backward_kernel(
    q_any, qh_any, k_any, v_any, g_any, x_any, wq_any, wk_any, wv_any, hidden_any, mlp_any,
    lse_ref, delta_ref, segs_ref, dwo_ref, sums_ref, put_early_ref, put_late_ref, short_ref,
    short_owner_ref, inner_ref, inner_owner_ref,
    grad_any, early_out, late_out, mlp_out,
    q, qh, k, v, g, gh, stats, own_m, bias, bias_h, dq, dk, dv, dwq, dwk, dwv, rows, hidden,
    parts_e, parts_l, near_e, halves_e, blocks_e, second_e, first_e,
    near_l, halves_l, blocks_l, second_l, first_l,
    near_m, halves_m, blocks_m, second_m, first_m,
    load_sem, sems_e, sems_l, sems_m, sems_h,
):
    me = coords()
    core = me["c"]
    side = lax.axis_index("seq")
    partner = shifted(me, "z", 2)
    loads = Local(load_sem)
    for number, (source, target) in enumerate(
        ((g_any, g), (q_any, q), (k_any, k), (v_any, v), (qh_any, qh), (mlp_any.at[:, core], own_m), (hidden_any, hidden))
    ):
        loads.start(number, source, target)
    for b in range(3):
        stats[b, 0:16, :] = lse_ref[b]
        stats[b, 16:32, :] = delta_ref[b]
    greet(me)
    mlp = Scatter(
        me, mlp_any, lambda part, at: own_m.at[part, at], near_m, halves_m, blocks_m, second_m, first_m,
        sems_m, WIDE_ORDER,
    )
    early = Scatter(
        me, parts_e, lambda part, at: parts_e.at[part, core, at], near_e, halves_e, blocks_e, second_e,
        first_e, sems_e, ORDER,
    )
    late = Scatter(
        me, parts_l, lambda part, at: parts_l.at[part, core, at], near_l, halves_l, blocks_l, second_l,
        first_l, sems_l, ORDER,
    )
    halo = Copies(sems_h, (gh, stats.at[pl.ds(3, 2)]), partner)
    loads.wait(0)
    for n in range(2):
        block = jnp.where(side == 1, n, 2 - n)
        rows_out = g.at[pl.ds(pl.multiple_of(block * BLOCK, BLOCK), BLOCK)]
        halo.send(0, rows_out, gh.at[pl.ds(n * BLOCK, BLOCK)], partner)
        halo.send(1, stats.at[block], stats.at[3 + n], partner)
    mlp.to_sibling()

    across = lax.broadcasted_iota(jnp.int32, (1, BLOCK), 1)
    down = lax.broadcasted_iota(jnp.int32, (BLOCK, 1), 0)
    starts = [BLOCK * n for n in range(3)] + [
        jnp.where(side == 0, 768 + BLOCK * n, -BLOCK * (n + 1)) for n in range(2)
    ]
    blocks = [jnp.where(side == 0, b, 2 - b) for b in range(3)]

    def seg_down(block):
        return jnp.broadcast_to(segs_ref[block, 0:1, :], (128, BLOCK)).T[:, 0:1]

    for n in range(5):
        seg_key, key_pos = seg_down(n), starts[n] + down
        for b in range(max(0, n - 2), 3):
            bias[b, pl.ds(n * BLOCK, BLOCK), :] = block_bias(
                blocks[b] * BLOCK + across, segs_ref[blocks[b], 0:1, :], key_pos, seg_key
            )
    reach = [
        (jnp.where(side == 0, BLOCK * (1 + n), 0), BLOCK * (2 - n)) for n in range(2)
    ]
    for n in range(2):
        for m in range(2 - n):
            block = jnp.where(side == 0, 1 + n + m, m)
            bias_h[n, pl.ds(m * BLOCK, BLOCK), :] = block_bias(
                starts[3 + n] + across, segs_ref[3 + n, 0:1, :], block * BLOCK + down, seg_down(block)
            )
    dk[...] = jnp.zeros_like(dk)
    dv[...] = jnp.zeros_like(dv)
    low = lax.broadcasted_iota(jnp.int32, (1, 128), 1) < 64
    nothing = jnp.zeros((), BF)

    def weights_back(keys, values, queries, grads, shift, stat, head):
        scores = dot(keys, queries, NT) + shift
        probs = jnp.exp(scores - stats[stat, pl.ds(head, 1), :])
        grad_probs = dot(values, grads, NT)
        grad_scores = probs * (grad_probs - stats[stat, pl.ds(16 + head, 1), :])
        return probs.astype(BF), grad_scores.astype(BF)

    def own_pair(pair, _):
        columns = pl.ds(pl.multiple_of(pair * 128, 128), 128)
        for b in range(3):
            count = 768 + BLOCK * b
            at = pl.ds(pl.multiple_of(blocks[b] * BLOCK, BLOCK), BLOCK)
            queries, grads = q[at, columns], g[at, columns]
            keys, values = k[pl.ds(0, count), columns], v[pl.ds(0, count), columns]
            grad_query = jnp.zeros((BLOCK, 128), F32)
            for e in range(2):
                keep = low if e == 0 else ~low
                queries_e, grads_e = jnp.where(keep, queries, nothing), jnp.where(keep, grads, nothing)
                probs, grad_scores = weights_back(
                    keys, values, queries_e, grads_e, bias[b, pl.ds(0, count), :], blocks[b], 2 * pair + e
                )
                dk[:, columns] += dot(grad_scores[:768], queries_e)
                dv[:, columns] += dot(probs[:768], grads_e)
                grad_query += dot(grad_scores, jnp.where(keep, keys, nothing), TN)
            dq[at, columns] = (grad_query * 0.125).astype(BF)
        return 0

    def halo_pair(pair, _):
        columns = pl.ds(pl.multiple_of(pair * 128, 128), 128)
        for n in range(2):
            start, count = reach[n]
            at = pl.ds(pl.multiple_of(start, BLOCK), count)
            here = pl.ds(n * BLOCK, BLOCK)
            queries, grads = qh[here, columns], gh[here, columns]
            keys, values = k[at, columns], v[at, columns]
            for e in range(2):
                keep = low if e == 0 else ~low
                queries_e, grads_e = jnp.where(keep, queries, nothing), jnp.where(keep, grads, nothing)
                probs, grad_scores = weights_back(
                    keys, values, queries_e, grads_e, bias_h[n, pl.ds(0, count), :], 3 + n, 2 * pair + e
                )
                dk[at, columns] += dot(grad_scores, queries_e)
                dv[at, columns] += dot(probs, grads_e)
        return 0

    loads.wait(1, 2, 3, 4, 5)
    lax.fori_loop(0, 1, own_pair, 0)
    mlp.opposite()
    lax.fori_loop(1, 3, own_pair, 0)
    mlp.nearest()
    mlp.neighbours()
    lax.fori_loop(3, 6, own_pair, 0)
    halo.finish()
    loads.start(7, x_any, g)
    loads.start(8, wq_any, q)
    loads.wait(7)
    dwq[...] = dot(g[...], dq[...], TN).astype(BF)

    def pack_late(group, _):
        at = pl.ds(pl.multiple_of(group * 48, 16), 48)
        for part in range(PARTS):
            columns = pl.ds(part * PART, PART)
            pieces = jnp.concatenate([dwq[at, columns], dwo_ref[at, columns]], axis=0)
            placed = dot(put_late_ref[...], pieces).astype(BF)
            for member in range(8):
                parts_l[slab_index(ORDER, part, slab_place(group, member))] = placed[16 * member : 16 * member + 16]
        return 0

    lax.fori_loop(0, 16, pack_late, 0, unroll=4)
    late.to_sibling()
    mlp.middle()
    halo.arrived(0)
    halo.arrived(1)
    lax.fori_loop(0, 2, halo_pair, 0)
    late.opposite()
    late.nearest()
    lax.fori_loop(2, 4, halo_pair, 0)
    late.neighbours()
    lax.fori_loop(4, 6, halo_pair, 0)
    mlp.final()
    loads.start(9, wk_any, k.at[pl.ds(0, 768)])
    loads.start(10, wv_any, v.at[pl.ds(0, 768)])
    dwk[...] = dot(g[...], dk[...].astype(BF), TN).astype(BF)
    dwv[...] = dot(g[...], dv[...].astype(BF), TN).astype(BF)

    rows[...] = jnp.zeros_like(rows)
    lane = lax.broadcasted_iota(jnp.int32, (1, 128), 1)
    for n in range(8):
        if n == 0:
            vec = row_sum(dq[...].astype(F32))
        elif n == 1:
            vec = row_sum(dv[...].astype(BF).astype(F32))
        else:
            vec = sums_ref[n : n + 1, :]
        spread = dot((short_owner_ref[...] * vec).astype(BF), short_ref[...], NT)
        rows[...] = jnp.where((lane >= 6 * n) & (lane < 6 * n + 6), spread, rows[...])
    for n in range(4):
        spread = dot((inner_owner_ref[...] * sums_ref[8 + n : 9 + n, :]).astype(BF), inner_ref[...], NT)
        at = pl.ds(32 * n, 32)
        rows[at, :] = jnp.where((lane >= 48) & (lane < 72), spread, rows[at, :])

    def pack_early(group, _):
        at = pl.ds(pl.multiple_of(group * 48, 16), 48)
        vec = rows[pl.ds(pl.multiple_of(group * 8, 8), 8), :]
        vec = jnp.concatenate([vec, jnp.zeros_like(vec)], axis=1)
        vec = jnp.concatenate([vec, jnp.zeros_like(vec)], axis=0).astype(BF)
        for part in range(PARTS):
            columns = pl.ds(part * PART, PART)
            last = vec if part == 0 else jnp.zeros_like(vec)
            pieces = jnp.concatenate([dwk[at, columns], dwv[at, columns], last], axis=0)
            placed = dot(put_early_ref[...], pieces).astype(BF)
            for member in range(8):
                parts_e[slab_index(ORDER, part, slab_place(group, member))] = placed[16 * member : 16 * member + 16]
        return 0

    lax.fori_loop(0, 16, pack_early, 0, unroll=4)
    early.to_sibling()
    late.middle()
    loads.wait(6, 8)
    hidden[...] += dot(dq[...], q[...], NT)
    early.opposite()
    early.nearest()
    loads.wait(9)
    hidden[...] += dot(dk[...].astype(BF), k[pl.ds(0, 768), :], NT)
    early.neighbours()
    late.final()
    loads.wait(10)
    hidden[...] += dot(dv[...].astype(BF), v[pl.ds(0, 768), :], NT)
    loads.start(11, hidden, grad_any)
    mlp.result(mlp_out)
    early.middle()
    late.result(late_out)
    early.final()
    early.result(early_out)
    loads.wait()


def run_backward(q, qh, k, v, g, x, wq, wk, wv, hidden, mlp, lse, delta, segs, dwo, sums):
    early, late, _, short, short_owner, inner, inner_owner = tables()
    fixed = (
        jnp.asarray(early.T, BF), jnp.asarray(late.T, BF), jnp.asarray(short, BF),
        jnp.asarray(short_owner), jnp.asarray(inner, BF), jnp.asarray(inner_owner),
    )
    vmem, anywhere = pl.BlockSpec(memory_space=pltpu.VMEM), pl.BlockSpec(memory_space=pl.ANY)
    sems = pltpu.SemaphoreType.DMA

    def steps(parts, rows, width):
        return [
            pltpu.VMEM((parts, *lead, rows, width), BF)
            for lead in ((4, 4, 4), (2, 2, 4), (2, 4, 4), (3, 4), (3,))
        ]

    return pl.pallas_call(
        backward_kernel,
        out_shape=(
            jax.ShapeDtypeStruct((768, 768), F32),
            jax.ShapeDtypeStruct((PARTS, ATTN_ROWS, PART), F32),
            jax.ShapeDtypeStruct((PARTS, ATTN_ROWS, PART), F32),
            jax.ShapeDtypeStruct((WIDES, MLP_ROWS, WIDE), F32),
        ),
        in_specs=[anywhere] * 11 + [vmem] * 11,
        out_specs=(anywhere, vmem, vmem, vmem),
        scratch_shapes=[
            pltpu.VMEM((768, 768), BF), pltpu.VMEM((512, 768), BF),
            pltpu.VMEM((1280, 768), BF), pltpu.VMEM((1280, 768), BF),
            pltpu.VMEM((768, 768), BF), pltpu.VMEM((512, 768), BF),
            pltpu.VMEM((5, 32, BLOCK), F32),
            pltpu.VMEM((WIDES, 4, 4, 4, MLP_ROWS, WIDE), BF),
            pltpu.VMEM((3, 1280, BLOCK), F32), pltpu.VMEM((2, 512, BLOCK), F32),
            pltpu.VMEM((768, 768), BF), pltpu.VMEM((768, 768), F32), pltpu.VMEM((768, 768), F32),
            *(pltpu.VMEM((768, 768), BF) for _ in range(3)),
            pltpu.VMEM((128, 128), F32), pltpu.VMEM((768, 768), F32),
            pltpu.VMEM((PARTS, 2, 4, 4, 4, ATTN_ROWS, PART), BF),
            pltpu.VMEM((PARTS, 2, 4, 4, 4, ATTN_ROWS, PART), BF),
            *steps(PARTS, ATTN_ROWS, PART), *steps(PARTS, ATTN_ROWS, PART), *steps(WIDES, MLP_ROWS, WIDE),
            sems((12,)), *(sems((2, Scatter.KINDS)) for _ in range(3)), sems((2, 2)),
        ],
        compiler_params=pltpu.CompilerParams(
            collective_id=1, has_side_effects=True, vmem_limit_bytes=VMEM_BYTES
        ),
        name="attend_back_and_scatter",
    )(q, qh, k, v, g, x, wq, wk, wv, hidden, mlp, lse, delta, segs, dwo, sums, *fixed)


def split_kernel(early_ref, late_ref, mlp_ref, grad_any, grad_out, wq, wk, wv, wo, win, wout, inner, *rest):
    short, staged, sems = rest[:8], rest[8], rest[9]
    moves = []
    for k in range(3):
        at = pl.ds(BLOCK * k, BLOCK)
        moves.append([
            pltpu.make_async_copy(grad_any.at[at], staged.at[at], sems.at[0, k]),
            pltpu.make_async_copy(staged.at[at], grad_out.at[at], sems.at[1, k]),
        ])
        moves[k][0].start()
    for fetch, put in moves:
        fetch.wait()
        put.start()
    for part in range(PARTS):
        columns = pl.ds(PART * part, PART)
        for ref, source, row in ((wk, early_ref, 0), (wv, early_ref, 6), (wq, late_ref, 0), (wo, late_ref, 6)):
            ref[:, columns] = source[part, row : row + 6, :]
    for part in range(WIDES):
        for k in range(4):
            win[:, pl.ds(WIDTH * k + WIDE * part, WIDE)] = mlp_ref[part, 6 * k : 6 * k + 6, :]
        wout[:, pl.ds(WIDE * part, WIDE)] = mlp_ref[part, 24:48, :]
    inner[...] = early_ref[0, 12, 48:72]
    for k in range(8):
        short[k][...] = early_ref[0, 12, 6 * k : 6 * k + 6]
    for fetch, put in moves:
        put.wait()


def split_results(early, late, mlp, grad):
    vmem, anywhere = pl.BlockSpec(memory_space=pltpu.VMEM), pl.BlockSpec(memory_space=pl.ANY)
    shapes = ((768, 768),) + ((6, 768),) * 4 + ((6, 3072), (24, 768), (24,)) + ((6,),) * 8
    return pl.pallas_call(
        split_kernel,
        out_shape=tuple(jax.ShapeDtypeStruct(shape, F32) for shape in shapes),
        in_specs=[vmem] * 3 + [anywhere],
        out_specs=(anywhere,) + (vmem,) * (len(shapes) - 1),
        scratch_shapes=[pltpu.VMEM((768, 768), F32), pltpu.SemaphoreType.DMA((2, 3))],
        compiler_params=pltpu.CompilerParams(vmem_limit_bytes=VMEM_BYTES),
        name="split_gradients",
    )(early, late, mlp, grad)


def per_device(
    inputs,
    segments,
    w_query,
    w_key,
    w_value,
    w_output,
    b_query,
    b_value,
    b_output,
    gain_attn,
    bias_attn,
    w_inner,
    b_inner,
    w_outer,
    b_outer,
    gain_out,
    bias_out,
    cotangent,
):
    tokens = inputs.reshape(768, 768)
    short = (b_query, b_value, b_output, gain_attn, bias_attn, b_outer, gain_out, bias_out)
    parts = (w_query, w_key, w_value, w_output, w_inner, w_outer, *short, b_inner)
    wq, wk, wv, wo, win, wout, q, qh, k, v, vec, mixed, lse, segs = run_forward(parts, tokens, segments)
    out, dwo, hidden, gmix, mlp, delta, sums = run_dense(
        tokens, mixed, cotangent.reshape(768, 768), wo, win, wout, vec
    )
    grad_input, early_sum, late_sum, mlp_sum = run_backward(
        q, qh, k, v, gmix, tokens, wq, wk, wv, hidden, mlp, lse, delta, segs, dwo, sums
    )
    grad_input, dwq, dwk, dwv, dwo, dwin, dwout, inner, *short = split_results(
        early_sum, late_sum, mlp_sum, grad_input
    )
    return (
        out.reshape(1, 768, 768),
        grad_input.reshape(1, 768, 768),
        dwq,
        dwk,
        dwv,
        dwo,
        *short[:5],
        dwin,
        inner,
        dwout,
        *short[5:],
    )


def solution(mesh):
    return jax.shard_map(
        per_device,
        mesh=mesh,
        in_specs=(
            P("dp", "seq", None),
            P("dp", "seq"),
            P(("seq", "dp"), None),
            P(("seq", "dp"), None),
            P(("seq", "dp"), None),
            P(("seq", "dp"), None),
            P(("seq", "dp")),
            P(("seq", "dp")),
            P(("seq", "dp")),
            P(("seq", "dp")),
            P(("seq", "dp")),
            P(("seq", "dp"), None),
            P(("seq", "dp")),
            P(("seq", "dp"), None),
            P(("seq", "dp")),
            P(("seq", "dp")),
            P(("seq", "dp")),
            P("dp", "seq", None),
        ),
        out_specs=(
            P("dp", "seq", None),
            P("dp", "seq", None),
            P(("seq", "dp"), None),
            P(("seq", "dp"), None),
            P(("seq", "dp"), None),
            P(("seq", "dp"), None),
            P(("seq", "dp")),
            P(("seq", "dp")),
            P(("seq", "dp")),
            P(("seq", "dp")),
            P(("seq", "dp")),
            P(("seq", "dp"), None),
            P(("seq", "dp")),
            P(("seq", "dp"), None),
            P(("seq", "dp")),
            P(("seq", "dp")),
            P(("seq", "dp")),
        ),
        check_vma=False,
    )
```

```python
import math

import jax
import jax.numpy as jnp
import numpy as np
from jax import lax
from jax.experimental import pallas as pl
from jax.experimental.pallas import tpu as pltpu
from jax.sharding import PartitionSpec as P

HALF_WIN = 512
EPS = 1e-12
NEG_FILL = -1e30


MESH = pl.DeviceIdType.MESH
BF, F32 = jnp.bfloat16, jnp.float32
WIDTH = 768
PART, PARTS = 256, 3
WIDE, WIDES = 384, 2
BLOCK = 256
ATTN_ROWS, MLP_ROWS = 16, 48
ORDER = (("x", "y", "z"), ("y", "z", "x"), ("z", "x", "y"))
WIDE_ORDER = (("z", "x", "y"), ("z", "y", "x"))
SHIFTS = (1, 3, 2)
VMEM_BYTES = 62 * 2**20
NN = (((1,), (0,)), ((), ()))
NT = (((1,), (1,)), ((), ()))
TN = (((0,), (0,)), ((), ()))


def dot(one, two, dims=NN):
    return lax.dot_general(one, two, dims, preferred_element_type=F32)


def coords():
    seq, dp = lax.axis_index("seq"), lax.axis_index("dp")
    return {"x": (dp // 4) % 4, "y": dp // 16, "z": seq * 2 + (dp // 2) % 2, "c": dp % 2}


def device(place):
    return {
        "seq": place["z"] // 2,
        "dp": place["y"] * 16 + place["x"] * 4 + (place["z"] % 2) * 2 + place["c"],
    }


def shifted(place, axis, by):
    moved = dict(place)
    moved[axis] = (place[axis] + by) % (2 if axis == "c" else 4)
    return device(moved)


def greet(place):
    barrier = pltpu.get_barrier_semaphore()
    others = [shifted(place, axis, by) for axis in "xyz" for by in SHIFTS] + [shifted(place, "c", 1)]
    for other in others:
        pl.semaphore_signal(barrier, inc=1, device_id=other, device_id_type=MESH)
    pl.semaphore_wait(barrier, len(others))


def slab_place(group, member):
    return {
        "x": (group % 2) * 2 + member // 4,
        "y": (group // 2) % 4,
        "z": (group // 8) * 2 + (member // 2) % 2,
        "c": member % 2,
    }


def slab_index(order, part, place):
    first, second, third = (place[axis] for axis in order[part])
    return (part, place["c"], third, second, first)


class Copies:
    def __init__(self, sems, sizes, anyone):
        self.sems, self.sizes, self.anyone = sems, sizes, anyone
        self.kinds = set()

    def describe(self, kind, source, target, to):
        return pltpu.make_async_remote_copy(
            src_ref=source, dst_ref=target, send_sem=self.sems.at[0, kind], recv_sem=self.sems.at[1, kind],
            device_id=to, device_id_type=MESH,
        )

    def send(self, kind, source, target, to):
        self.describe(kind, source, target, to).start()
        self.kinds.add(kind)

    def arrived(self, kind):
        self.describe(kind, self.sizes[kind], self.sizes[kind], self.anyone).wait_recv()

    def sent(self, *kinds):
        for kind in kinds:
            self.describe(kind, self.sizes[kind], self.sizes[kind], self.anyone).wait_send()
            self.kinds.remove(kind)

    def finish(self):
        self.sent(*sorted(self.kinds))


class Gather:
    KINDS = 10

    def __init__(self, me, held, sems, order):
        self.order, self.parts = order, range(len(order))
        self.me, self.held, self.core = me, held, me["c"]
        self.other = shifted(me, "c", 1)
        all_parts = held.at[:, self.core]
        three, two = pl.ds(0, 3), pl.ds(0, 2)
        sizes = (
            all_parts.at[:, 0, 0, three], all_parts.at[:, 0, three], all_parts.at[:, two, two],
            all_parts.at[:, two, two], all_parts.at[:, two, two], all_parts.at[:, 0, 0],
            all_parts.at[:, 0, three], all_parts.at[:, two, two], all_parts.at[:, two, two],
            all_parts.at[:, two, two],
        )
        self.copies = Copies(sems, sizes, self.other)
        self.mine = [tuple(me[axis] for axis in order[part]) for part in self.parts]

    def send(self, kind, block, to):
        self.copies.send(kind, block, block, to)

    def first(self):
        for part in self.parts:
            m1, m2, m3 = self.mine[part]
            for by in SHIFTS:
                self.send(0, self.held.at[part, self.core, m3, m2, m1], shifted(self.me, self.order[part][0], by))

    def second(self):
        self.copies.arrived(0)
        for part in self.parts:
            m1, m2, m3 = self.mine[part]
            for by in SHIFTS:
                self.send(1, self.held.at[part, self.core, m3, m2], shifted(self.me, self.order[part][1], by))
        for part in self.parts:
            m1, m2, m3 = self.mine[part]
            self.send(5, self.held.at[part, self.core, m3, m2], self.other)

    def third(self):
        self.copies.arrived(1)
        for late in range(2):
            for part in self.parts:
                m3 = self.mine[part][2]
                for k, by in enumerate((1, 3)):
                    half = self.held.at[part, self.core, m3, pl.ds(2 * (k ^ late), 2)]
                    self.send(2 + late, half, shifted(self.me, self.order[part][2], by))
        for part in self.parts:
            m1, m2, m3 = self.mine[part]
            for by in SHIFTS:
                self.send(6, self.held.at[part, self.core, m3, (m2 - by + 4) % 4], self.other)

    def fourth(self):
        self.copies.arrived(2)
        halves = []
        for part in self.parts:
            m3 = self.mine[part][2]
            for k, by in enumerate((1, 3)):
                half = self.held.at[part, self.core, (m3 - by + 4) % 4, pl.ds(2 * k, 2)]
                self.send(4, half, shifted(self.me, self.order[part][2], by))
                halves.append(half)
        for half in halves:
            self.send(7, half, self.other)

    def fifth(self):
        self.copies.arrived(3)
        for part in self.parts:
            m3 = self.mine[part][2]
            for k, by in enumerate((1, 3)):
                self.send(8, self.held.at[part, self.core, (m3 - by + 4) % 4, pl.ds(2 - 2 * k, 2)], self.other)
        self.copies.arrived(4)
        for part in self.parts:
            for k in range(2):
                half = self.held.at[part, self.core, (self.mine[part][2] + 2) % 4, pl.ds(2 * k, 2)]
                self.send(9, half, self.other)

    def last(self):
        for kind in range(5, 10):
            self.copies.arrived(kind)
        self.copies.finish()


def tables():
    early = np.zeros((112, 128), np.float32)
    late = np.zeros((96, 128), np.float32)
    mlp = np.zeros((192, 192), np.float32)
    for i in range(8):
        early[96 + i, 16 * i + 12] = 1
        for t in range(6):
            for w in range(2):
                early[48 * w + 6 * i + t, 16 * i + 6 * w + t] = 1
                late[48 * w + 6 * i + t, 16 * i + 6 * w + t] = 1
            for w in range(4):
                mlp[48 * w + 6 * i + t, 24 * i + 6 * w + t] = 1
    lane, column = np.arange(128)[:, None], np.arange(WIDTH)[None]
    short = ((lane < 48) & (lane % 6 == column % 6)).astype(np.float32)
    short_owner = (lane == column // 6).astype(np.float32)
    inner = (lane - 48 == column % 24).astype(np.float32)
    inner_owner = (lane[:32] == column // 24).astype(np.float32)
    return early, late, mlp, short, short_owner, inner, inner_owner


def block_bias(query_pos, query_seg, key_pos, key_seg):
    allowed = (query_seg == key_seg) & (jnp.abs(query_pos - key_pos) <= HALF_WIN)
    return jnp.where(allowed, 0.0, NEG_FILL)


class Local:
    def __init__(self, sems):
        self.sems, self.started = sems, {}

    def start(self, number, source, target):
        self.started[number] = pltpu.make_async_copy(source, target, self.sems.at[number])
        self.started[number].start()

    def wait(self, *numbers):
        for number in numbers or list(self.started):
            self.started.pop(number).wait()


def eight(held, order, part, group):
    return [held[slab_index(order, part, slab_place(group, member))] for member in range(8)]


def forward_kernel(
    wq_part, wk_part, wv_part, wo_part, win_part, wout_part,
    bq_part, bv_part, bo_part, ga_part, ba_part, bout_part, go_part, bo2_part, binner_part, x_ref, seg_ref,
    early_ref, late_ref, pick_mlp_ref, short_ref, short_owner_ref, inner_ref, inner_owner_ref,
    wq_any, wk_any, wv_any, wo_any, win_any, wout_any, q_any, qh_any, k_any, v_any,
    e0_any, e1_any, e2_any, vec_ref, mixed_ref, inv_ref, top_ref, segs_ref,
    wq, wk, wv, wo, win, wout, q, qh, k, v,
    held_e, held_l, held_m, rows, xh, bias, top_cols, e0, e1, e2,
    sems_e, sems_l, sems_m, sems_h, out_sem, e_sem,
):
    me = coords()
    side = lax.axis_index("seq")
    short = (bq_part, bv_part, bo_part, ga_part, ba_part, bout_part, go_part, bo2_part)
    row = jnp.concatenate(
        [ref[...].astype(F32).reshape(1, 6) for ref in short]
        + [binner_part[...].astype(F32).reshape(1, 24), jnp.zeros((1, WIDTH - 72), F32)], axis=1,
    )
    early_rows = jnp.concatenate(
        [wk_part[...].astype(F32), wv_part[...].astype(F32), row, jnp.zeros((3, WIDTH), F32)], axis=0
    ).astype(BF)
    late_rows = jnp.concatenate(
        [wq_part[...].astype(F32), wo_part[...].astype(F32), jnp.zeros((4, WIDTH), F32)], axis=0
    ).astype(BF)
    for part in range(WIDES):
        held_e[slab_index(WIDE_ORDER, part, me)] = early_rows[:, WIDE * part : WIDE * (part + 1)]
        held_l[slab_index(WIDE_ORDER, part, me)] = late_rows[:, WIDE * part : WIDE * (part + 1)]
    greet(me)
    early = Gather(me, held_e, sems_e, WIDE_ORDER)
    late = Gather(me, held_l, sems_l, WIDE_ORDER)
    mlp = Gather(me, held_m, sems_m, ORDER)
    outs = Local(out_sem)
    partner = shifted(me, "z", 2)
    halo = Copies(sems_h, (xh, segs_ref.at[pl.ds(3, 2)]), partner)
    early.first()
    late.first()
    for n in range(3):
        segs_ref[n] = jnp.broadcast_to(seg_ref[:, BLOCK * n : BLOCK * (n + 1)].astype(F32), (8, BLOCK))
    mlp_rows = jnp.concatenate(
        [win_part[:, WIDTH * n : WIDTH * (n + 1)].astype(F32) for n in range(4)]
        + [wout_part[...].astype(F32)], axis=0,
    ).astype(BF)
    for part in range(PARTS):
        held_m[slab_index(ORDER, part, me)] = mlp_rows[:, PART * part : PART * (part + 1)]
    early.second()
    late.second()
    for n in range(2):
        block = jnp.where(side == 1, n, 2 - n)
        rows_out = x_ref.at[pl.ds(pl.multiple_of(block * BLOCK, BLOCK), BLOCK)]
        halo.send(0, rows_out, xh.at[pl.ds(n * BLOCK, BLOCK)], partner)
        halo.send(1, segs_ref.at[block], segs_ref.at[3 + n], partner)
    early.third()
    late.third()
    across = lax.broadcasted_iota(jnp.int32, (1, BLOCK), 1)
    down = lax.broadcasted_iota(jnp.int32, (BLOCK, 1), 0)
    starts = [BLOCK * n for n in range(3)] + [
        jnp.where(side == 0, 768 + BLOCK * n, -BLOCK * (n + 1)) for n in range(2)
    ]
    blocks = [jnp.where(side == 0, b, 2 - b) for b in range(3)]

    def fill_bias(b, key_blocks):
        seg_here = segs_ref[blocks[b], 0:1, :]
        seg_down = jnp.broadcast_to(seg_here, (128, BLOCK)).T[:, 0:1]
        for n in key_blocks:
            bias[b, :, pl.ds(n * BLOCK, BLOCK)] = block_bias(
                blocks[b] * BLOCK + down, seg_down, starts[n] + across, segs_ref[n, 0:1, :]
            )

    for b in range(3):
        fill_bias(b, range(3))
    mlp.first()
    early.fourth()
    late.fourth()
    early.fifth()
    late.fifth()
    early.last()
    mlp.second()

    def unpack_early(group, _):
        at = pl.ds(pl.multiple_of(group * 48, 16), 48)
        for part in range(WIDES):
            picked = dot(early_ref[...], jnp.concatenate(eight(held_e, WIDE_ORDER, part, group), axis=0))
            for n, ref in enumerate((wk, wv)):
                ref[at, pl.ds(part * WIDE, WIDE)] = picked[48 * n : 48 * n + 48].astype(BF)
            if part == 0:
                rows[pl.ds(pl.multiple_of(group * 8, 8), 8), :] = picked[96:104, :128]
        return 0

    lax.fori_loop(0, 16, unpack_early, 0, unroll=4)
    outs.start(0, wk, wk_any)
    outs.start(1, wv, wv_any)
    lane = lax.broadcasted_iota(jnp.int32, (1, 128), 1)
    for n in range(2):
        chosen = jnp.where((lane >= 6 * n) & (lane < 6 * n + 6), rows[...], 0.0).astype(BF)
        vec_ref[n : n + 1, :] = jnp.sum(
            dot(chosen, short_ref[...]) * short_owner_ref[...], axis=0, keepdims=True
        )
    def project_key(tokens, at):
        k[at, :] = dot(tokens[...], wk[...]).astype(BF)
        v[at, :] = (dot(tokens[...], wv[...]) + vec_ref[1:2, :]).astype(BF)

    def project_query(tokens, target):
        target[...] = (dot(tokens[...], wq[...]) + vec_ref[0:1, :]).astype(BF) * jnp.asarray(0.125, BF)

    project_key(x_ref, pl.ds(0, 768))
    late.last()
    for n in range(2, 8):
        chosen = jnp.where((lane >= 6 * n) & (lane < 6 * n + 6), rows[...], 0.0).astype(BF)
        vec_ref[n : n + 1, :] = jnp.sum(
            dot(chosen, short_ref[...]) * short_owner_ref[...], axis=0, keepdims=True
        )
    for n in range(4):
        chosen = rows[pl.ds(32 * n, 32), :].astype(BF)
        vec_ref[8 + n : 9 + n, :] = jnp.sum(
            dot(chosen, inner_ref[...]) * inner_owner_ref[...], axis=0, keepdims=True
        )

    mlp.third()

    def unpack_late(group, _):
        at = pl.ds(pl.multiple_of(group * 48, 16), 48)
        for part in range(WIDES):
            picked = dot(late_ref[...], jnp.concatenate(eight(held_l, WIDE_ORDER, part, group), axis=0))
            for n, ref in enumerate((wq, wo)):
                ref[at, pl.ds(part * WIDE, WIDE)] = picked[48 * n : 48 * n + 48].astype(BF)
        return 0

    lax.fori_loop(0, 16, unpack_late, 0, unroll=4)
    outs.start(2, wq, wq_any)
    outs.start(3, wo, wo_any)
    project_query(x_ref, q)
    outs.start(4, q, q_any)

    low = lane < 64

    slots, kept = (e0, e1, e2), (e0_any, e1_any, e2_any)

    def keep_copy(b, pair):
        return pltpu.make_async_copy(slots[b].at[pair % 2], kept[b].at[pair], e_sem.at[b, pair % 2])

    def attend(pair, those, reused):
        columns = pl.ds(pl.multiple_of(pair * 128, 128), 128)
        items = [(b, e) for b in those for e in range(2)]
        if reused:
            for b in those:
                keep_copy(b, pair - 2).wait()

        def place(b):
            return pl.ds(pl.multiple_of(blocks[b] * BLOCK, BLOCK), BLOCK)

        def scores_of(b, e):
            count = 768 + BLOCK * b
            queries = jnp.where(low if e == 0 else ~low, q[place(b), columns], jnp.zeros((), BF))
            return dot(queries, k[pl.ds(0, count), columns], NT) + bias[b, :, pl.ds(0, count)]

        scores, outs_of = scores_of(*items[0]), []
        for n, (b, e) in enumerate(items):
            later = scores_of(*items[n + 1]) if n + 1 < len(items) else None
            top = jnp.max(scores, axis=1, keepdims=True)
            weights = jnp.exp(scores - top).astype(BF)
            slots[b][pair % 2, pl.ds(BLOCK * e, BLOCK), :] = weights
            values = v[pl.ds(0, 768 + BLOCK * b), columns]
            outs_of.append(dot(weights, jnp.where(low if e == 0 else ~low, values, jnp.ones((), BF))))
            top_cols[place(b), :] = jnp.where(lane == 2 * pair + e, top, top_cols[place(b), :])
            scores = later
            if e == 1:
                inverse = 1.0 / pltpu.roll(jnp.where(low, outs_of[1], outs_of[0]), 64, 1)
                inv_ref[place(b), columns] = inverse
                mixed_ref[place(b), columns] = (jnp.where(low, outs_of[0], outs_of[1]) * inverse).astype(BF)
                outs_of = []
        for b in those:
            keep_copy(b, pair).start()

    def near_first(pair, _):
        attend(pair, (0,), False)
        return 0

    def near_next(pair, _):
        attend(pair, (0,), True)
        return 0

    def far_first(pair, _):
        attend(pair, (1, 2), False)
        return 0

    def far_next(pair, _):
        attend(pair, (1, 2), True)
        return 0

    lax.fori_loop(0, 2, near_first, 0, unroll=2)
    lax.fori_loop(2, 6, near_next, 0, unroll=2)
    halo.arrived(0)
    halo.arrived(1)
    for b in range(1, 3):
        fill_bias(b, range(3, 3 + b))
    project_key(xh, pl.ds(768, 512))
    project_query(xh, qh)
    outs.start(5, qh, qh_any)
    outs.start(6, k, k_any)
    outs.start(7, v, v_any)
    mlp.fourth()
    lax.fori_loop(0, 2, far_first, 0)
    lax.fori_loop(2, 3, far_next, 0)
    mlp.fifth()
    lax.fori_loop(3, 5, far_next, 0)
    mlp.last()

    def unpack_mlp(group, _):
        at = pl.ds(pl.multiple_of(group * 48, 16), 48)
        at_outer = pl.ds(pl.multiple_of(group * 192, 64), 192)
        for part in range(PARTS):
            slabs = eight(held_m, ORDER, part, group)
            picked = dot(pick_mlp_ref[...], jnp.concatenate([slab[:24] for slab in slabs], axis=0)).astype(BF)
            for n in range(4):
                win[at, pl.ds(n * WIDTH + part * PART, PART)] = picked[48 * n : 48 * n + 48]
            wout[at_outer, pl.ds(part * PART, PART)] = jnp.concatenate([slab[24:] for slab in slabs], axis=0)
        return 0

    lax.fori_loop(0, 16, unpack_mlp, 0, unroll=4)
    outs.start(8, win, win_any)
    outs.start(9, wout, wout_any)
    lax.fori_loop(5, 6, far_next, 0)
    for b in range(3):
        top_ref[b] = top_cols[pl.ds(b * BLOCK, BLOCK), :].T[:16]
        for pair in (4, 5):
            keep_copy(b, pair).wait()
    halo.finish()
    outs.wait()


def run_forward(parts, tokens, seg_row):
    early, late, mlp, short, short_owner, inner, inner_owner = tables()
    fixed = (
        jnp.asarray(early, BF), jnp.asarray(late, BF), jnp.asarray(mlp, BF), jnp.asarray(short, BF),
        jnp.asarray(short_owner), jnp.asarray(inner, BF), jnp.asarray(inner_owner),
    )
    vmem, anywhere = pl.BlockSpec(memory_space=pltpu.VMEM), pl.BlockSpec(memory_space=pl.ANY)
    large = (
        [(768, 768)] * 4 + [(768, 3072), (3072, 768), (768, 768), (512, 768), (1280, 768), (1280, 768)]
    )
    kept = [(6, 2 * BLOCK, 768 + BLOCK * b) for b in range(3)]
    small = [((16, 768), F32), ((768, 768), BF), ((768, 768), F32), ((3, 16, BLOCK), F32), ((5, 8, BLOCK), F32)]
    sems = pltpu.SemaphoreType.DMA
    return pl.pallas_call(
        forward_kernel,
        out_shape=tuple(jax.ShapeDtypeStruct(shape, BF) for shape in large + kept)
        + tuple(jax.ShapeDtypeStruct(*shape) for shape in small),
        in_specs=[vmem] * 24,
        out_specs=(anywhere,) * len(large + kept) + (vmem,) * len(small),
        scratch_shapes=[
            *(pltpu.VMEM(shape, BF) for shape in large),
            pltpu.VMEM((WIDES, 2, 4, 4, 4, ATTN_ROWS, WIDE), BF),
            pltpu.VMEM((WIDES, 2, 4, 4, 4, ATTN_ROWS, WIDE), BF),
            pltpu.VMEM((PARTS, 2, 4, 4, 4, MLP_ROWS, PART), BF),
            pltpu.VMEM((128, 128), F32),
            pltpu.VMEM((512, 768), BF),
            pltpu.VMEM((3, BLOCK, 1280), F32),
            pltpu.VMEM((768, 128), F32),
            *(pltpu.VMEM((2, *shape[1:]), BF) for shape in kept),
            *(sems((2, Gather.KINDS)) for _ in range(3)), sems((2, 2)), sems((10,)), sems((3, 2)),
        ],
        compiler_params=pltpu.CompilerParams(
            collective_id=0, has_side_effects=True, vmem_limit_bytes=VMEM_BYTES
        ),
        name="gather_and_attend",
    )(*parts, tokens, seg_row, *fixed)


class Scatter:
    KINDS = 8

    def __init__(self, me, parts, own, near, halves, blocks, second, first, sems, order):
        self.order, self.every = order, range(len(order))
        self.me, self.core = me, me["c"]
        self.parts, self.own, self.near, self.halves = parts, own, near, halves
        self.blocks, self.second, self.first = blocks, second, first
        self.other = shifted(me, "c", 1)
        sizes = (near.at[:, 0],) * 4 + (halves, blocks, second, first)
        self.copies = Copies(sems, sizes, self.other)
        self.mine = [tuple(me[axis] for axis in order[part]) for part in self.every]

    def add(self, target, sources, count):
        def body(index, _):
            if len(sources) == 1:
                target[index] = target[index] + sources[0][index]
            else:
                total = target[index].astype(F32)
                for source in sources:
                    total = total + source[index].astype(F32)
                target[index] = total.astype(BF)
            return 0

        lax.fori_loop(0, count, body, 0)

    def to_sibling(self):
        for k, by in enumerate((2, 1, 3, 0)):
            for part in self.every:
                at = (self.mine[part][2] + by) % 4
                self.copies.send(k, self.parts.at[part, 1 - self.core, at], self.near.at[part, at], self.other)

    def near_sum(self, k, by):
        self.copies.arrived(k)
        for part in self.every:
            at = (self.mine[part][2] + by) % 4
            self.add(self.near.at[part, at], [self.own(part, at)], 4)

    def opposite(self):
        self.near_sum(0, 2)
        for part in self.every:
            m3 = self.mine[part][2]
            for k, by in enumerate((1, 3)):
                half = self.near.at[part, (m3 + 2) % 4, pl.ds(2 * k, 2)]
                self.copies.send(4, half, self.halves.at[part, k], shifted(self.me, self.order[part][2], by))

    def nearest(self):
        self.near_sum(1, 1)
        self.near_sum(2, 3)
        self.near_sum(3, 0)

    def neighbours(self):
        self.copies.arrived(4)
        for part in self.every:
            m3 = self.mine[part][2]
            for k, by in enumerate((1, 3)):
                block = self.near.at[part, (m3 + by) % 4]
                self.add(block.at[pl.ds(2 * k, 2)], [self.halves.at[part, k]], 2)
                self.copies.send(5, block, self.blocks.at[part, k], shifted(self.me, self.order[part][2], by))

    def middle(self):
        self.copies.arrived(5)
        for part in self.every:
            m1, m2, m3 = self.mine[part]
            block = self.near.at[part, m3]
            self.add(block, [self.blocks.at[part, 0], self.blocks.at[part, 1]], 4)
            for k, by in enumerate(SHIFTS):
                self.copies.send(
                    6, block.at[(m2 + by) % 4], self.second.at[part, k], shifted(self.me, self.order[part][1], by)
                )

    def final(self):
        self.copies.arrived(6)
        for part in self.every:
            m1, m2, m3 = self.mine[part]
            block = self.near.at[part, m3, pl.ds(m2, 1)]
            self.add(block, [self.second.at[part, pl.ds(k, 1)] for k in range(3)], 1)
            for k, by in enumerate(SHIFTS):
                self.copies.send(
                    7, block.at[0, (m1 + by) % 4], self.first.at[part, k], shifted(self.me, self.order[part][0], by)
                )

    def result(self, out_ref):
        self.copies.arrived(7)
        for part in self.every:
            m1, m2, m3 = self.mine[part]
            total = self.near[part, m3, m2, m1].astype(F32)
            for k in range(3):
                total = total + self.first[part, k].astype(F32)
            out_ref[part] = total
        self.copies.finish()


def row_sum(block):
    return jnp.sum(block, axis=0, keepdims=True)


def normed_of(hidden):
    centred = hidden - jnp.mean(hidden, axis=1, keepdims=True)
    inverse = lax.rsqrt(jnp.mean(centred * centred, axis=1, keepdims=True) + EPS)
    return centred * inverse, inverse


def dense_kernel(
    x_any, mixed_any, cot_any, wo_any, win_any, wout_any, inv_any, vec_ref, put_mlp_ref, heads_ref,
    out_any, dwo_any, hidden_any, gmix_any, parts_any, delta_ref, sums_ref,
    x, mixed, cot, wo, win, wout, inv, out, gmix, parts,
    active, slope, normed, inverse, first_bf, total, grad_bf, load_sem, store_sem, chunk_sem,
):
    loads, stores = Local(load_sem), Local(store_sem)
    for n, (source, target) in enumerate(((mixed_any, mixed), (wo_any, wo), (x_any, x))):
        loads.start(n, source, target)

    def chunk_loads(index):
        columns = pl.ds(pl.multiple_of(index * WIDTH, WIDTH), WIDTH)
        return (
            pltpu.make_async_copy(win_any.at[:, columns], win.at[:, columns], chunk_sem.at[0, index]),
            pltpu.make_async_copy(wout_any.at[columns], wout.at[columns], chunk_sem.at[1, index]),
        )

    sums_ref[...] = jnp.zeros_like(sums_ref)

    def add_sum(row, block):
        sums_ref[pl.ds(row, 1), :] += row_sum(block)

    def row_block(index):
        return pl.ds(pl.multiple_of(index * BLOCK, BLOCK), BLOCK)

    loads.wait(0, 1, 2)
    for n in range(4):
        for one in chunk_loads(n):
            one.start()
    loads.start(3, cot_any, cot)
    loads.start(4, inv_any, inv)

    def branch_of(index):
        return dot(mixed[row_block(index), :], wo[...]) + vec_ref[2:3, :]

    branch = branch_of(0)
    for n in range(3):
        later = branch_of(n + 1) if n < 2 else None
        at = row_block(n)
        normed[at, :], spread = normed_of(x[at, :].astype(F32) + branch)
        inverse[at, :] = jnp.broadcast_to(spread, (BLOCK, 128))
        first_bf[at, :] = (normed[at, :] * vec_ref[3:4, :] + vec_ref[4:5, :]).astype(BF)
        branch = later
    rate, bend = math.sqrt(2 / math.pi), 0.044715

    def inner_of(n):
        for one in chunk_loads(n):
            one.wait()
        return dot(first_bf[...], win[:, WIDTH * n : WIDTH * (n + 1)]) + vec_ref[8 + n : 9 + n, :]

    u = inner_of(0)
    for n in range(4):
        later = inner_of(n + 1) if n < 3 else None
        columns = slice(WIDTH * n, WIDTH * (n + 1))
        square = u * u
        bent = jnp.tanh(rate * u * (1 + bend * square))
        half = 0.5 * (1 + bent)
        active[:, columns] = (u * half).astype(BF)
        slope[:, columns] = (
            half + u * half * (1 - bent) * (rate + (3 * rate * bend) * square)
        ).astype(BF)
        outer = dot(active[:, columns], wout[columns, :])
        total[...] = outer if n == 0 else total[...] + outer
        u = later

    def norm_two(index, _):
        at = row_block(index)
        first = normed[at, :] * vec_ref[3:4, :] + vec_ref[4:5, :]
        normed_two, spread = normed_of(first + (total[at, :] + vec_ref[5:6, :]))
        out[at, :] = (normed_two * vec_ref[6:7, :] + vec_ref[7:8, :]).astype(BF)
        grad = cot[at, :].astype(F32)
        add_sum(6, grad * normed_two)
        add_sum(7, grad)
        scaled = grad * vec_ref[6:7, :]
        mean_grad = jnp.mean(scaled, axis=1, keepdims=True)
        mean_cross = jnp.mean(scaled * normed_two, axis=1, keepdims=True)
        back = spread * (scaled - mean_grad - normed_two * mean_cross)
        total[at, :] = back
        grad_bf[at, :] = back.astype(BF)
        add_sum(5, grad_bf[at, :].astype(F32))
        return 0

    loads.wait(3)
    lax.fori_loop(0, 3, norm_two, 0)
    stores.start(0, out, out_any)

    def outer_block(index, _):
        columns = pl.ds(pl.multiple_of(index * WIDTH, WIDTH), WIDTH)
        grad_inner = (dot(grad_bf[...], wout[columns, :], NT) * slope[:, columns].astype(F32)).astype(BF)
        add_sum(8 + index, grad_inner.astype(F32))
        total[...] += dot(grad_inner, win[:, columns], NT)
        active[:, columns] = dot(active[:, columns], grad_bf[...], TN).astype(BF)
        slope[:, columns] = dot(first_bf[...], grad_inner, TN).astype(BF)
        return 0

    lax.fori_loop(0, 4, outer_block, 0)

    def back_one(index, _):
        at = row_block(index)
        grad, normed_one = total[at, :], normed[at, :]
        add_sum(3, grad * normed_one)
        add_sum(4, grad)
        scaled = grad * vec_ref[3:4, :]
        mean_grad = jnp.mean(scaled, axis=1, keepdims=True)
        mean_cross = jnp.mean(scaled * normed_one, axis=1, keepdims=True)
        back = inverse[at, 0:1] * (scaled - mean_grad - normed_one * mean_cross)
        total[at, :] = back
        grad_bf[at, :] = back.astype(BF)
        add_sum(2, grad_bf[at, :].astype(F32))
        return 0

    lax.fori_loop(0, 3, back_one, 0)
    stores.start(1, total, hidden_any)
    loads.wait(4)
    gmix[...] = (dot(grad_bf[...], wo[...], NT) * inv[...]).astype(BF)
    stores.start(2, gmix, gmix_any)
    first_bf[...] = dot(mixed[...], grad_bf[...], TN).astype(BF)
    stores.start(3, first_bf, dwo_any)

    for part in range(WIDES):

        def pack(group, _):
            at = pl.ds(pl.multiple_of(group * 48, 16), 48)
            at_outer = pl.ds(pl.multiple_of((group % 4) * 192, 64), 192)
            pieces = [slope[at, pl.ds(k * WIDTH + part * WIDE, WIDE)] for k in range(4)]
            placed = dot(put_mlp_ref[...], jnp.concatenate(pieces, axis=0)).astype(BF)
            outer_columns = pl.ds(pl.multiple_of((group // 4) * WIDTH + part * WIDE, 128), WIDE)
            outer = active[at_outer, outer_columns]
            for member in range(8):
                these = slice(24 * member, 24 * member + 24)
                parts[slab_index(WIDE_ORDER, part, slab_place(group, member))] = jnp.concatenate(
                    [placed[these], outer[these]], axis=0
                )
            return 0

        lax.fori_loop(0, 16, pack, 0, unroll=4)
        stores.start(4 + part, parts.at[part], parts_any.at[part])
    for k in range(3):
        at = pl.ds(BLOCK * k, BLOCK)
        product = mixed[at, :].astype(F32) * gmix[at, :].astype(F32)
        high = product.astype(BF)
        rest = (product - high.astype(F32)).astype(BF)
        delta_ref[k] = dot(heads_ref[...], high, NT) + dot(heads_ref[...], rest, NT)
    stores.wait()


def run_dense(tokens, mixed, cot, wo, win, wout, inv, vec):
    mlp = tables()[2]
    heads = (np.arange(16)[:, None] == np.arange(WIDTH)[None] // 64).astype(np.float32)
    vmem, anywhere = pl.BlockSpec(memory_space=pltpu.VMEM), pl.BlockSpec(memory_space=pl.ANY)
    parts_shape = (WIDES, 2, 4, 4, 4, MLP_ROWS, WIDE)
    shapes = (
        ((768, 768), BF), ((768, 768), BF), ((768, 768), F32), ((768, 768), BF), (parts_shape, BF),
        ((3, 16, BLOCK), F32), ((16, 768), F32),
    )
    sems = pltpu.SemaphoreType.DMA
    return pl.pallas_call(
        dense_kernel,
        out_shape=tuple(jax.ShapeDtypeStruct(*shape) for shape in shapes),
        in_specs=[anywhere] * 7 + [vmem] * 3,
        out_specs=(anywhere,) * 5 + (vmem,) * 2,
        scratch_shapes=[
            *(pltpu.VMEM((768, 768), BF) for _ in range(4)),
            pltpu.VMEM((768, 3072), BF), pltpu.VMEM((3072, 768), BF), pltpu.VMEM((768, 768), F32),
            pltpu.VMEM((768, 768), BF), pltpu.VMEM((768, 768), BF), pltpu.VMEM(parts_shape, BF),
            pltpu.VMEM((768, 3072), BF), pltpu.VMEM((768, 3072), BF), pltpu.VMEM((768, 768), F32),
            pltpu.VMEM((768, 128), F32), pltpu.VMEM((768, 768), BF), pltpu.VMEM((768, 768), F32),
            pltpu.VMEM((768, 768), BF), sems((5,)), sems((7,)), sems((2, 4)),
        ],
        compiler_params=pltpu.CompilerParams(vmem_limit_bytes=VMEM_BYTES),
        name="feed_forward",
    )(tokens, mixed, cot, wo, win, wout, inv, vec, jnp.asarray(mlp.T, BF), jnp.asarray(heads, BF))


def backward_kernel(
    q_any, qh_any, k_any, v_any, g_any, x_any, wq_any, wk_any, wv_any, hidden_any, mlp_any,
    e0_any, e1_any, e2_any, top_ref, delta_ref, segs_ref, dwo_ref, sums_ref, put_early_ref, put_late_ref, short_ref,
    short_owner_ref, inner_ref, inner_owner_ref,
    grad_any, early_out, late_out, mlp_out,
    q, qh, k, v, g, gh, stats, stat_cols, own_m, e0, e1, e2, bias, dq, dk, dv, grad_k, grad_v,
    dw, dwv, rows, hidden,
    parts, near_e, halves_e, blocks_e, second_e, first_e,
    near_l, halves_l, blocks_l, second_l, first_l,
    near_m, halves_m, blocks_m, second_m, first_m,
    load_sem, e_sem, sems_e, sems_l, sems_m, sems_h,
):
    me = coords()
    core = me["c"]
    side = lax.axis_index("seq")
    partner = shifted(me, "z", 2)
    loads = Local(load_sem)
    kept, slots = (e0_any, e1_any, e2_any), (e0, e1, e2)

    def keep_copy(b, pair):
        return pltpu.make_async_copy(kept[b].at[pair], slots[b].at[pair % 2], e_sem.at[b, pair % 2])

    loads.start(0, g_any, g)
    loads.start(5, mlp_any.at[:, core], own_m)
    for b in range(3):
        stats[b, 0:16, :] = top_ref[b]
        stats[b, 16:32, :] = delta_ref[b]

    def turn(block):
        both = jnp.concatenate([stats[block], jnp.zeros((96, BLOCK), F32)], axis=0)
        stat_cols[block] = both.T

    for b in range(3):
        turn(b)
    greet(me)
    mlp = Scatter(
        me, mlp_any, lambda part, at: own_m.at[part, at], near_m, halves_m, blocks_m, second_m, first_m,
        sems_m, WIDE_ORDER,
    )
    early = Scatter(
        me, parts, lambda part, at: parts.at[part, core, at], near_e, halves_e, blocks_e, second_e,
        first_e, sems_e, ORDER,
    )
    late = Scatter(
        me, parts, lambda part, at: parts.at[part, core, at], near_l, halves_l, blocks_l, second_l,
        first_l, sems_l, ORDER,
    )
    halo = Copies(sems_h, (gh, stats.at[pl.ds(3, 2)]), partner)
    loads.wait(0)
    for n in range(2):
        block = jnp.where(side == 1, n, 2 - n)
        rows_out = g.at[pl.ds(pl.multiple_of(block * BLOCK, BLOCK), BLOCK)]
        halo.send(0, rows_out, gh.at[pl.ds(n * BLOCK, BLOCK)], partner)
        halo.send(1, stats.at[block], stats.at[3 + n], partner)
    mlp.to_sibling()

    for number, (source, target) in enumerate(((v_any, v), (q_any, q), (k_any, k)), 1):
        loads.start(number, source, target)
    for b in range(3):
        keep_copy(b, 0).start()
    loads.start(4, qh_any, qh)
    loads.start(6, hidden_any, hidden)
    across = lax.broadcasted_iota(jnp.int32, (1, BLOCK), 1)
    down = lax.broadcasted_iota(jnp.int32, (BLOCK, 1), 0)
    blocks = [jnp.where(side == 0, b, 2 - b) for b in range(3)]
    reach = [
        (jnp.where(side == 0, BLOCK * (1 + n), 0), BLOCK * (2 - n)) for n in range(2)
    ]

    def fill_bias():
        for n in range(2):
            seg_down = jnp.broadcast_to(segs_ref[3 + n, 0:1, :], (128, BLOCK)).T[:, 0:1]
            start = jnp.where(side == 0, 768 + BLOCK * n, -BLOCK * (n + 1))
            for m in range(2 - n):
                block = jnp.where(side == 0, 1 + n + m, m)
                bias[n, :, pl.ds(m * BLOCK, BLOCK)] = block_bias(
                    start + down, seg_down, block * BLOCK + across, segs_ref[block, 0:1, :]
                )

    dk[...] = jnp.zeros_like(dk)
    dv[...] = jnp.zeros_like(dv)
    lane = lax.broadcasted_iota(jnp.int32, (1, 128), 1)
    low = lane < 64
    high_rows = lax.broadcasted_iota(jnp.int32, (128, 1), 0) >= 64
    nothing = jnp.zeros((), BF)

    def one_head(block, e):
        return jnp.where(low if e == 0 else ~low, block, nothing)

    def two_heads(turned):
        return jnp.concatenate(
            [jnp.where(high_rows, nothing, turned), jnp.where(high_rows, turned, nothing)], axis=1
        )

    def stat(block, row):
        return jnp.sum(jnp.where(lane == row, stat_cols[block], 0.0), axis=1, keepdims=True)

    def own_pair(pair, ahead):
        columns = pl.ds(pl.multiple_of(pair * 128, 128), 128)
        here = pl.ds(pl.multiple_of(pair * 128, 128), 128)
        for b in range(3):
            keep_copy(b, pair).wait()
        if ahead:
            for b in range(3):
                keep_copy(b, pair + 1).start()

        def place(b):
            return pl.ds(pl.multiple_of(blocks[b] * BLOCK, BLOCK), BLOCK)

        def products(b):
            values = v[pl.ds(0, 768 + BLOCK * b), columns]
            return [dot(one_head(g[place(b), columns], e), values, NT) for e in range(2)]

        grad_weights = products(0)
        for b in range(3):
            later = products(b + 1) if b < 2 else None
            weights = slots[b].at[pair % 2]
            grad_scores = [
                (
                    weights[pl.ds(BLOCK * e, BLOCK), :].astype(F32)
                    * (grad_weights[e] - stat(blocks[b], 16 + 2 * pair + e))
                ).astype(BF)
                for e in range(2)
            ]
            own = jnp.concatenate([block[:, :768] for block in grad_scores], axis=0)
            dk[here, :] += dot(two_heads(q[place(b), columns].T), own)
            dv[here, :] += dot(two_heads(g[place(b), columns].T), weights[:, pl.ds(0, 768)])
            keys = k[pl.ds(0, 768 + BLOCK * b), columns]
            grad_query = dot(grad_scores[0], one_head(keys, 0)) + dot(grad_scores[1], one_head(keys, 1))
            dq[place(b), columns] = (grad_query * 0.125).astype(BF)
            grad_weights = later

    def own_next(pair, _):
        own_pair(pair, True)
        return 0

    def own_last(pair, _):
        own_pair(pair, False)
        return 0

    def halo_pair(pair, _):
        columns = pl.ds(pl.multiple_of(pair * 128, 128), 128)
        here = pl.ds(pl.multiple_of(pair * 128, 128), 128)
        items = [(n, e) for n in range(2) for e in range(2)]

        def keys_at(n):
            return pl.ds(pl.multiple_of(reach[n][0], BLOCK), reach[n][1])

        def products(n, e):
            those = pl.ds(n * BLOCK, BLOCK)
            scores = dot(one_head(qh[those, columns], e), k[keys_at(n), columns], NT)
            grad_weights = dot(one_head(gh[those, columns], e), v[keys_at(n), columns], NT)
            return scores + bias[n, :, pl.ds(0, reach[n][1])], grad_weights

        ready = [products(*item) for item in items]
        for n in range(2):
            weights, grad_scores = [], []
            for e in range(2):
                scores, grad_weights = ready[2 * n + e]
                raised = jnp.exp(scores - stat(3 + n, 2 * pair + e))
                weights.append(raised.astype(BF))
                grad_scores.append((raised * (grad_weights - stat(3 + n, 16 + 2 * pair + e))).astype(BF))
            those = pl.ds(n * BLOCK, BLOCK)
            dk[here, keys_at(n)] += dot(two_heads(qh[those, columns].T), jnp.concatenate(grad_scores, axis=0))
            dv[here, keys_at(n)] += dot(two_heads(gh[those, columns].T), jnp.concatenate(weights, axis=0))
        grad_k[:, columns] = dk[here, :].T.astype(BF)
        grad_v[:, columns] = dv[here, :].T.astype(BF)
        return 0

    fill_bias()
    loads.wait(5)
    mlp.opposite()
    loads.wait(1, 2, 3)
    lax.fori_loop(0, 3, own_next, 0)
    mlp.nearest()
    lax.fori_loop(3, 4, own_next, 0)
    mlp.neighbours()
    lax.fori_loop(4, 5, own_next, 0)
    lax.fori_loop(5, 6, own_last, 0)
    halo.finish()
    loads.start(7, x_any, g)
    loads.start(8, wq_any, q)
    loads.wait(7)
    dw[...] = dot(g[...], dq[...], TN).astype(BF)

    def pack_late(group, _):
        at = pl.ds(pl.multiple_of(group * 48, 16), 48)
        for part in range(PARTS):
            columns = pl.ds(part * PART, PART)
            pieces = jnp.concatenate([dw[at, columns], dwo_ref[at, columns]], axis=0)
            placed = dot(put_late_ref[...], pieces).astype(BF)
            for member in range(8):
                parts[slab_index(ORDER, part, slab_place(group, member))] = placed[16 * member : 16 * member + 16]
        return 0

    lax.fori_loop(0, 16, pack_late, 0, unroll=4)
    late.to_sibling()
    halo.arrived(0)
    halo.arrived(1)
    for n in range(2):
        turn(3 + n)
    loads.wait(4)
    lax.fori_loop(0, 2, halo_pair, 0)
    late.opposite()
    late.nearest()
    lax.fori_loop(2, 6, halo_pair, 0)
    mlp.middle()
    loads.start(9, wk_any, k.at[pl.ds(0, 768)])
    loads.start(10, wv_any, v.at[pl.ds(0, 768)])
    dw[...] = dot(g[...], grad_k[...], TN).astype(BF)
    dwv[...] = dot(g[...], grad_v[...], TN).astype(BF)
    late.neighbours()

    rows[...] = jnp.zeros_like(rows)
    for n in range(8):
        if n == 0:
            vec = row_sum(dq[...].astype(F32))
        elif n == 1:
            vec = row_sum(grad_v[...].astype(F32))
        else:
            vec = sums_ref[n : n + 1, :]
        spread = dot((short_owner_ref[...] * vec).astype(BF), short_ref[...], NT)
        rows[...] = jnp.where((lane >= 6 * n) & (lane < 6 * n + 6), spread, rows[...])
    for n in range(4):
        spread = dot((inner_owner_ref[...] * sums_ref[8 + n : 9 + n, :]).astype(BF), inner_ref[...], NT)
        at = pl.ds(32 * n, 32)
        rows[at, :] = jnp.where((lane >= 48) & (lane < 72), spread, rows[at, :])

    def pack_early(group, _):
        at = pl.ds(pl.multiple_of(group * 48, 16), 48)
        vec = rows[pl.ds(pl.multiple_of(group * 8, 8), 8), :]
        vec = jnp.concatenate([vec, jnp.zeros_like(vec)], axis=1)
        vec = jnp.concatenate([vec, jnp.zeros_like(vec)], axis=0).astype(BF)
        for part in range(PARTS):
            columns = pl.ds(part * PART, PART)
            last = vec if part == 0 else jnp.zeros_like(vec)
            pieces = jnp.concatenate([dw[at, columns], dwv[at, columns], last], axis=0)
            placed = dot(put_early_ref[...], pieces).astype(BF)
            for member in range(8):
                parts[slab_index(ORDER, part, slab_place(group, member))] = placed[16 * member : 16 * member + 16]
        return 0

    late.copies.sent(0, 1, 2, 3)
    lax.fori_loop(0, 16, pack_early, 0, unroll=4)
    early.to_sibling()
    loads.wait(6, 8)
    hidden[...] += dot(dq[...], q[...], NT)
    early.opposite()
    early.nearest()
    loads.wait(9)
    hidden[...] += dot(grad_k[...], k[pl.ds(0, 768), :], NT)
    mlp.final()
    early.neighbours()
    loads.wait(10)
    hidden[...] += dot(grad_v[...], v[pl.ds(0, 768), :], NT)
    loads.start(11, hidden, grad_any)
    late.middle()
    early.middle()
    late.final()
    mlp.result(mlp_out)
    early.final()
    late.result(late_out)
    early.result(early_out)
    loads.wait()


def run_backward(q, qh, k, v, g, x, wq, wk, wv, hidden, mlp, kept, top, delta, segs, dwo, sums):
    early, late, _, short, short_owner, inner, inner_owner = tables()
    fixed = (
        jnp.asarray(early.T, BF), jnp.asarray(late.T, BF), jnp.asarray(short, BF),
        jnp.asarray(short_owner), jnp.asarray(inner, BF), jnp.asarray(inner_owner),
    )
    vmem, anywhere = pl.BlockSpec(memory_space=pltpu.VMEM), pl.BlockSpec(memory_space=pl.ANY)
    sems = pltpu.SemaphoreType.DMA

    def steps(parts, rows, width):
        return [
            pltpu.VMEM((parts, *lead, rows, width), BF)
            for lead in ((4, 4, 4), (2, 2, 4), (2, 4, 4), (3, 4), (3,))
        ]

    return pl.pallas_call(
        backward_kernel,
        out_shape=(
            jax.ShapeDtypeStruct((768, 768), F32),
            jax.ShapeDtypeStruct((PARTS, ATTN_ROWS, PART), F32),
            jax.ShapeDtypeStruct((PARTS, ATTN_ROWS, PART), F32),
            jax.ShapeDtypeStruct((WIDES, MLP_ROWS, WIDE), F32),
        ),
        in_specs=[anywhere] * 14 + [vmem] * 11,
        out_specs=(anywhere, vmem, vmem, vmem),
        scratch_shapes=[
            pltpu.VMEM((768, 768), BF), pltpu.VMEM((512, 768), BF),
            pltpu.VMEM((1280, 768), BF), pltpu.VMEM((1280, 768), BF),
            pltpu.VMEM((768, 768), BF), pltpu.VMEM((512, 768), BF),
            pltpu.VMEM((5, 32, BLOCK), F32), pltpu.VMEM((5, BLOCK, 128), F32),
            pltpu.VMEM((WIDES, 4, 4, 4, MLP_ROWS, WIDE), BF),
            *(pltpu.VMEM((2, *one.shape[1:]), BF) for one in kept), pltpu.VMEM((2, BLOCK, 512), F32),
            pltpu.VMEM((768, 768), BF), pltpu.VMEM((768, 768), F32), pltpu.VMEM((768, 768), F32),
            *(pltpu.VMEM((768, 768), BF) for _ in range(4)),
            pltpu.VMEM((128, 128), F32), pltpu.VMEM((768, 768), F32),
            pltpu.VMEM((PARTS, 2, 4, 4, 4, ATTN_ROWS, PART), BF),
            *steps(PARTS, ATTN_ROWS, PART), *steps(PARTS, ATTN_ROWS, PART), *steps(WIDES, MLP_ROWS, WIDE),
            sems((12,)), sems((3, 2)), *(sems((2, Scatter.KINDS)) for _ in range(3)), sems((2, 2)),
        ],
        compiler_params=pltpu.CompilerParams(
            collective_id=1, has_side_effects=True, vmem_limit_bytes=VMEM_BYTES
        ),
        name="attend_back_and_scatter",
    )(q, qh, k, v, g, x, wq, wk, wv, hidden, mlp, *kept, top, delta, segs, dwo, sums, *fixed)


def split_kernel(early_ref, late_ref, mlp_ref, grad_any, grad_out, wq, wk, wv, wo, win, wout, inner, *rest):
    short, staged, sems = rest[:8], rest[8], rest[9]
    moves = []
    for k in range(3):
        at = pl.ds(BLOCK * k, BLOCK)
        moves.append([
            pltpu.make_async_copy(grad_any.at[at], staged.at[at], sems.at[0, k]),
            pltpu.make_async_copy(staged.at[at], grad_out.at[at], sems.at[1, k]),
        ])
        moves[k][0].start()
    for fetch, put in moves:
        fetch.wait()
        put.start()
    for part in range(PARTS):
        columns = pl.ds(PART * part, PART)
        for ref, source, row in ((wk, early_ref, 0), (wv, early_ref, 6), (wq, late_ref, 0), (wo, late_ref, 6)):
            ref[:, columns] = source[part, row : row + 6, :]
    for part in range(WIDES):
        for k in range(4):
            win[:, pl.ds(WIDTH * k + WIDE * part, WIDE)] = mlp_ref[part, 6 * k : 6 * k + 6, :]
        wout[:, pl.ds(WIDE * part, WIDE)] = mlp_ref[part, 24:48, :]
    inner[...] = early_ref[0, 12, 48:72]
    for k in range(8):
        short[k][...] = early_ref[0, 12, 6 * k : 6 * k + 6]
    for fetch, put in moves:
        put.wait()


def split_results(early, late, mlp, grad):
    vmem, anywhere = pl.BlockSpec(memory_space=pltpu.VMEM), pl.BlockSpec(memory_space=pl.ANY)
    shapes = ((768, 768),) + ((6, 768),) * 4 + ((6, 3072), (24, 768), (24,)) + ((6,),) * 8
    return pl.pallas_call(
        split_kernel,
        out_shape=tuple(jax.ShapeDtypeStruct(shape, F32) for shape in shapes),
        in_specs=[vmem] * 3 + [anywhere],
        out_specs=(anywhere,) + (vmem,) * (len(shapes) - 1),
        scratch_shapes=[pltpu.VMEM((768, 768), F32), pltpu.SemaphoreType.DMA((2, 3))],
        compiler_params=pltpu.CompilerParams(vmem_limit_bytes=VMEM_BYTES),
        name="split_gradients",
    )(early, late, mlp, grad)


def per_device(
    inputs,
    segments,
    w_query,
    w_key,
    w_value,
    w_output,
    b_query,
    b_value,
    b_output,
    gain_attn,
    bias_attn,
    w_inner,
    b_inner,
    w_outer,
    b_outer,
    gain_out,
    bias_out,
    cotangent,
):
    tokens = inputs.reshape(768, 768)
    short = (b_query, b_value, b_output, gain_attn, bias_attn, b_outer, gain_out, bias_out)
    parts = (w_query, w_key, w_value, w_output, w_inner, w_outer, *short, b_inner)
    wq, wk, wv, wo, win, wout, q, qh, k, v, *kept, vec, mixed, inv, top, segs = run_forward(parts, tokens, segments)
    out, dwo, hidden, gmix, mlp, delta, sums = run_dense(
        tokens, mixed, cotangent.reshape(768, 768), wo, win, wout, inv, vec
    )
    grad_input, early_sum, late_sum, mlp_sum = run_backward(
        q, qh, k, v, gmix, tokens, wq, wk, wv, hidden, mlp, kept, top, delta, segs, dwo, sums
    )
    grad_input, dwq, dwk, dwv, dwo, dwin, dwout, inner, *short = split_results(
        early_sum, late_sum, mlp_sum, grad_input
    )
    return (
        out.reshape(1, 768, 768),
        grad_input.reshape(1, 768, 768),
        dwq,
        dwk,
        dwv,
        dwo,
        *short[:5],
        dwin,
        inner,
        dwout,
        *short[5:],
    )


def solution(mesh):
    return jax.shard_map(
        per_device,
        mesh=mesh,
        in_specs=(
            P("dp", "seq", None),
            P("dp", "seq"),
            P(("seq", "dp"), None),
            P(("seq", "dp"), None),
            P(("seq", "dp"), None),
            P(("seq", "dp"), None),
            P(("seq", "dp")),
            P(("seq", "dp")),
            P(("seq", "dp")),
            P(("seq", "dp")),
            P(("seq", "dp")),
            P(("seq", "dp"), None),
            P(("seq", "dp")),
            P(("seq", "dp"), None),
            P(("seq", "dp")),
            P(("seq", "dp")),
            P(("seq", "dp")),
            P("dp", "seq", None),
        ),
        out_specs=(
            P("dp", "seq", None),
            P("dp", "seq", None),
            P(("seq", "dp"), None),
            P(("seq", "dp"), None),
            P(("seq", "dp"), None),
            P(("seq", "dp"), None),
            P(("seq", "dp")),
            P(("seq", "dp")),
            P(("seq", "dp")),
            P(("seq", "dp")),
            P(("seq", "dp")),
            P(("seq", "dp"), None),
            P(("seq", "dp")),
            P(("seq", "dp"), None),
            P(("seq", "dp")),
            P(("seq", "dp")),
            P(("seq", "dp")),
        ),
        check_vma=False,
    )
```

```python
import math

import jax
import jax.numpy as jnp
import numpy as np
from jax import lax
from jax.experimental import pallas as pl
from jax.experimental.pallas import tpu as pltpu
from jax.sharding import PartitionSpec as P

HALF_WIN = 512
EPS = 1e-12
NEG_FILL = -1e30


MESH = pl.DeviceIdType.MESH
BF, F32 = jnp.bfloat16, jnp.float32
WIDTH = 768
PART, PARTS = 256, 3
WIDE, WIDES = 384, 2
BLOCK = 256
ATTN_ROWS, MLP_ROWS = 16, 48
ORDER = (("x", "y", "z"), ("y", "z", "x"), ("z", "x", "y"))
WIDE_ORDER = (("z", "x", "y"), ("z", "y", "x"))
BACK_ORDER = (("x", "z", "y"), ("z", "y", "x"))
SHIFTS = (1, 3, 2)
VMEM_BYTES = 62 * 2**20
NN = (((1,), (0,)), ((), ()))
NT = (((1,), (1,)), ((), ()))
TN = (((0,), (0,)), ((), ()))


def dot(one, two, dims=NN):
    return lax.dot_general(one, two, dims, preferred_element_type=F32)


def coords():
    seq, dp = lax.axis_index("seq"), lax.axis_index("dp")
    return {"x": (dp // 4) % 4, "y": dp // 16, "z": seq * 2 + (dp // 2) % 2, "c": dp % 2}


def device(place):
    return {
        "seq": place["z"] // 2,
        "dp": place["y"] * 16 + place["x"] * 4 + (place["z"] % 2) * 2 + place["c"],
    }


def shifted(place, axis, by):
    moved = dict(place)
    moved[axis] = (place[axis] + by) % (2 if axis == "c" else 4)
    return device(moved)


def greet(place):
    barrier = pltpu.get_barrier_semaphore()
    others = [shifted(place, axis, by) for axis in "xyz" for by in SHIFTS] + [shifted(place, "c", 1)]
    for other in others:
        pl.semaphore_signal(barrier, inc=1, device_id=other, device_id_type=MESH)
    pl.semaphore_wait(barrier, len(others))


def slab_place(group, member):
    return {
        "x": (group % 2) * 2 + member // 4,
        "y": (group // 2) % 4,
        "z": (group // 8) * 2 + (member // 2) % 2,
        "c": member % 2,
    }


def slab_index(order, part, place):
    first, second, third = (place[axis] for axis in order[part])
    return (part, place["c"], third, second, first)


class Copies:
    def __init__(self, sems, sizes, anyone):
        self.sems, self.sizes, self.anyone = sems, sizes, anyone
        self.kinds = set()

    def describe(self, kind, source, target, to):
        return pltpu.make_async_remote_copy(
            src_ref=source, dst_ref=target, send_sem=self.sems.at[0, kind], recv_sem=self.sems.at[1, kind],
            device_id=to, device_id_type=MESH,
        )

    def send(self, kind, source, target, to):
        self.describe(kind, source, target, to).start()
        self.kinds.add(kind)

    def arrived(self, kind):
        self.describe(kind, self.sizes[kind], self.sizes[kind], self.anyone).wait_recv()

    def sent(self, *kinds):
        for kind in kinds:
            self.describe(kind, self.sizes[kind], self.sizes[kind], self.anyone).wait_send()
            self.kinds.remove(kind)

    def finish(self):
        self.sent(*sorted(self.kinds))


class Gather:
    KINDS = 10

    def __init__(self, me, held, sems, order):
        self.order, self.parts = order, range(len(order))
        self.me, self.held, self.core = me, held, me["c"]
        self.other = shifted(me, "c", 1)
        all_parts = held.at[:, self.core]
        three, two = pl.ds(0, 3), pl.ds(0, 2)
        sizes = (
            all_parts.at[:, 0, 0, three], all_parts.at[:, 0, three], all_parts.at[:, two, two],
            all_parts.at[:, two, two], all_parts.at[:, two, two], all_parts.at[:, 0, 0],
            all_parts.at[:, 0, three], all_parts.at[:, two, two], all_parts.at[:, two, two],
            all_parts.at[:, two, two],
        )
        self.copies = Copies(sems, sizes, self.other)
        self.mine = [tuple(me[axis] for axis in order[part]) for part in self.parts]

    def send(self, kind, block, to):
        self.copies.send(kind, block, block, to)

    def first(self):
        for part in self.parts:
            m1, m2, m3 = self.mine[part]
            for by in SHIFTS:
                self.send(0, self.held.at[part, self.core, m3, m2, m1], shifted(self.me, self.order[part][0], by))

    def second(self):
        self.copies.arrived(0)
        for part in self.parts:
            m1, m2, m3 = self.mine[part]
            for by in SHIFTS:
                self.send(1, self.held.at[part, self.core, m3, m2], shifted(self.me, self.order[part][1], by))
        for part in self.parts:
            m1, m2, m3 = self.mine[part]
            self.send(5, self.held.at[part, self.core, m3, m2], self.other)

    def third(self):
        self.copies.arrived(1)
        for late in range(2):
            for part in self.parts:
                m3 = self.mine[part][2]
                for k, by in enumerate((1, 3)):
                    half = self.held.at[part, self.core, m3, pl.ds(2 * (k ^ late), 2)]
                    self.send(2 + late, half, shifted(self.me, self.order[part][2], by))
        for part in self.parts:
            m1, m2, m3 = self.mine[part]
            for by in SHIFTS:
                self.send(6, self.held.at[part, self.core, m3, (m2 - by + 4) % 4], self.other)

    def fourth(self):
        self.copies.arrived(2)
        halves = []
        for part in self.parts:
            m3 = self.mine[part][2]
            for k, by in enumerate((1, 3)):
                half = self.held.at[part, self.core, (m3 - by + 4) % 4, pl.ds(2 * k, 2)]
                self.send(4, half, shifted(self.me, self.order[part][2], by))
                halves.append(half)
        for half in halves:
            self.send(7, half, self.other)

    def fifth(self):
        self.copies.arrived(3)
        for part in self.parts:
            m3 = self.mine[part][2]
            for k, by in enumerate((1, 3)):
                self.send(8, self.held.at[part, self.core, (m3 - by + 4) % 4, pl.ds(2 - 2 * k, 2)], self.other)

    def sixth(self):
        self.copies.arrived(4)
        for part in self.parts:
            for k in range(2):
                half = self.held.at[part, self.core, (self.mine[part][2] + 2) % 4, pl.ds(2 * k, 2)]
                self.send(9, half, self.other)

    def last(self):
        for kind in range(5, 10):
            self.copies.arrived(kind)
        self.copies.finish()


def tables():
    early = np.zeros((112, 128), np.float32)
    late = np.zeros((96, 128), np.float32)
    mlp = np.zeros((192, 192), np.float32)
    for i in range(8):
        early[96 + i, 16 * i + 12] = 1
        for t in range(6):
            for w in range(2):
                early[48 * w + 6 * i + t, 16 * i + 6 * w + t] = 1
                late[48 * w + 6 * i + t, 16 * i + 6 * w + t] = 1
            for w in range(4):
                mlp[48 * w + 6 * i + t, 24 * i + 6 * w + t] = 1
    lane, column = np.arange(128)[:, None], np.arange(WIDTH)[None]
    short = ((lane < 48) & (lane % 6 == column % 6)).astype(np.float32)
    short_owner = (lane == column // 6).astype(np.float32)
    inner = (lane - 48 == column % 24).astype(np.float32)
    inner_owner = (lane[:32] == column // 24).astype(np.float32)
    return early, late, mlp, short, short_owner, inner, inner_owner


def block_bias(query_pos, query_seg, key_pos, key_seg):
    allowed = (query_seg == key_seg) & (jnp.abs(query_pos - key_pos) <= HALF_WIN)
    return jnp.where(allowed, 0.0, NEG_FILL)


class Local:
    def __init__(self, sems):
        self.sems, self.started = sems, {}

    def start(self, number, source, target):
        self.started[number] = pltpu.make_async_copy(source, target, self.sems.at[number])
        self.started[number].start()

    def wait(self, *numbers):
        for number in numbers or list(self.started):
            self.started.pop(number).wait()


def eight(held, order, part, group):
    return [held[slab_index(order, part, slab_place(group, member))] for member in range(8)]


def forward_kernel(
    wq_part, wk_part, wv_part, wo_part, win_part, wout_part,
    bq_part, bv_part, bo_part, ga_part, ba_part, bout_part, go_part, bo2_part, binner_part, seg_ref, x_any,
    early_any, late_any, mlp_any, short_any, short_owner_any, inner_any, inner_owner_any,
    wq_any, wk_any, wv_any, wo_any, win_any, wout_any, q_any, qh_any, k_any, v_any,
    e0_any, e1_any, e2_any, mixed_any, inv_any, vec_ref, top_ref, segs_ref,
    wq, wk, wv, wo, win, wout, q, qh, k, v,
    held_e, held_l, held_m, rows, xh, bias, top_cols, e0, e1, e2, mixed, inverses,
    x_ref, early_ref, late_ref, pick_mlp_ref, short_ref, short_owner_ref, inner_ref, inner_owner_ref,
    sems_e, sems_l, sems_m, sems_h, out_sem, e_sem, load_sem,
):
    me = coords()
    side = lax.axis_index("seq")
    loads = Local(load_sem)
    for number, (source, target) in enumerate((
        (x_any, x_ref), (early_any, early_ref), (late_any, late_ref), (mlp_any, pick_mlp_ref), (short_any, short_ref),
        (short_owner_any, short_owner_ref), (inner_any, inner_ref), (inner_owner_any, inner_owner_ref),
    )):
        loads.start(number, source, target)
    short = (bq_part, bv_part, bo_part, ga_part, ba_part, bout_part, go_part, bo2_part)
    row = jnp.concatenate(
        [ref[...].astype(F32).reshape(1, 6) for ref in short]
        + [binner_part[...].astype(F32).reshape(1, 24), jnp.zeros((1, WIDTH - 72), F32)], axis=1,
    )
    early_rows = jnp.concatenate(
        [wk_part[...].astype(F32), wv_part[...].astype(F32), row, jnp.zeros((3, WIDTH), F32)], axis=0
    ).astype(BF)
    late_rows = jnp.concatenate(
        [wq_part[...].astype(F32), wo_part[...].astype(F32), jnp.zeros((4, WIDTH), F32)], axis=0
    ).astype(BF)
    for part in range(WIDES):
        held_e[slab_index(WIDE_ORDER, part, me)] = early_rows[:, WIDE * part : WIDE * (part + 1)]
        held_l[slab_index(WIDE_ORDER, part, me)] = late_rows[:, WIDE * part : WIDE * (part + 1)]
    greet(me)
    early = Gather(me, held_e, sems_e, WIDE_ORDER)
    late = Gather(me, held_l, sems_l, WIDE_ORDER)
    mlp = Gather(me, held_m, sems_m, ORDER)
    outs = Local(out_sem)
    partner = shifted(me, "z", 2)
    halo = Copies(sems_h, (xh, segs_ref.at[pl.ds(3, 2)]), partner)
    early.first()
    late.first()
    mlp_rows = jnp.concatenate(
        [win_part[:, WIDTH * n : WIDTH * (n + 1)].astype(F32) for n in range(4)]
        + [wout_part[...].astype(F32)], axis=0,
    ).astype(BF)
    for part in range(PARTS):
        held_m[slab_index(ORDER, part, me)] = mlp_rows[:, PART * part : PART * (part + 1)]
    mlp.first()
    for n in range(3):
        segs_ref[n] = jnp.broadcast_to(seg_ref[:, BLOCK * n : BLOCK * (n + 1)].astype(F32), (8, BLOCK))
    early.second()
    late.second()
    loads.wait()
    for n in range(2):
        block = jnp.where(side == 1, n, 2 - n)
        rows_out = x_ref.at[pl.ds(pl.multiple_of(block * BLOCK, BLOCK), BLOCK)]
        halo.send(0, rows_out, xh.at[pl.ds(n * BLOCK, BLOCK)], partner)
        halo.send(1, segs_ref.at[block], segs_ref.at[3 + n], partner)
    early.third()
    across = lax.broadcasted_iota(jnp.int32, (1, BLOCK), 1)
    down = lax.broadcasted_iota(jnp.int32, (BLOCK, 1), 0)
    starts = [BLOCK * n for n in range(3)] + [
        jnp.where(side == 0, 768 + BLOCK * n, -BLOCK * (n + 1)) for n in range(2)
    ]
    blocks = [jnp.where(side == 0, b, 2 - b) for b in range(3)]

    def fill_bias(b, key_blocks):
        seg_here = segs_ref[blocks[b], 0:1, :]
        seg_down = jnp.broadcast_to(seg_here, (128, BLOCK)).T[:, 0:1]
        for n in key_blocks:
            bias[b, :, pl.ds(n * BLOCK, BLOCK)] = block_bias(
                blocks[b] * BLOCK + down, seg_down, starts[n] + across, segs_ref[n, 0:1, :]
            )

    for b in range(3):
        fill_bias(b, range(3))
    early.fourth()
    late.third()
    early.fifth()
    early.sixth()
    late.fourth()
    early.last()
    mlp.second()

    def unpack_early(group, _):
        at = pl.ds(pl.multiple_of(group * 48, 16), 48)
        for part in range(WIDES):
            picked = dot(early_ref[...], jnp.concatenate(eight(held_e, WIDE_ORDER, part, group), axis=0))
            for n, ref in enumerate((wk, wv)):
                ref[at, pl.ds(part * WIDE, WIDE)] = picked[48 * n : 48 * n + 48].astype(BF)
            if part == 0:
                rows[pl.ds(pl.multiple_of(group * 8, 8), 8), :] = picked[96:104, :128]
        return 0

    lax.fori_loop(0, 16, unpack_early, 0, unroll=4)
    outs.start(0, wk, wk_any)
    outs.start(1, wv, wv_any)
    lane = lax.broadcasted_iota(jnp.int32, (1, 128), 1)
    for n in range(2):
        chosen = jnp.where((lane >= 6 * n) & (lane < 6 * n + 6), rows[...], 0.0).astype(BF)
        vec_ref[n : n + 1, :] = jnp.sum(
            dot(chosen, short_ref[...]) * short_owner_ref[...], axis=0, keepdims=True
        )
    def project_key(tokens, at):
        k[at, :] = dot(tokens[...], wk[...]).astype(BF)
        v[at, :] = (dot(tokens[...], wv[...]) + vec_ref[1:2, :]).astype(BF)

    def project_query(tokens, target):
        target[...] = (dot(tokens[...], wq[...]) + vec_ref[0:1, :]).astype(BF) * jnp.asarray(0.125, BF)

    late.fifth()
    late.sixth()
    project_key(x_ref, pl.ds(0, 768))
    late.last()

    def unpack_late(group, _):
        at = pl.ds(pl.multiple_of(group * 48, 16), 48)
        for part in range(WIDES):
            picked = dot(late_ref[...], jnp.concatenate(eight(held_l, WIDE_ORDER, part, group), axis=0))
            for n, ref in enumerate((wq, wo)):
                ref[at, pl.ds(part * WIDE, WIDE)] = picked[48 * n : 48 * n + 48].astype(BF)
        return 0

    lax.fori_loop(0, 16, unpack_late, 0, unroll=4)
    mlp.third()
    outs.start(2, wq, wq_any)
    outs.start(3, wo, wo_any)
    project_query(x_ref, q)
    outs.start(4, q, q_any)

    low = lane < 64

    slots, kept = (e0, e1, e2), (e0_any, e1_any, e2_any)

    def keep_copy(b, pair):
        slot = pair if b == 0 else pair % 2
        return pltpu.make_async_copy(slots[b].at[slot], kept[b].at[pair], e_sem.at[b, slot])

    def attend(pair, those, reused):
        columns = pl.ds(pl.multiple_of(pair * 128, 128), 128)
        items = [(b, e) for b in those for e in range(2)]
        if reused:
            for b in those:
                keep_copy(b, pair - 2).wait()

        def place(b):
            return pl.ds(pl.multiple_of(blocks[b] * BLOCK, BLOCK), BLOCK)

        def scores_of(b, e):
            count = 768 + BLOCK * b
            queries = jnp.where(low if e == 0 else ~low, q[place(b), columns], jnp.zeros((), BF))
            return dot(queries, k[pl.ds(0, count), columns], NT) + bias[b, :, pl.ds(0, count)]

        scores, outs_of = scores_of(*items[0]), []
        for n, (b, e) in enumerate(items):
            later = scores_of(*items[n + 1]) if n + 1 < len(items) else None
            top = jnp.max(scores, axis=1, keepdims=True)
            weights = jnp.exp(scores - top).astype(BF)
            slots[b][pair if b == 0 else pair % 2, pl.ds(BLOCK * e, BLOCK), :] = weights
            values = v[pl.ds(0, 768 + BLOCK * b), columns]
            outs_of.append(dot(weights, jnp.where(low if e == 0 else ~low, values, jnp.ones((), BF))))
            top_cols[place(b), :] = jnp.where(lane == 2 * pair + e, top, top_cols[place(b), :])
            scores = later
            if e == 1:
                inverse = 1.0 / pltpu.roll(jnp.where(low, outs_of[1], outs_of[0]), 64, 1)
                inverses[place(b), columns] = inverse
                mixed[place(b), columns] = (jnp.where(low, outs_of[0], outs_of[1]) * inverse).astype(BF)
                outs_of = []
        for b in those:
            keep_copy(b, pair).start()

    def near(pair, _):
        attend(pair, (0,), False)
        return 0

    def far_first(pair, _):
        attend(pair, (1, 2), False)
        return 0

    def far_next(pair, _):
        attend(pair, (1, 2), True)
        return 0

    lax.fori_loop(0, 6, near, 0, unroll=2)
    halo.arrived(0)
    halo.arrived(1)
    for b in range(1, 3):
        fill_bias(b, range(3, 3 + b))
    project_key(xh, pl.ds(768, 512))
    project_query(xh, qh)
    outs.start(5, qh, qh_any)
    outs.start(6, k, k_any)
    outs.start(7, v, v_any)
    mlp.fourth()
    mlp.fifth()
    lax.fori_loop(0, 2, far_first, 0, unroll=2)
    lax.fori_loop(2, 3, far_next, 0)
    mlp.sixth()
    lax.fori_loop(3, 4, far_next, 0)
    for n in range(2, 8):
        chosen = jnp.where((lane >= 6 * n) & (lane < 6 * n + 6), rows[...], 0.0).astype(BF)
        vec_ref[n : n + 1, :] = jnp.sum(
            dot(chosen, short_ref[...]) * short_owner_ref[...], axis=0, keepdims=True
        )
    for n in range(4):
        chosen = rows[pl.ds(32 * n, 32), :].astype(BF)
        vec_ref[8 + n : 9 + n, :] = jnp.sum(
            dot(chosen, inner_ref[...]) * inner_owner_ref[...], axis=0, keepdims=True
        )
    mlp.last()

    def unpack_mlp(group, _):
        at = pl.ds(pl.multiple_of(group * 48, 16), 48)
        at_outer = pl.ds(pl.multiple_of(group * 192, 64), 192)
        for part in range(PARTS):
            slabs = eight(held_m, ORDER, part, group)
            picked = dot(pick_mlp_ref[...], jnp.concatenate([slab[:24] for slab in slabs], axis=0)).astype(BF)
            for n in range(4):
                win[at, pl.ds(n * WIDTH + part * PART, PART)] = picked[48 * n : 48 * n + 48]
            wout[at_outer, pl.ds(part * PART, PART)] = jnp.concatenate([slab[24:] for slab in slabs], axis=0)
        return 0

    lax.fori_loop(0, 16, unpack_mlp, 0, unroll=4)
    outs.start(8, win, win_any)
    outs.start(9, wout, wout_any)
    lax.fori_loop(4, 6, far_next, 0, unroll=2)
    outs.start(10, mixed, mixed_any)
    outs.start(11, inverses, inv_any)
    for b in range(3):
        top_ref[b] = top_cols[pl.ds(b * BLOCK, BLOCK), :].T[:16]
        for pair in range(0 if b == 0 else 4, 6):
            keep_copy(b, pair).wait()
    halo.finish()
    outs.wait()


def run_forward(parts, tokens, seg_row):
    early, late, mlp, short, short_owner, inner, inner_owner = tables()
    fixed = (
        jnp.asarray(early, BF), jnp.asarray(late, BF), jnp.asarray(mlp, BF), jnp.asarray(short, BF),
        jnp.asarray(short_owner), jnp.asarray(inner, BF), jnp.asarray(inner_owner),
    )
    vmem, anywhere = pl.BlockSpec(memory_space=pltpu.VMEM), pl.BlockSpec(memory_space=pl.ANY)
    large = (
        [(768, 768)] * 4 + [(768, 3072), (3072, 768), (768, 768), (512, 768), (1280, 768), (1280, 768)]
    )
    kept = [(6, 2 * BLOCK, 768 + BLOCK * b) for b in range(3)]
    small = [((16, 768), F32), ((3, 16, BLOCK), F32), ((5, 8, BLOCK), F32)]
    per_pair = [((768, 768), BF), ((768, 768), F32)]
    sems = pltpu.SemaphoreType.DMA
    return pl.pallas_call(
        forward_kernel,
        out_shape=tuple(jax.ShapeDtypeStruct(shape, BF) for shape in large + kept)
        + tuple(jax.ShapeDtypeStruct(*shape) for shape in per_pair + small),
        in_specs=[vmem] * 16 + [anywhere] * 8,
        out_specs=(anywhere,) * len(large + kept + per_pair) + (vmem,) * len(small),
        scratch_shapes=[
            *(pltpu.VMEM(shape, BF) for shape in large),
            pltpu.VMEM((WIDES, 2, 4, 4, 4, ATTN_ROWS, WIDE), BF),
            pltpu.VMEM((WIDES, 2, 4, 4, 4, ATTN_ROWS, WIDE), BF),
            pltpu.VMEM((PARTS, 2, 4, 4, 4, MLP_ROWS, PART), BF),
            pltpu.VMEM((128, 128), F32),
            pltpu.VMEM((512, 768), BF),
            pltpu.VMEM((3, BLOCK, 1280), F32),
            pltpu.VMEM((768, 128), F32),
            *(pltpu.VMEM((6 if b == 0 else 2, *shape[1:]), BF) for b, shape in enumerate(kept)),
            *(pltpu.VMEM(*shape) for shape in per_pair),
            pltpu.VMEM((768, 768), BF), *(pltpu.VMEM(one.shape, one.dtype) for one in fixed),
            *(sems((2, Gather.KINDS)) for _ in range(3)), sems((2, 2)), sems((12,)), sems((3, 6)), sems((8,)),
        ],
        compiler_params=pltpu.CompilerParams(
            collective_id=0, has_side_effects=True, vmem_limit_bytes=VMEM_BYTES
        ),
        name="gather_and_attend",
    )(*parts, seg_row, tokens, *fixed)


class Scatter:
    KINDS = 8

    def __init__(self, me, parts, own, near, halves, blocks, second, first, sems, order):
        self.order, self.every = order, range(len(order))
        self.me, self.core = me, me["c"]
        self.parts, self.own, self.near, self.halves = parts, own, near, halves
        self.blocks, self.second, self.first = blocks, second, first
        self.other = shifted(me, "c", 1)
        sizes = (near.at[:, 0],) * 4 + (halves, blocks, second, first)
        self.copies = Copies(sems, sizes, self.other)
        self.mine = [tuple(me[axis] for axis in order[part]) for part in self.every]

    def add(self, target, sources, count):
        def body(index, _):
            if len(sources) == 1:
                target[index] = target[index] + sources[0][index]
            else:
                total = target[index].astype(F32)
                for source in sources:
                    total = total + source[index].astype(F32)
                target[index] = total.astype(BF)
            return 0

        lax.fori_loop(0, count, body, 0)

    def to_sibling(self):
        for k, by in enumerate((2, 1, 3, 0)):
            for part in self.every:
                at = (self.mine[part][2] + by) % 4
                self.copies.send(k, self.parts.at[part, 1 - self.core, at], self.near.at[part, at], self.other)

    def near_sum(self, k, by):
        self.copies.arrived(k)
        for part in self.every:
            at = (self.mine[part][2] + by) % 4
            self.add(self.near.at[part, at], [self.own(part, at)], 4)

    def opposite(self):
        self.near_sum(0, 2)
        for part in self.every:
            m3 = self.mine[part][2]
            for k, by in enumerate((1, 3)):
                half = self.near.at[part, (m3 + 2) % 4, pl.ds(2 * k, 2)]
                self.copies.send(4, half, self.halves.at[part, k], shifted(self.me, self.order[part][2], by))

    def nearest(self):
        self.near_sum(1, 1)
        self.near_sum(2, 3)
        self.near_sum(3, 0)

    def neighbours(self):
        self.copies.arrived(4)
        for part in self.every:
            m3 = self.mine[part][2]
            for k, by in enumerate((1, 3)):
                block = self.near.at[part, (m3 + by) % 4]
                self.add(block.at[pl.ds(2 * k, 2)], [self.halves.at[part, k]], 2)
                self.copies.send(5, block, self.blocks.at[part, k], shifted(self.me, self.order[part][2], by))

    def middle(self):
        self.copies.arrived(5)
        for part in self.every:
            m1, m2, m3 = self.mine[part]
            block = self.near.at[part, m3]
            self.add(block, [self.blocks.at[part, 0], self.blocks.at[part, 1]], 4)
            for k, by in enumerate(SHIFTS):
                self.copies.send(
                    6, block.at[(m2 + by) % 4], self.second.at[part, k], shifted(self.me, self.order[part][1], by)
                )

    def final(self):
        self.copies.arrived(6)
        for part in self.every:
            m1, m2, m3 = self.mine[part]
            block = self.near.at[part, m3, pl.ds(m2, 1)]
            self.add(block, [self.second.at[part, pl.ds(k, 1)] for k in range(3)], 1)
            for k, by in enumerate(SHIFTS):
                self.copies.send(
                    7, block.at[0, (m1 + by) % 4], self.first.at[part, k], shifted(self.me, self.order[part][0], by)
                )

    def result(self, out_ref):
        self.copies.arrived(7)
        for part in self.every:
            m1, m2, m3 = self.mine[part]
            total = self.near[part, m3, m2, m1].astype(F32)
            for k in range(3):
                total = total + self.first[part, k].astype(F32)
            out_ref[part] = total
        self.copies.finish()


def row_sum(block):
    return jnp.sum(block, axis=0, keepdims=True)


def normed_of(hidden):
    centred = hidden - jnp.mean(hidden, axis=1, keepdims=True)
    inverse = lax.rsqrt(jnp.mean(centred * centred, axis=1, keepdims=True) + EPS)
    return centred * inverse, inverse


def dense_kernel(
    x_any, mixed_any, cot_any, wo_any, win_any, wout_any, inv_any, vec_ref, put_mlp_ref, heads_ref,
    out_any, dwo_any, hidden_any, gmix_any, parts_any, delta_ref, sums_ref,
    x, mixed, cot, wo, win, wout, inv, out, gmix, parts,
    active, slope, normed, inverse, first_bf, total, grad_bf, load_sem, store_sem, chunk_sem,
):
    loads, stores = Local(load_sem), Local(store_sem)
    for n, (source, target) in enumerate(((mixed_any, mixed), (wo_any, wo), (x_any, x))):
        loads.start(n, source, target)

    def chunk_loads(index):
        columns = pl.ds(pl.multiple_of(index * WIDTH, WIDTH), WIDTH)
        return (
            pltpu.make_async_copy(win_any.at[:, columns], win.at[:, columns], chunk_sem.at[0, index]),
            pltpu.make_async_copy(wout_any.at[columns], wout.at[columns], chunk_sem.at[1, index]),
        )

    sums_ref[...] = jnp.zeros_like(sums_ref)

    def add_sum(row, block):
        sums_ref[pl.ds(row, 1), :] += row_sum(block)

    def row_block(index):
        return pl.ds(pl.multiple_of(index * BLOCK, BLOCK), BLOCK)

    loads.wait(0, 1, 2)
    for n in range(4):
        for one in chunk_loads(n):
            one.start()
    loads.start(3, cot_any, cot)
    loads.start(4, inv_any, inv)

    def branch_of(index):
        return dot(mixed[row_block(index), :], wo[...]) + vec_ref[2:3, :]

    branch = branch_of(0)
    for n in range(3):
        later = branch_of(n + 1) if n < 2 else None
        at = row_block(n)
        normed[at, :], spread = normed_of(x[at, :].astype(F32) + branch)
        inverse[at, :] = jnp.broadcast_to(spread, (BLOCK, 128))
        first_bf[at, :] = (normed[at, :] * vec_ref[3:4, :] + vec_ref[4:5, :]).astype(BF)
        branch = later
    rate, bend = math.sqrt(2 / math.pi), 0.044715

    def inner_of(n):
        for one in chunk_loads(n):
            one.wait()
        return dot(first_bf[...], win[:, WIDTH * n : WIDTH * (n + 1)]) + vec_ref[8 + n : 9 + n, :]

    u = inner_of(0)
    for n in range(4):
        later = inner_of(n + 1) if n < 3 else None
        columns = slice(WIDTH * n, WIDTH * (n + 1))
        square = u * u
        bent = jnp.tanh(rate * u * (1 + bend * square))
        half = 0.5 * (1 + bent)
        active[:, columns] = (u * half).astype(BF)
        slope[:, columns] = (
            half + u * half * (1 - bent) * (rate + (3 * rate * bend) * square)
        ).astype(BF)
        outer = dot(active[:, columns], wout[columns, :])
        total[...] = outer if n == 0 else total[...] + outer
        u = later

    def norm_two(index, _):
        at = row_block(index)
        first = normed[at, :] * vec_ref[3:4, :] + vec_ref[4:5, :]
        normed_two, spread = normed_of(first + (total[at, :] + vec_ref[5:6, :]))
        out[at, :] = (normed_two * vec_ref[6:7, :] + vec_ref[7:8, :]).astype(BF)
        grad = cot[at, :].astype(F32)
        add_sum(6, grad * normed_two)
        add_sum(7, grad)
        scaled = grad * vec_ref[6:7, :]
        mean_grad = jnp.mean(scaled, axis=1, keepdims=True)
        mean_cross = jnp.mean(scaled * normed_two, axis=1, keepdims=True)
        back = spread * (scaled - mean_grad - normed_two * mean_cross)
        total[at, :] = back
        grad_bf[at, :] = back.astype(BF)
        add_sum(5, grad_bf[at, :].astype(F32))
        return 0

    loads.wait(3)
    lax.fori_loop(0, 3, norm_two, 0)
    stores.start(0, out, out_any)

    def outer_block(index, _):
        columns = pl.ds(pl.multiple_of(index * WIDTH, WIDTH), WIDTH)
        grad_inner = (dot(grad_bf[...], wout[columns, :], NT) * slope[:, columns].astype(F32)).astype(BF)
        add_sum(8 + index, grad_inner.astype(F32))
        total[...] += dot(grad_inner, win[:, columns], NT)
        active[:, columns] = dot(active[:, columns], grad_bf[...], TN).astype(BF)
        slope[:, columns] = dot(first_bf[...], grad_inner, TN).astype(BF)
        return 0

    lax.fori_loop(0, 4, outer_block, 0)

    for part in range(WIDES):

        def pack(group, _):
            at = pl.ds(pl.multiple_of(group * 48, 16), 48)
            at_outer = pl.ds(pl.multiple_of((group % 4) * 192, 64), 192)
            pieces = [slope[at, pl.ds(k * WIDTH + part * WIDE, WIDE)] for k in range(4)]
            placed = dot(put_mlp_ref[...], jnp.concatenate(pieces, axis=0)).astype(BF)
            outer_columns = pl.ds(pl.multiple_of((group // 4) * WIDTH + part * WIDE, 128), WIDE)
            outer = active[at_outer, outer_columns]
            for member in range(8):
                these = slice(24 * member, 24 * member + 24)
                parts[slab_index(BACK_ORDER, part, slab_place(group, member))] = jnp.concatenate(
                    [placed[these], outer[these]], axis=0
                )
            return 0

        lax.fori_loop(0, 16, pack, 0, unroll=4)
        stores.start(4 + part, parts.at[part], parts_any.at[part])

    def back_one(index, _):
        at = row_block(index)
        grad, normed_one = total[at, :], normed[at, :]
        add_sum(3, grad * normed_one)
        add_sum(4, grad)
        scaled = grad * vec_ref[3:4, :]
        mean_grad = jnp.mean(scaled, axis=1, keepdims=True)
        mean_cross = jnp.mean(scaled * normed_one, axis=1, keepdims=True)
        back = inverse[at, 0:1] * (scaled - mean_grad - normed_one * mean_cross)
        total[at, :] = back
        grad_bf[at, :] = back.astype(BF)
        add_sum(2, grad_bf[at, :].astype(F32))
        return 0

    lax.fori_loop(0, 3, back_one, 0)
    stores.start(1, total, hidden_any)
    loads.wait(4)
    gmix[...] = (dot(grad_bf[...], wo[...], NT) * inv[...]).astype(BF)
    stores.start(2, gmix, gmix_any)
    first_bf[...] = dot(mixed[...], grad_bf[...], TN).astype(BF)
    stores.start(3, first_bf, dwo_any)

    for k in range(3):
        at = pl.ds(BLOCK * k, BLOCK)
        product = mixed[at, :].astype(F32) * gmix[at, :].astype(F32)
        high = product.astype(BF)
        rest = (product - high.astype(F32)).astype(BF)
        delta_ref[k] = dot(heads_ref[...], high, NT) + dot(heads_ref[...], rest, NT)
    stores.wait()


def run_dense(tokens, mixed, cot, wo, win, wout, inv, vec):
    mlp = tables()[2]
    heads = (np.arange(16)[:, None] == np.arange(WIDTH)[None] // 64).astype(np.float32)
    vmem, anywhere = pl.BlockSpec(memory_space=pltpu.VMEM), pl.BlockSpec(memory_space=pl.ANY)
    parts_shape = (WIDES, 2, 4, 4, 4, MLP_ROWS, WIDE)
    shapes = (
        ((768, 768), BF), ((768, 768), BF), ((768, 768), F32), ((768, 768), BF), (parts_shape, BF),
        ((3, 16, BLOCK), F32), ((16, 768), F32),
    )
    sems = pltpu.SemaphoreType.DMA
    return pl.pallas_call(
        dense_kernel,
        out_shape=tuple(jax.ShapeDtypeStruct(*shape) for shape in shapes),
        in_specs=[anywhere] * 7 + [vmem] * 3,
        out_specs=(anywhere,) * 5 + (vmem,) * 2,
        scratch_shapes=[
            *(pltpu.VMEM((768, 768), BF) for _ in range(4)),
            pltpu.VMEM((768, 3072), BF), pltpu.VMEM((3072, 768), BF), pltpu.VMEM((768, 768), F32),
            pltpu.VMEM((768, 768), BF), pltpu.VMEM((768, 768), BF), pltpu.VMEM(parts_shape, BF),
            pltpu.VMEM((768, 3072), BF), pltpu.VMEM((768, 3072), BF), pltpu.VMEM((768, 768), F32),
            pltpu.VMEM((768, 128), F32), pltpu.VMEM((768, 768), BF), pltpu.VMEM((768, 768), F32),
            pltpu.VMEM((768, 768), BF), sems((5,)), sems((7,)), sems((2, 4)),
        ],
        compiler_params=pltpu.CompilerParams(vmem_limit_bytes=VMEM_BYTES),
        name="feed_forward",
    )(tokens, mixed, cot, wo, win, wout, inv, vec, jnp.asarray(mlp.T, BF), jnp.asarray(heads, BF))


def backward_kernel(
    q_any, qh_any, k_any, v_any, g_any, x_any, wq_any, wk_any, wv_any, hidden_any, mlp_any,
    e0_any, e1_any, e2_any, dwo_any, put_early_any, put_late_any, short_any, short_owner_any, inner_any,
    inner_owner_any, top_ref, delta_ref, segs_ref, sums_ref,
    grad_any, early_out, late_out, mlp_out,
    q, qh, k, v, g, gh, stats, stat_cols, own_m, e0, e1, e2, bias, dq, dk, dv, grad_k, grad_v,
    dw, dwv, rows, hidden,
    dwo_ref, put_early_ref, put_late_ref, short_ref, short_owner_ref, inner_ref, inner_owner_ref,
    parts, near_e, halves_e, blocks_e, second_e, first_e,
    near_l, halves_l, blocks_l, second_l, first_l,
    near_m, halves_m, blocks_m, second_m, first_m,
    load_sem, e_sem, sems_e, sems_l, sems_m, sems_h,
):
    me = coords()
    core = me["c"]
    side = lax.axis_index("seq")
    partner = shifted(me, "z", 2)
    loads = Local(load_sem)
    kept, slots = (e0_any, e1_any, e2_any), (e0, e1, e2)

    def keep_copy(b, pair):
        return pltpu.make_async_copy(kept[b].at[pair], slots[b].at[pair % 2], e_sem.at[b, pair % 2])

    for number, (source, target) in enumerate(((g_any, g), (v_any, v), (q_any, q), (k_any, k))):
        loads.start(number, source, target)
    for b in range(3):
        keep_copy(b, 0).start()
    for b in range(3):
        stats[b, 0:16, :] = top_ref[b]
        stats[b, 16:32, :] = delta_ref[b]

    def turn(block):
        both = jnp.concatenate([stats[block], jnp.zeros((96, BLOCK), F32)], axis=0)
        stat_cols[block] = both.T

    for b in range(3):
        turn(b)
    greet(me)
    mlp = Scatter(
        me, mlp_any, lambda part, at: own_m.at[part, at], near_m, halves_m, blocks_m, second_m, first_m,
        sems_m, BACK_ORDER,
    )
    early = Scatter(
        me, parts, lambda part, at: parts.at[part, core, at], near_e, halves_e, blocks_e, second_e,
        first_e, sems_e, ORDER,
    )
    late = Scatter(
        me, parts, lambda part, at: parts.at[part, core, at], near_l, halves_l, blocks_l, second_l,
        first_l, sems_l, ORDER,
    )
    halo = Copies(sems_h, (gh, stats.at[pl.ds(3, 2)]), partner)
    loads.wait(0)
    for n in range(2):
        block = jnp.where(side == 1, n, 2 - n)
        rows_out = g.at[pl.ds(pl.multiple_of(block * BLOCK, BLOCK), BLOCK)]
        halo.send(0, rows_out, gh.at[pl.ds(n * BLOCK, BLOCK)], partner)
        halo.send(1, stats.at[block], stats.at[3 + n], partner)
    mlp.to_sibling()

    loads.start(5, mlp_any.at[:, core], own_m)
    loads.start(4, qh_any, qh)
    for number, (source, target) in enumerate((
        (dwo_any, dwo_ref), (put_early_any, put_early_ref), (put_late_any, put_late_ref), (short_any, short_ref),
        (short_owner_any, short_owner_ref), (inner_any, inner_ref), (inner_owner_any, inner_owner_ref),
    ), 12):
        loads.start(number, source, target)
    loads.start(6, hidden_any, hidden)
    across = lax.broadcasted_iota(jnp.int32, (1, BLOCK), 1)
    down = lax.broadcasted_iota(jnp.int32, (BLOCK, 1), 0)
    blocks = [jnp.where(side == 0, b, 2 - b) for b in range(3)]
    reach = [
        (jnp.where(side == 0, BLOCK * (1 + n), 0), BLOCK * (2 - n)) for n in range(2)
    ]

    def fill_bias():
        for n in range(2):
            seg_down = jnp.broadcast_to(segs_ref[3 + n, 0:1, :], (128, BLOCK)).T[:, 0:1]
            start = jnp.where(side == 0, 768 + BLOCK * n, -BLOCK * (n + 1))
            for m in range(2 - n):
                block = jnp.where(side == 0, 1 + n + m, m)
                bias[n, :, pl.ds(m * BLOCK, BLOCK)] = block_bias(
                    start + down, seg_down, block * BLOCK + across, segs_ref[block, 0:1, :]
                )

    dk[...] = jnp.zeros_like(dk)
    dv[...] = jnp.zeros_like(dv)
    lane = lax.broadcasted_iota(jnp.int32, (1, 128), 1)
    low = lane < 64
    high_rows = lax.broadcasted_iota(jnp.int32, (128, 1), 0) >= 64
    nothing = jnp.zeros((), BF)

    def one_head(block, e):
        return jnp.where(low if e == 0 else ~low, block, nothing)

    def two_heads(turned):
        return jnp.concatenate(
            [jnp.where(high_rows, nothing, turned), jnp.where(high_rows, turned, nothing)], axis=1
        )

    def stat(block, row):
        return jnp.sum(jnp.where(lane == row, stat_cols[block], 0.0), axis=1, keepdims=True)

    def own_pair(pair, ahead):
        columns = pl.ds(pl.multiple_of(pair * 128, 128), 128)
        here = pl.ds(pl.multiple_of(pair * 128, 128), 128)
        for b in range(3):
            keep_copy(b, pair).wait()
        if ahead:
            for b in range(3):
                keep_copy(b, pair + 1).start()

        def place(b):
            return pl.ds(pl.multiple_of(blocks[b] * BLOCK, BLOCK), BLOCK)

        def products(b):
            values = v[pl.ds(0, 768 + BLOCK * b), columns]
            return [dot(one_head(g[place(b), columns], e), values, NT) for e in range(2)]

        grad_weights = products(0)
        for b in range(3):
            later = products(b + 1) if b < 2 else None
            weights = slots[b].at[pair % 2]
            grad_scores = [
                (
                    weights[pl.ds(BLOCK * e, BLOCK), :].astype(F32)
                    * (grad_weights[e] - stat(blocks[b], 16 + 2 * pair + e))
                ).astype(BF)
                for e in range(2)
            ]
            own = jnp.concatenate([block[:, :768] for block in grad_scores], axis=0)
            dk[here, :] += dot(two_heads(q[place(b), columns].T), own)
            dv[here, :] += dot(two_heads(g[place(b), columns].T), weights[:, pl.ds(0, 768)])
            keys = k[pl.ds(0, 768 + BLOCK * b), columns]
            grad_query = dot(grad_scores[0], one_head(keys, 0)) + dot(grad_scores[1], one_head(keys, 1))
            dq[place(b), columns] = (grad_query * 0.125).astype(BF)
            grad_weights = later

    def own_next(pair, _):
        own_pair(pair, True)
        return 0

    def own_last(pair, _):
        own_pair(pair, False)
        return 0

    def halo_pair(pair, _):
        columns = pl.ds(pl.multiple_of(pair * 128, 128), 128)
        here = pl.ds(pl.multiple_of(pair * 128, 128), 128)
        items = [(n, e) for n in range(2) for e in range(2)]

        def keys_at(n):
            return pl.ds(pl.multiple_of(reach[n][0], BLOCK), reach[n][1])

        def products(n, e):
            those = pl.ds(n * BLOCK, BLOCK)
            scores = dot(one_head(qh[those, columns], e), k[keys_at(n), columns], NT)
            grad_weights = dot(one_head(gh[those, columns], e), v[keys_at(n), columns], NT)
            return scores + bias[n, :, pl.ds(0, reach[n][1])], grad_weights

        ready = [products(*item) for item in items]
        for n in range(2):
            weights, grad_scores = [], []
            for e in range(2):
                scores, grad_weights = ready[2 * n + e]
                raised = jnp.exp(scores - stat(3 + n, 2 * pair + e))
                weights.append(raised.astype(BF))
                grad_scores.append((raised * (grad_weights - stat(3 + n, 16 + 2 * pair + e))).astype(BF))
            those = pl.ds(n * BLOCK, BLOCK)
            dk[here, keys_at(n)] += dot(two_heads(qh[those, columns].T), jnp.concatenate(grad_scores, axis=0))
            dv[here, keys_at(n)] += dot(two_heads(gh[those, columns].T), jnp.concatenate(weights, axis=0))
        grad_k[:, columns] = dk[here, :].T.astype(BF)
        grad_v[:, columns] = dv[here, :].T.astype(BF)
        return 0

    fill_bias()
    loads.wait(1, 2, 3)
    lax.fori_loop(0, 1, own_next, 0)
    loads.wait(5)
    mlp.opposite()
    lax.fori_loop(1, 3, own_next, 0)
    mlp.nearest()
    lax.fori_loop(3, 4, own_next, 0)
    mlp.neighbours()
    lax.fori_loop(4, 5, own_next, 0)
    lax.fori_loop(5, 6, own_last, 0)
    halo.finish()
    loads.start(7, x_any, g)
    loads.start(8, wq_any, q)
    loads.wait(7, *range(12, 19))
    dw[...] = dot(g[...], dq[...], TN).astype(BF)

    def pack_late(group, _):
        at = pl.ds(pl.multiple_of(group * 48, 16), 48)
        for part in range(PARTS):
            columns = pl.ds(part * PART, PART)
            pieces = jnp.concatenate([dw[at, columns], dwo_ref[at, columns]], axis=0)
            placed = dot(put_late_ref[...], pieces).astype(BF)
            for member in range(8):
                parts[slab_index(ORDER, part, slab_place(group, member))] = placed[16 * member : 16 * member + 16]
        return 0

    lax.fori_loop(0, 16, pack_late, 0, unroll=4)
    late.to_sibling()
    halo.arrived(0)
    halo.arrived(1)
    for n in range(2):
        turn(3 + n)
    loads.wait(4)
    lax.fori_loop(0, 2, halo_pair, 0, unroll=2)
    late.opposite()
    late.nearest()
    lax.fori_loop(2, 4, halo_pair, 0, unroll=2)
    mlp.middle()
    late.neighbours()
    lax.fori_loop(4, 6, halo_pair, 0, unroll=2)
    loads.start(9, wk_any, k.at[pl.ds(0, 768)])
    loads.start(10, wv_any, v.at[pl.ds(0, 768)])
    dw[...] = dot(g[...], grad_k[...], TN).astype(BF)
    dwv[...] = dot(g[...], grad_v[...], TN).astype(BF)

    rows[...] = jnp.zeros_like(rows)
    for n in range(8):
        if n == 0:
            vec = row_sum(dq[...].astype(F32))
        elif n == 1:
            vec = row_sum(grad_v[...].astype(F32))
        else:
            vec = sums_ref[n : n + 1, :]
        spread = dot((short_owner_ref[...] * vec).astype(BF), short_ref[...], NT)
        rows[...] = jnp.where((lane >= 6 * n) & (lane < 6 * n + 6), spread, rows[...])
    for n in range(4):
        spread = dot((inner_owner_ref[...] * sums_ref[8 + n : 9 + n, :]).astype(BF), inner_ref[...], NT)
        at = pl.ds(32 * n, 32)
        rows[at, :] = jnp.where((lane >= 48) & (lane < 72), spread, rows[at, :])

    def pack_early(group, _):
        at = pl.ds(pl.multiple_of(group * 48, 16), 48)
        vec = rows[pl.ds(pl.multiple_of(group * 8, 8), 8), :]
        vec = jnp.concatenate([vec, jnp.zeros_like(vec)], axis=1)
        vec = jnp.concatenate([vec, jnp.zeros_like(vec)], axis=0).astype(BF)
        for part in range(PARTS):
            columns = pl.ds(part * PART, PART)
            last = vec if part == 0 else jnp.zeros_like(vec)
            pieces = jnp.concatenate([dw[at, columns], dwv[at, columns], last], axis=0)
            placed = dot(put_early_ref[...], pieces).astype(BF)
            for member in range(8):
                parts[slab_index(ORDER, part, slab_place(group, member))] = placed[16 * member : 16 * member + 16]
        return 0

    late.copies.sent(0, 1, 2, 3)
    lax.fori_loop(0, 16, pack_early, 0, unroll=4)
    early.to_sibling()
    loads.wait(6, 8)
    hidden[...] += dot(dq[...], q[...], NT)
    early.opposite()
    early.nearest()
    loads.wait(9)
    hidden[...] += dot(grad_k[...], k[pl.ds(0, 768), :], NT)
    early.neighbours()
    late.middle()
    mlp.final()
    loads.wait(10)
    hidden[...] += dot(grad_v[...], v[pl.ds(0, 768), :], NT)
    loads.start(11, hidden, grad_any)
    early.middle()
    late.final()
    early.final()
    mlp.result(mlp_out)
    late.result(late_out)
    early.result(early_out)
    loads.wait()


def run_backward(q, qh, k, v, g, x, wq, wk, wv, hidden, mlp, kept, top, delta, segs, dwo, sums):
    early, late, _, short, short_owner, inner, inner_owner = tables()
    fixed = (
        jnp.asarray(early.T, BF), jnp.asarray(late.T, BF), jnp.asarray(short, BF),
        jnp.asarray(short_owner), jnp.asarray(inner, BF), jnp.asarray(inner_owner),
    )
    vmem, anywhere = pl.BlockSpec(memory_space=pltpu.VMEM), pl.BlockSpec(memory_space=pl.ANY)
    sems = pltpu.SemaphoreType.DMA

    def steps(parts, rows, width):
        return [
            pltpu.VMEM((parts, *lead, rows, width), BF)
            for lead in ((4, 4, 4), (2, 2, 4), (2, 4, 4), (3, 4), (3,))
        ]

    return pl.pallas_call(
        backward_kernel,
        out_shape=(
            jax.ShapeDtypeStruct((768, 768), F32),
            jax.ShapeDtypeStruct((PARTS, ATTN_ROWS, PART), F32),
            jax.ShapeDtypeStruct((PARTS, ATTN_ROWS, PART), F32),
            jax.ShapeDtypeStruct((WIDES, MLP_ROWS, WIDE), F32),
        ),
        in_specs=[anywhere] * 21 + [vmem] * 4,
        out_specs=(anywhere, vmem, vmem, vmem),
        scratch_shapes=[
            pltpu.VMEM((768, 768), BF), pltpu.VMEM((512, 768), BF),
            pltpu.VMEM((1280, 768), BF), pltpu.VMEM((1280, 768), BF),
            pltpu.VMEM((768, 768), BF), pltpu.VMEM((512, 768), BF),
            pltpu.VMEM((5, 32, BLOCK), F32), pltpu.VMEM((5, BLOCK, 128), F32),
            pltpu.VMEM((WIDES, 4, 4, 4, MLP_ROWS, WIDE), BF),
            *(pltpu.VMEM((2, *one.shape[1:]), BF) for one in kept), pltpu.VMEM((2, BLOCK, 512), F32),
            pltpu.VMEM((768, 768), BF), pltpu.VMEM((768, 768), F32), pltpu.VMEM((768, 768), F32),
            *(pltpu.VMEM((768, 768), BF) for _ in range(4)),
            pltpu.VMEM((128, 128), F32), pltpu.VMEM((768, 768), F32), pltpu.VMEM((768, 768), BF),
            *(pltpu.VMEM(one.shape, one.dtype) for one in fixed),
            pltpu.VMEM((PARTS, 2, 4, 4, 4, ATTN_ROWS, PART), BF),
            *steps(PARTS, ATTN_ROWS, PART), *steps(PARTS, ATTN_ROWS, PART), *steps(WIDES, MLP_ROWS, WIDE),
            sems((19,)), sems((3, 2)), *(sems((2, Scatter.KINDS)) for _ in range(3)), sems((2, 2)),
        ],
        compiler_params=pltpu.CompilerParams(
            collective_id=1, has_side_effects=True, vmem_limit_bytes=VMEM_BYTES
        ),
        name="attend_back_and_scatter",
    )(q, qh, k, v, g, x, wq, wk, wv, hidden, mlp, *kept, dwo, *fixed, top, delta, segs, sums)


def split_kernel(early_any, late_any, mlp_any, grad_any, grad_out, wq, wk, wv, wo, win, wout, inner, *rest):
    short, (early, late, mlp, staged, sums_sem, sems) = rest[:8], rest[8:]
    moves, sums = [], Local(sums_sem)
    for k in range(3):
        at = pl.ds(BLOCK * k, BLOCK)
        moves.append([
            pltpu.make_async_copy(grad_any.at[at], staged.at[at], sems.at[0, k]),
            pltpu.make_async_copy(staged.at[at], grad_out.at[at], sems.at[1, k]),
        ])
        moves[k][0].start()
    for number, (source, target) in enumerate(((early_any, early), (late_any, late), (mlp_any, mlp))):
        sums.start(number, source, target)
    for fetch, put in moves:
        fetch.wait()
        put.start()
    sums.wait()
    for part in range(PARTS):
        columns = pl.ds(PART * part, PART)
        for ref, source, row in ((wk, early, 0), (wv, early, 6), (wq, late, 0), (wo, late, 6)):
            ref[:, columns] = source[part, row : row + 6, :]
    for part in range(WIDES):
        for k in range(4):
            win[:, pl.ds(WIDTH * k + WIDE * part, WIDE)] = mlp[part, 6 * k : 6 * k + 6, :]
        wout[:, pl.ds(WIDE * part, WIDE)] = mlp[part, 24:48, :]
    inner[...] = early[0, 12, 48:72]
    for k in range(8):
        short[k][...] = early[0, 12, 6 * k : 6 * k + 6]
    for fetch, put in moves:
        put.wait()


def split_results(early, late, mlp, grad):
    vmem, anywhere = pl.BlockSpec(memory_space=pltpu.VMEM), pl.BlockSpec(memory_space=pl.ANY)
    shapes = ((768, 768),) + ((6, 768),) * 4 + ((6, 3072), (24, 768), (24,)) + ((6,),) * 8
    return pl.pallas_call(
        split_kernel,
        out_shape=tuple(jax.ShapeDtypeStruct(shape, F32) for shape in shapes),
        in_specs=[anywhere] * 4,
        out_specs=(anywhere,) + (vmem,) * (len(shapes) - 1),
        scratch_shapes=[
            *(pltpu.VMEM(one.shape, F32) for one in (early, late, mlp)), pltpu.VMEM((768, 768), F32),
            pltpu.SemaphoreType.DMA((3,)), pltpu.SemaphoreType.DMA((2, 3)),
        ],
        compiler_params=pltpu.CompilerParams(vmem_limit_bytes=VMEM_BYTES),
        name="split_gradients",
    )(early, late, mlp, grad)


def per_device(
    inputs,
    segments,
    w_query,
    w_key,
    w_value,
    w_output,
    b_query,
    b_value,
    b_output,
    gain_attn,
    bias_attn,
    w_inner,
    b_inner,
    w_outer,
    b_outer,
    gain_out,
    bias_out,
    cotangent,
):
    tokens = inputs.reshape(768, 768)
    short = (b_query, b_value, b_output, gain_attn, bias_attn, b_outer, gain_out, bias_out)
    parts = (w_query, w_key, w_value, w_output, w_inner, w_outer, *short, b_inner)
    wq, wk, wv, wo, win, wout, q, qh, k, v, *kept, mixed, inv, vec, top, segs = run_forward(parts, tokens, segments)
    out, dwo, hidden, gmix, mlp, delta, sums = run_dense(
        tokens, mixed, cotangent.reshape(768, 768), wo, win, wout, inv, vec
    )
    grad_input, early_sum, late_sum, mlp_sum = run_backward(
        q, qh, k, v, gmix, tokens, wq, wk, wv, hidden, mlp, kept, top, delta, segs, dwo, sums
    )
    grad_input, dwq, dwk, dwv, dwo, dwin, dwout, inner, *short = split_results(
        early_sum, late_sum, mlp_sum, grad_input
    )
    return (
        out.reshape(1, 768, 768),
        grad_input.reshape(1, 768, 768),
        dwq,
        dwk,
        dwv,
        dwo,
        *short[:5],
        dwin,
        inner,
        dwout,
        *short[5:],
    )


def solution(mesh):
    return jax.shard_map(
        per_device,
        mesh=mesh,
        in_specs=(
            P("dp", "seq", None),
            P("dp", "seq"),
            P(("seq", "dp"), None),
            P(("seq", "dp"), None),
            P(("seq", "dp"), None),
            P(("seq", "dp"), None),
            P(("seq", "dp")),
            P(("seq", "dp")),
            P(("seq", "dp")),
            P(("seq", "dp")),
            P(("seq", "dp")),
            P(("seq", "dp"), None),
            P(("seq", "dp")),
            P(("seq", "dp"), None),
            P(("seq", "dp")),
            P(("seq", "dp")),
            P(("seq", "dp")),
            P("dp", "seq", None),
        ),
        out_specs=(
            P("dp", "seq", None),
            P("dp", "seq", None),
            P(("seq", "dp"), None),
            P(("seq", "dp"), None),
            P(("seq", "dp"), None),
            P(("seq", "dp"), None),
            P(("seq", "dp")),
            P(("seq", "dp")),
            P(("seq", "dp")),
            P(("seq", "dp")),
            P(("seq", "dp")),
            P(("seq", "dp"), None),
            P(("seq", "dp")),
            P(("seq", "dp"), None),
            P(("seq", "dp")),
            P(("seq", "dp")),
            P(("seq", "dp")),
        ),
        check_vma=False,
    )
```

```python
import math

import jax
import jax.numpy as jnp
import numpy as np
from jax import lax
from jax.experimental import pallas as pl
from jax.experimental.pallas import tpu as pltpu
from jax.sharding import PartitionSpec as P

HALF_WIN = 512
EPS = 1e-12
NEG_FILL = -1e30


MESH = pl.DeviceIdType.MESH
BF, F32 = jnp.bfloat16, jnp.float32
WIDTH = 768
PART, PARTS = 256, 3
WIDE, WIDES = 384, 2
BLOCK = 256
ATTN_ROWS, MLP_ROWS = 16, 48
ORDER = (("x", "y", "z"), ("y", "z", "x"), ("z", "x", "y"))
WIDE_ORDER = (("z", "x", "y"), ("z", "y", "x"))
BACK_ORDER = (("x", "z", "y"), ("z", "y", "x"))
SHIFTS = (1, 3, 2)
VMEM_BYTES = 62 * 2**20
NN = (((1,), (0,)), ((), ()))
NT = (((1,), (1,)), ((), ()))
TN = (((0,), (0,)), ((), ()))


def dot(one, two, dims=NN):
    return lax.dot_general(one, two, dims, preferred_element_type=F32)


def coords():
    seq, dp = lax.axis_index("seq"), lax.axis_index("dp")
    return {"x": (dp // 4) % 4, "y": dp // 16, "z": seq * 2 + (dp // 2) % 2, "c": dp % 2}


def device(place):
    return {
        "seq": place["z"] // 2,
        "dp": place["y"] * 16 + place["x"] * 4 + (place["z"] % 2) * 2 + place["c"],
    }


def shifted(place, axis, by):
    moved = dict(place)
    moved[axis] = (place[axis] + by) % (2 if axis == "c" else 4)
    return device(moved)


def greet(place):
    barrier = pltpu.get_barrier_semaphore()
    others = [shifted(place, axis, by) for axis in "xyz" for by in SHIFTS] + [shifted(place, "c", 1)]
    for other in others:
        pl.semaphore_signal(barrier, inc=1, device_id=other, device_id_type=MESH)
    pl.semaphore_wait(barrier, len(others))


def slab_place(group, member):
    return {
        "x": (group % 2) * 2 + member // 4,
        "y": (group // 2) % 4,
        "z": (group // 8) * 2 + (member // 2) % 2,
        "c": member % 2,
    }


def slab_index(order, part, place):
    first, second, third = (place[axis] for axis in order[part])
    return (part, place["c"], third, second, first)


class Copies:
    def __init__(self, sems, sizes, anyone):
        self.sems, self.sizes, self.anyone = sems, sizes, anyone
        self.kinds = set()

    def describe(self, kind, source, target, to):
        return pltpu.make_async_remote_copy(
            src_ref=source, dst_ref=target, send_sem=self.sems.at[0, kind], recv_sem=self.sems.at[1, kind],
            device_id=to, device_id_type=MESH,
        )

    def send(self, kind, source, target, to):
        self.describe(kind, source, target, to).start()
        self.kinds.add(kind)

    def arrived(self, kind):
        self.describe(kind, self.sizes[kind], self.sizes[kind], self.anyone).wait_recv()

    def sent(self, *kinds):
        for kind in kinds:
            self.describe(kind, self.sizes[kind], self.sizes[kind], self.anyone).wait_send()
            self.kinds.remove(kind)

    def finish(self):
        self.sent(*sorted(self.kinds))


class Gather:
    KINDS = 10

    def __init__(self, me, held, sems, order):
        self.order, self.parts = order, range(len(order))
        self.me, self.held, self.core = me, held, me["c"]
        self.other = shifted(me, "c", 1)
        all_parts = held.at[:, self.core]
        three, two = pl.ds(0, 3), pl.ds(0, 2)
        sizes = (
            all_parts.at[:, 0, 0, three], all_parts.at[:, 0, three], all_parts.at[:, two, two],
            all_parts.at[:, two, two], all_parts.at[:, two, two], all_parts.at[:, 0, 0],
            all_parts.at[:, 0, three], all_parts.at[:, two, two], all_parts.at[:, two, two],
            all_parts.at[:, two, two],
        )
        self.copies = Copies(sems, sizes, self.other)
        self.mine = [tuple(me[axis] for axis in order[part]) for part in self.parts]

    def send(self, kind, block, to):
        self.copies.send(kind, block, block, to)

    def first(self):
        for part in self.parts:
            m1, m2, m3 = self.mine[part]
            for by in SHIFTS:
                self.send(0, self.held.at[part, self.core, m3, m2, m1], shifted(self.me, self.order[part][0], by))

    def second(self):
        self.copies.arrived(0)
        for part in self.parts:
            m1, m2, m3 = self.mine[part]
            for by in SHIFTS:
                self.send(1, self.held.at[part, self.core, m3, m2], shifted(self.me, self.order[part][1], by))
        for part in self.parts:
            m1, m2, m3 = self.mine[part]
            self.send(5, self.held.at[part, self.core, m3, m2], self.other)

    def third(self):
        self.copies.arrived(1)
        for late in range(2):
            for part in self.parts:
                m3 = self.mine[part][2]
                for k, by in enumerate((1, 3)):
                    half = self.held.at[part, self.core, m3, pl.ds(2 * (k ^ late), 2)]
                    self.send(2 + late, half, shifted(self.me, self.order[part][2], by))
        for part in self.parts:
            m1, m2, m3 = self.mine[part]
            for by in SHIFTS:
                self.send(6, self.held.at[part, self.core, m3, (m2 - by + 4) % 4], self.other)

    def fourth(self):
        self.copies.arrived(2)
        halves = []
        for part in self.parts:
            m3 = self.mine[part][2]
            for k, by in enumerate((1, 3)):
                half = self.held.at[part, self.core, (m3 - by + 4) % 4, pl.ds(2 * k, 2)]
                self.send(4, half, shifted(self.me, self.order[part][2], by))
                halves.append(half)
        for half in halves:
            self.send(7, half, self.other)

    def fifth(self):
        self.copies.arrived(3)
        for part in self.parts:
            m3 = self.mine[part][2]
            for k, by in enumerate((1, 3)):
                self.send(8, self.held.at[part, self.core, (m3 - by + 4) % 4, pl.ds(2 - 2 * k, 2)], self.other)

    def sixth(self):
        self.copies.arrived(4)
        for part in self.parts:
            for k in range(2):
                half = self.held.at[part, self.core, (self.mine[part][2] + 2) % 4, pl.ds(2 * k, 2)]
                self.send(9, half, self.other)

    def last(self):
        for kind in range(5, 10):
            self.copies.arrived(kind)
        self.copies.finish()


def tables():
    early = np.zeros((112, 128), np.float32)
    late = np.zeros((96, 128), np.float32)
    mlp = np.zeros((192, 192), np.float32)
    for i in range(8):
        early[96 + i, 16 * i + 12] = 1
        for t in range(6):
            for w in range(2):
                early[48 * w + 6 * i + t, 16 * i + 6 * w + t] = 1
                late[48 * w + 6 * i + t, 16 * i + 6 * w + t] = 1
            for w in range(4):
                mlp[48 * w + 6 * i + t, 24 * i + 6 * w + t] = 1
    lane, column = np.arange(128)[:, None], np.arange(WIDTH)[None]
    short = ((lane < 48) & (lane % 6 == column % 6)).astype(np.float32)
    short_owner = (lane == column // 6).astype(np.float32)
    inner = (lane - 48 == column % 24).astype(np.float32)
    inner_owner = (lane[:32] == column // 24).astype(np.float32)
    return early, late, mlp, short, short_owner, inner, inner_owner


def block_bias(query_pos, query_seg, key_pos, key_seg):
    allowed = (query_seg == key_seg) & (jnp.abs(query_pos - key_pos) <= HALF_WIN)
    return jnp.where(allowed, 0.0, NEG_FILL)


class Local:
    def __init__(self, sems):
        self.sems, self.started = sems, {}

    def start(self, number, source, target):
        self.started[number] = pltpu.make_async_copy(source, target, self.sems.at[number])
        self.started[number].start()

    def wait(self, *numbers):
        for number in numbers or list(self.started):
            self.started.pop(number).wait()


def eight(held, order, part, group):
    return [held[slab_index(order, part, slab_place(group, member))] for member in range(8)]


def forward_kernel(
    wq_part, wk_part, wv_part, wo_part, win_part, wout_part,
    bq_part, bv_part, bo_part, ga_part, ba_part, bout_part, go_part, bo2_part, binner_part, seg_ref, x_any,
    early_any, late_any, mlp_any, short_any, short_owner_any, inner_any, inner_owner_any,
    wq_any, wk_any, wv_any, wo_any, win_any, wout_any, q_any, qh_any, k_any, v_any,
    e0_any, e1_any, e2_any, mixed_any, inv_any, vec_ref, top_ref, segs_ref,
    wq, wk, wv, wo, win, wout, q, qh, k, v,
    held_e, held_l, held_m, rows, xh, bias, top_cols, e0, e1, e2, mixed, inverses,
    x_ref, early_ref, late_ref, pick_mlp_ref, short_ref, short_owner_ref, inner_ref, inner_owner_ref,
    sems_e, sems_l, sems_m, sems_h, out_sem, e_sem, load_sem,
):
    me = coords()
    side = lax.axis_index("seq")
    loads = Local(load_sem)
    for number, (source, target) in enumerate((
        (x_any, x_ref), (early_any, early_ref), (late_any, late_ref), (mlp_any, pick_mlp_ref), (short_any, short_ref),
        (short_owner_any, short_owner_ref), (inner_any, inner_ref), (inner_owner_any, inner_owner_ref),
    )):
        loads.start(number, source, target)
    short = (bq_part, bv_part, bo_part, ga_part, ba_part, bout_part, go_part, bo2_part)
    row = jnp.concatenate(
        [ref[...].astype(F32).reshape(1, 6) for ref in short]
        + [binner_part[...].astype(F32).reshape(1, 24), jnp.zeros((1, WIDTH - 72), F32)], axis=1,
    )
    early_rows = jnp.concatenate(
        [wk_part[...].astype(F32), wv_part[...].astype(F32), row, jnp.zeros((3, WIDTH), F32)], axis=0
    ).astype(BF)
    late_rows = jnp.concatenate(
        [wq_part[...].astype(F32), wo_part[...].astype(F32), jnp.zeros((4, WIDTH), F32)], axis=0
    ).astype(BF)
    for part in range(WIDES):
        held_e[slab_index(WIDE_ORDER, part, me)] = early_rows[:, WIDE * part : WIDE * (part + 1)]
        held_l[slab_index(WIDE_ORDER, part, me)] = late_rows[:, WIDE * part : WIDE * (part + 1)]
    greet(me)
    early = Gather(me, held_e, sems_e, WIDE_ORDER)
    late = Gather(me, held_l, sems_l, WIDE_ORDER)
    mlp = Gather(me, held_m, sems_m, ORDER)
    outs = Local(out_sem)
    partner = shifted(me, "z", 2)
    halo = Copies(sems_h, (xh, segs_ref.at[pl.ds(3, 2)]), partner)
    early.first()
    late.first()
    mlp_rows = jnp.concatenate(
        [win_part[:, WIDTH * n : WIDTH * (n + 1)].astype(F32) for n in range(4)]
        + [wout_part[...].astype(F32)], axis=0,
    ).astype(BF)
    for part in range(PARTS):
        held_m[slab_index(ORDER, part, me)] = mlp_rows[:, PART * part : PART * (part + 1)]
    mlp.first()
    for n in range(3):
        segs_ref[n] = jnp.broadcast_to(seg_ref[:, BLOCK * n : BLOCK * (n + 1)].astype(F32), (8, BLOCK))
    early.second()
    late.second()
    loads.wait()
    for n in range(2):
        block = jnp.where(side == 1, n, 2 - n)
        rows_out = x_ref.at[pl.ds(pl.multiple_of(block * BLOCK, BLOCK), BLOCK)]
        halo.send(0, rows_out, xh.at[pl.ds(n * BLOCK, BLOCK)], partner)
        halo.send(1, segs_ref.at[block], segs_ref.at[3 + n], partner)
    early.third()
    across = lax.broadcasted_iota(jnp.int32, (1, BLOCK), 1)
    down = lax.broadcasted_iota(jnp.int32, (BLOCK, 1), 0)
    starts = [BLOCK * n for n in range(3)] + [
        jnp.where(side == 0, 768 + BLOCK * n, -BLOCK * (n + 1)) for n in range(2)
    ]
    blocks = [jnp.where(side == 0, b, 2 - b) for b in range(3)]

    def fill_bias(b, key_blocks):
        seg_here = segs_ref[blocks[b], 0:1, :]
        seg_down = jnp.broadcast_to(seg_here, (128, BLOCK)).T[:, 0:1]
        for n in key_blocks:
            bias[b, :, pl.ds(n * BLOCK, BLOCK)] = block_bias(
                blocks[b] * BLOCK + down, seg_down, starts[n] + across, segs_ref[n, 0:1, :]
            )

    for b in range(3):
        fill_bias(b, range(3))
    early.fourth()
    late.third()
    early.fifth()
    early.sixth()
    late.fourth()
    early.last()
    mlp.second()

    def unpack_early(group, _):
        at = pl.ds(pl.multiple_of(group * 48, 16), 48)
        for part in range(WIDES):
            picked = dot(early_ref[...], jnp.concatenate(eight(held_e, WIDE_ORDER, part, group), axis=0))
            for n, ref in enumerate((wk, wv)):
                ref[at, pl.ds(part * WIDE, WIDE)] = picked[48 * n : 48 * n + 48].astype(BF)
            if part == 0:
                rows[pl.ds(pl.multiple_of(group * 8, 8), 8), :] = picked[96:104, :128]
        return 0

    lax.fori_loop(0, 16, unpack_early, 0, unroll=16)
    outs.start(0, wk, wk_any)
    outs.start(1, wv, wv_any)
    lane = lax.broadcasted_iota(jnp.int32, (1, 128), 1)
    for n in range(2):
        chosen = jnp.where((lane >= 6 * n) & (lane < 6 * n + 6), rows[...], 0.0).astype(BF)
        vec_ref[n : n + 1, :] = jnp.sum(
            dot(chosen, short_ref[...]) * short_owner_ref[...], axis=0, keepdims=True
        )
    def project_key(tokens, at):
        k[at, :] = dot(tokens[...], wk[...]).astype(BF)
        v[at, :] = (dot(tokens[...], wv[...]) + vec_ref[1:2, :]).astype(BF)

    def project_query(tokens, target):
        target[...] = (dot(tokens[...], wq[...]) + vec_ref[0:1, :]).astype(BF) * jnp.asarray(0.125, BF)

    late.fifth()
    late.sixth()
    project_key(x_ref, pl.ds(0, 768))
    late.last()

    def unpack_late(group, _):
        at = pl.ds(pl.multiple_of(group * 48, 16), 48)
        for part in range(WIDES):
            picked = dot(late_ref[...], jnp.concatenate(eight(held_l, WIDE_ORDER, part, group), axis=0))
            for n, ref in enumerate((wq, wo)):
                ref[at, pl.ds(part * WIDE, WIDE)] = picked[48 * n : 48 * n + 48].astype(BF)
        return 0

    lax.fori_loop(0, 16, unpack_late, 0, unroll=16)
    mlp.third()
    outs.start(2, wq, wq_any)
    outs.start(3, wo, wo_any)
    project_query(x_ref, q)
    outs.start(4, q, q_any)

    low = lane < 64

    slots, kept = (e0, e1, e2), (e0_any, e1_any, e2_any)

    def keep_copy(b, pair):
        slot = pair if b == 0 else pair % 2
        return pltpu.make_async_copy(slots[b].at[slot], kept[b].at[pair], e_sem.at[b, slot])

    def attend(pair, those, reused):
        columns = pl.ds(pl.multiple_of(pair * 128, 128), 128)
        items = [(b, e) for b in those for e in range(2)]
        if reused:
            for b in those:
                keep_copy(b, pair - 2).wait()

        def place(b):
            return pl.ds(pl.multiple_of(blocks[b] * BLOCK, BLOCK), BLOCK)

        def scores_of(b, e):
            count = 768 + BLOCK * b
            queries = jnp.where(low if e == 0 else ~low, q[place(b), columns], jnp.zeros((), BF))
            return dot(queries, k[pl.ds(0, count), columns], NT) + bias[b, :, pl.ds(0, count)]

        scores, outs_of = scores_of(*items[0]), []
        for n, (b, e) in enumerate(items):
            later = scores_of(*items[n + 1]) if n + 1 < len(items) else None
            top = jnp.max(scores, axis=1, keepdims=True)
            weights = jnp.exp(scores - top).astype(BF)
            slots[b][pair if b == 0 else pair % 2, pl.ds(BLOCK * e, BLOCK), :] = weights
            values = v[pl.ds(0, 768 + BLOCK * b), columns]
            outs_of.append(dot(weights, jnp.where(low if e == 0 else ~low, values, jnp.ones((), BF))))
            top_cols[place(b), :] = jnp.where(lane == 2 * pair + e, top, top_cols[place(b), :])
            scores = later
            if e == 1:
                inverse = 1.0 / pltpu.roll(jnp.where(low, outs_of[1], outs_of[0]), 64, 1)
                inverses[place(b), columns] = inverse
                mixed[place(b), columns] = (jnp.where(low, outs_of[0], outs_of[1]) * inverse).astype(BF)
                outs_of = []
        for b in those:
            keep_copy(b, pair).start()

    def near(pair, _):
        attend(pair, (0,), False)
        return 0

    def far_first(pair, _):
        attend(pair, (1, 2), False)
        return 0

    def far_next(pair, _):
        attend(pair, (1, 2), True)
        return 0

    lax.fori_loop(0, 6, near, 0, unroll=2)
    halo.arrived(0)
    halo.arrived(1)
    for b in range(1, 3):
        fill_bias(b, range(3, 3 + b))
    project_key(xh, pl.ds(768, 512))
    project_query(xh, qh)
    outs.start(5, qh, qh_any)
    outs.start(6, k, k_any)
    outs.start(7, v, v_any)
    mlp.fourth()
    mlp.fifth()
    lax.fori_loop(0, 2, far_first, 0, unroll=2)
    lax.fori_loop(2, 3, far_next, 0)
    mlp.sixth()
    lax.fori_loop(3, 4, far_next, 0)
    for n in range(2, 8):
        chosen = jnp.where((lane >= 6 * n) & (lane < 6 * n + 6), rows[...], 0.0).astype(BF)
        vec_ref[n : n + 1, :] = jnp.sum(
            dot(chosen, short_ref[...]) * short_owner_ref[...], axis=0, keepdims=True
        )
    for n in range(4):
        chosen = rows[pl.ds(32 * n, 32), :].astype(BF)
        vec_ref[8 + n : 9 + n, :] = jnp.sum(
            dot(chosen, inner_ref[...]) * inner_owner_ref[...], axis=0, keepdims=True
        )
    mlp.last()

    def unpack_mlp(group, _):
        at = pl.ds(pl.multiple_of(group * 48, 16), 48)
        at_outer = pl.ds(pl.multiple_of(group * 192, 64), 192)
        for part in range(PARTS):
            slabs = eight(held_m, ORDER, part, group)
            picked = dot(pick_mlp_ref[...], jnp.concatenate([slab[:24] for slab in slabs], axis=0)).astype(BF)
            for n in range(4):
                win[at, pl.ds(n * WIDTH + part * PART, PART)] = picked[48 * n : 48 * n + 48]
            wout[at_outer, pl.ds(part * PART, PART)] = jnp.concatenate([slab[24:] for slab in slabs], axis=0)
        return 0

    lax.fori_loop(0, 16, unpack_mlp, 0, unroll=8)
    outs.start(8, win, win_any)
    outs.start(9, wout, wout_any)
    lax.fori_loop(4, 6, far_next, 0, unroll=2)
    outs.start(10, mixed, mixed_any)
    outs.start(11, inverses, inv_any)
    for b in range(3):
        top_ref[b] = top_cols[pl.ds(b * BLOCK, BLOCK), :].T[:16]
        for pair in range(0 if b == 0 else 4, 6):
            keep_copy(b, pair).wait()
    halo.finish()
    outs.wait()


def run_forward(parts, tokens, seg_row):
    early, late, mlp, short, short_owner, inner, inner_owner = tables()
    fixed = (
        jnp.asarray(early, BF), jnp.asarray(late, BF), jnp.asarray(mlp, BF), jnp.asarray(short, BF),
        jnp.asarray(short_owner), jnp.asarray(inner, BF), jnp.asarray(inner_owner),
    )
    vmem, anywhere = pl.BlockSpec(memory_space=pltpu.VMEM), pl.BlockSpec(memory_space=pl.ANY)
    large = (
        [(768, 768)] * 4 + [(768, 3072), (3072, 768), (768, 768), (512, 768), (1280, 768), (1280, 768)]
    )
    kept = [(6, 2 * BLOCK, 768 + BLOCK * b) for b in range(3)]
    small = [((16, 768), F32), ((3, 16, BLOCK), F32), ((5, 8, BLOCK), F32)]
    per_pair = [((768, 768), BF), ((768, 768), F32)]
    sems = pltpu.SemaphoreType.DMA
    return pl.pallas_call(
        forward_kernel,
        out_shape=tuple(jax.ShapeDtypeStruct(shape, BF) for shape in large + kept)
        + tuple(jax.ShapeDtypeStruct(*shape) for shape in per_pair + small),
        in_specs=[vmem] * 16 + [anywhere] * 8,
        out_specs=(anywhere,) * len(large + kept + per_pair) + (vmem,) * len(small),
        scratch_shapes=[
            *(pltpu.VMEM(shape, BF) for shape in large),
            pltpu.VMEM((WIDES, 2, 4, 4, 4, ATTN_ROWS, WIDE), BF),
            pltpu.VMEM((WIDES, 2, 4, 4, 4, ATTN_ROWS, WIDE), BF),
            pltpu.VMEM((PARTS, 2, 4, 4, 4, MLP_ROWS, PART), BF),
            pltpu.VMEM((128, 128), F32),
            pltpu.VMEM((512, 768), BF),
            pltpu.VMEM((3, BLOCK, 1280), F32),
            pltpu.VMEM((768, 128), F32),
            *(pltpu.VMEM((6 if b == 0 else 2, *shape[1:]), BF) for b, shape in enumerate(kept)),
            *(pltpu.VMEM(*shape) for shape in per_pair),
            pltpu.VMEM((768, 768), BF), *(pltpu.VMEM(one.shape, one.dtype) for one in fixed),
            *(sems((2, Gather.KINDS)) for _ in range(3)), sems((2, 2)), sems((12,)), sems((3, 6)), sems((8,)),
        ],
        compiler_params=pltpu.CompilerParams(
            collective_id=0, has_side_effects=True, vmem_limit_bytes=VMEM_BYTES
        ),
        name="gather_and_attend",
    )(*parts, seg_row, tokens, *fixed)


class Scatter:
    KINDS = 8

    def __init__(self, me, parts, own, near, halves, blocks, second, first, sems, order):
        self.order, self.every = order, range(len(order))
        self.me, self.core = me, me["c"]
        self.parts, self.own, self.near, self.halves = parts, own, near, halves
        self.blocks, self.second, self.first = blocks, second, first
        self.other = shifted(me, "c", 1)
        sizes = (near.at[:, 0],) * 4 + (halves, blocks, second, first)
        self.copies = Copies(sems, sizes, self.other)
        self.mine = [tuple(me[axis] for axis in order[part]) for part in self.every]

    def add(self, target, sources, count):
        def body(index, _):
            if len(sources) == 1:
                target[index] = target[index] + sources[0][index]
            else:
                total = target[index].astype(F32)
                for source in sources:
                    total = total + source[index].astype(F32)
                target[index] = total.astype(BF)
            return 0

        lax.fori_loop(0, count, body, 0, unroll=count)

    def to_sibling(self):
        for k, by in enumerate((2, 1, 3, 0)):
            for part in self.every:
                at = (self.mine[part][2] + by) % 4
                self.copies.send(k, self.parts.at[part, 1 - self.core, at], self.near.at[part, at], self.other)

    def near_sum(self, k, by):
        self.copies.arrived(k)
        for part in self.every:
            at = (self.mine[part][2] + by) % 4
            self.add(self.near.at[part, at], [self.own(part, at)], 4)

    def opposite(self):
        self.near_sum(0, 2)
        for part in self.every:
            m3 = self.mine[part][2]
            for k, by in enumerate((1, 3)):
                half = self.near.at[part, (m3 + 2) % 4, pl.ds(2 * k, 2)]
                self.copies.send(4, half, self.halves.at[part, k], shifted(self.me, self.order[part][2], by))

    def nearest(self):
        self.near_sum(1, 1)
        self.near_sum(2, 3)
        self.near_sum(3, 0)

    def neighbours(self):
        self.copies.arrived(4)
        for part in self.every:
            m3 = self.mine[part][2]
            for k, by in enumerate((1, 3)):
                block = self.near.at[part, (m3 + by) % 4]
                self.add(block.at[pl.ds(2 * k, 2)], [self.halves.at[part, k]], 2)
                self.copies.send(5, block, self.blocks.at[part, k], shifted(self.me, self.order[part][2], by))

    def middle(self):
        self.copies.arrived(5)
        for part in self.every:
            m1, m2, m3 = self.mine[part]
            block = self.near.at[part, m3]
            self.add(block, [self.blocks.at[part, 0], self.blocks.at[part, 1]], 4)
            for k, by in enumerate(SHIFTS):
                self.copies.send(
                    6, block.at[(m2 + by) % 4], self.second.at[part, k], shifted(self.me, self.order[part][1], by)
                )

    def final(self):
        self.copies.arrived(6)
        for part in self.every:
            m1, m2, m3 = self.mine[part]
            block = self.near.at[part, m3, pl.ds(m2, 1)]
            self.add(block, [self.second.at[part, pl.ds(k, 1)] for k in range(3)], 1)
            for k, by in enumerate(SHIFTS):
                self.copies.send(
                    7, block.at[0, (m1 + by) % 4], self.first.at[part, k], shifted(self.me, self.order[part][0], by)
                )

    def result(self, out_ref):
        self.copies.arrived(7)
        for part in self.every:
            m1, m2, m3 = self.mine[part]
            total = self.near[part, m3, m2, m1].astype(F32)
            for k in range(3):
                total = total + self.first[part, k].astype(F32)
            out_ref[part] = total
        self.copies.finish()


def row_sum(block):
    return jnp.sum(block, axis=0, keepdims=True)


def normed_of(hidden):
    centred = hidden - jnp.mean(hidden, axis=1, keepdims=True)
    inverse = lax.rsqrt(jnp.mean(centred * centred, axis=1, keepdims=True) + EPS)
    return centred * inverse, inverse


def dense_kernel(
    x_any, mixed_any, cot_any, wo_any, win_any, wout_any, inv_any, vec_ref, put_mlp_ref, heads_ref,
    out_any, dwo_any, hidden_any, gmix_any, parts_any, delta_ref, sums_ref,
    x, mixed, cot, wo, win, wout, inv, out, gmix, parts,
    active, slope, normed, inverse, first_bf, total, grad_bf, load_sem, store_sem, chunk_sem,
):
    loads, stores = Local(load_sem), Local(store_sem)
    for n, (source, target) in enumerate(((mixed_any, mixed), (wo_any, wo), (x_any, x))):
        loads.start(n, source, target)

    def chunk_loads(index):
        columns = pl.ds(pl.multiple_of(index * WIDTH, WIDTH), WIDTH)
        return (
            pltpu.make_async_copy(win_any.at[:, columns], win.at[:, columns], chunk_sem.at[0, index]),
            pltpu.make_async_copy(wout_any.at[columns], wout.at[columns], chunk_sem.at[1, index]),
        )

    sums_ref[...] = jnp.zeros_like(sums_ref)

    def add_sum(row, block):
        sums_ref[pl.ds(row, 1), :] += row_sum(block)

    def row_block(index):
        return pl.ds(pl.multiple_of(index * BLOCK, BLOCK), BLOCK)

    loads.wait(0, 1, 2)
    for n in range(4):
        for one in chunk_loads(n):
            one.start()
    loads.start(3, cot_any, cot)
    loads.start(4, inv_any, inv)

    def branch_of(index):
        return dot(mixed[row_block(index), :], wo[...]) + vec_ref[2:3, :]

    branch = branch_of(0)
    for n in range(3):
        later = branch_of(n + 1) if n < 2 else None
        at = row_block(n)
        normed[at, :], spread = normed_of(x[at, :].astype(F32) + branch)
        inverse[at, :] = jnp.broadcast_to(spread, (BLOCK, 128))
        first_bf[at, :] = (normed[at, :] * vec_ref[3:4, :] + vec_ref[4:5, :]).astype(BF)
        branch = later
    rate, bend = math.sqrt(2 / math.pi), 0.044715

    PIECE = 256

    def inner_of(n):
        columns = slice(PIECE * n, PIECE * (n + 1))
        chunk, rest = PIECE * n // WIDTH, PIECE * n % WIDTH
        if rest == 0:
            for one in chunk_loads(chunk):
                one.wait()
        return dot(first_bf[...], win[:, columns]) + vec_ref[8 + chunk : 9 + chunk, rest : rest + PIECE]

    u = inner_of(0)
    for n in range(4 * WIDTH // PIECE):
        later = inner_of(n + 1) if PIECE * (n + 1) < 4 * WIDTH else None
        columns = slice(PIECE * n, PIECE * (n + 1))
        square = u * u
        bent = jnp.tanh(rate * u * (1 + bend * square))
        half = 0.5 * (1 + bent)
        raised = u * half
        active[:, columns] = raised.astype(BF)
        slope[:, columns] = (half + raised * (1 - bent) * (rate + (3 * rate * bend) * square)).astype(BF)
        if PIECE * (n + 1) % WIDTH == 0:
            chunk = slice(PIECE * (n + 1) - WIDTH, PIECE * (n + 1))
            outer = dot(active[:, chunk], wout[chunk, :])
            total[...] = outer if chunk.start == 0 else total[...] + outer
        u = later

    def norm_two(index, _):
        at = row_block(index)
        first = normed[at, :] * vec_ref[3:4, :] + vec_ref[4:5, :]
        normed_two, spread = normed_of(first + (total[at, :] + vec_ref[5:6, :]))
        out[at, :] = (normed_two * vec_ref[6:7, :] + vec_ref[7:8, :]).astype(BF)
        grad = cot[at, :].astype(F32)
        add_sum(6, grad * normed_two)
        add_sum(7, grad)
        scaled = grad * vec_ref[6:7, :]
        mean_grad = jnp.mean(scaled, axis=1, keepdims=True)
        mean_cross = jnp.mean(scaled * normed_two, axis=1, keepdims=True)
        back = spread * (scaled - mean_grad - normed_two * mean_cross)
        total[at, :] = back
        grad_bf[at, :] = back.astype(BF)
        add_sum(5, grad_bf[at, :].astype(F32))
        return 0

    loads.wait(3)
    lax.fori_loop(0, 3, norm_two, 0, unroll=3)
    stores.start(0, out, out_any)

    def outer_block(index, _):
        columns = pl.ds(pl.multiple_of(index * WIDTH, WIDTH), WIDTH)
        grad_inner = (dot(grad_bf[...], wout[columns, :], NT) * slope[:, columns].astype(F32)).astype(BF)
        add_sum(8 + index, grad_inner.astype(F32))
        total[...] += dot(grad_inner, win[:, columns], NT)
        active[:, columns] = dot(active[:, columns], grad_bf[...], TN).astype(BF)
        slope[:, columns] = dot(first_bf[...], grad_inner, TN).astype(BF)
        return 0

    lax.fori_loop(0, 4, outer_block, 0)

    for part in range(WIDES):

        def pack(group, _):
            at = pl.ds(pl.multiple_of(group * 48, 16), 48)
            at_outer = pl.ds(pl.multiple_of((group % 4) * 192, 64), 192)
            pieces = [slope[at, pl.ds(k * WIDTH + part * WIDE, WIDE)] for k in range(4)]
            placed = dot(put_mlp_ref[...], jnp.concatenate(pieces, axis=0)).astype(BF)
            outer_columns = pl.ds(pl.multiple_of((group // 4) * WIDTH + part * WIDE, 128), WIDE)
            outer = active[at_outer, outer_columns]
            for member in range(8):
                these = slice(24 * member, 24 * member + 24)
                parts[slab_index(BACK_ORDER, part, slab_place(group, member))] = jnp.concatenate(
                    [placed[these], outer[these]], axis=0
                )
            return 0

        lax.fori_loop(0, 16, pack, 0, unroll=8)
        stores.start(4 + part, parts.at[part], parts_any.at[part])

    def back_one(index, _):
        at = row_block(index)
        grad, normed_one = total[at, :], normed[at, :]
        add_sum(3, grad * normed_one)
        add_sum(4, grad)
        scaled = grad * vec_ref[3:4, :]
        mean_grad = jnp.mean(scaled, axis=1, keepdims=True)
        mean_cross = jnp.mean(scaled * normed_one, axis=1, keepdims=True)
        back = inverse[at, 0:1] * (scaled - mean_grad - normed_one * mean_cross)
        total[at, :] = back
        grad_bf[at, :] = back.astype(BF)
        add_sum(2, grad_bf[at, :].astype(F32))
        return 0

    lax.fori_loop(0, 3, back_one, 0, unroll=3)
    stores.start(1, total, hidden_any)
    loads.wait(4)
    gmix[...] = (dot(grad_bf[...], wo[...], NT) * inv[...]).astype(BF)
    stores.start(2, gmix, gmix_any)
    first_bf[...] = dot(mixed[...], grad_bf[...], TN).astype(BF)
    stores.start(3, first_bf, dwo_any)

    for k in range(3):
        at = pl.ds(BLOCK * k, BLOCK)
        product = mixed[at, :].astype(F32) * gmix[at, :].astype(F32)
        high = product.astype(BF)
        rest = (product - high.astype(F32)).astype(BF)
        delta_ref[k] = dot(heads_ref[...], high, NT) + dot(heads_ref[...], rest, NT)
    stores.wait()


def run_dense(tokens, mixed, cot, wo, win, wout, inv, vec):
    mlp = tables()[2]
    heads = (np.arange(16)[:, None] == np.arange(WIDTH)[None] // 64).astype(np.float32)
    vmem, anywhere = pl.BlockSpec(memory_space=pltpu.VMEM), pl.BlockSpec(memory_space=pl.ANY)
    parts_shape = (WIDES, 2, 4, 4, 4, MLP_ROWS, WIDE)
    shapes = (
        ((768, 768), BF), ((768, 768), BF), ((768, 768), F32), ((768, 768), BF), (parts_shape, BF),
        ((3, 16, BLOCK), F32), ((16, 768), F32),
    )
    sems = pltpu.SemaphoreType.DMA
    return pl.pallas_call(
        dense_kernel,
        out_shape=tuple(jax.ShapeDtypeStruct(*shape) for shape in shapes),
        in_specs=[anywhere] * 7 + [vmem] * 3,
        out_specs=(anywhere,) * 5 + (vmem,) * 2,
        scratch_shapes=[
            *(pltpu.VMEM((768, 768), BF) for _ in range(4)),
            pltpu.VMEM((768, 3072), BF), pltpu.VMEM((3072, 768), BF), pltpu.VMEM((768, 768), F32),
            pltpu.VMEM((768, 768), BF), pltpu.VMEM((768, 768), BF), pltpu.VMEM(parts_shape, BF),
            pltpu.VMEM((768, 3072), BF), pltpu.VMEM((768, 3072), BF), pltpu.VMEM((768, 768), F32),
            pltpu.VMEM((768, 128), F32), pltpu.VMEM((768, 768), BF), pltpu.VMEM((768, 768), F32),
            pltpu.VMEM((768, 768), BF), sems((5,)), sems((7,)), sems((2, 4)),
        ],
        compiler_params=pltpu.CompilerParams(vmem_limit_bytes=VMEM_BYTES),
        name="feed_forward",
    )(tokens, mixed, cot, wo, win, wout, inv, vec, jnp.asarray(mlp.T, BF), jnp.asarray(heads, BF))


def backward_kernel(
    q_any, qh_any, k_any, v_any, g_any, x_any, wq_any, wk_any, wv_any, hidden_any, mlp_any,
    e0_any, e1_any, e2_any, dwo_any, put_early_any, put_late_any, short_any, short_owner_any, inner_any,
    inner_owner_any, top_ref, delta_ref, segs_ref, sums_ref,
    grad_any, early_out, late_out, mlp_out,
    q, qh, k, v, g, gh, stats, stat_cols, own_m, e0, e1, e2, bias, dq, dk, dv, grad_k, grad_v,
    dw, dwv, rows, hidden,
    dwo_ref, put_early_ref, put_late_ref, short_ref, short_owner_ref, inner_ref, inner_owner_ref,
    parts, near_e, halves_e, blocks_e, second_e, first_e,
    near_l, halves_l, blocks_l, second_l, first_l,
    near_m, halves_m, blocks_m, second_m, first_m,
    load_sem, e_sem, sems_e, sems_l, sems_m, sems_h,
):
    me = coords()
    core = me["c"]
    side = lax.axis_index("seq")
    partner = shifted(me, "z", 2)
    loads = Local(load_sem)
    kept, slots = (e0_any, e1_any, e2_any), (e0, e1, e2)

    def keep_copy(b, pair):
        return pltpu.make_async_copy(kept[b].at[pair], slots[b].at[pair % 2], e_sem.at[b, pair % 2])

    for number, (source, target) in enumerate(((g_any, g), (v_any, v), (q_any, q), (k_any, k))):
        loads.start(number, source, target)
    for b in range(3):
        keep_copy(b, 0).start()
    for b in range(3):
        stats[b, 0:16, :] = top_ref[b]
        stats[b, 16:32, :] = delta_ref[b]

    def turn(block):
        both = jnp.concatenate([stats[block], jnp.zeros((96, BLOCK), F32)], axis=0)
        stat_cols[block] = both.T

    for b in range(3):
        turn(b)
    across = lax.broadcasted_iota(jnp.int32, (1, BLOCK), 1)
    down = lax.broadcasted_iota(jnp.int32, (BLOCK, 1), 0)
    blocks = [jnp.where(side == 0, b, 2 - b) for b in range(3)]
    reach = [
        (jnp.where(side == 0, BLOCK * (1 + n), 0), BLOCK * (2 - n)) for n in range(2)
    ]

    def fill_bias():
        for n in range(2):
            seg_down = jnp.broadcast_to(segs_ref[3 + n, 0:1, :], (128, BLOCK)).T[:, 0:1]
            start = jnp.where(side == 0, 768 + BLOCK * n, -BLOCK * (n + 1))
            for m in range(2 - n):
                block = jnp.where(side == 0, 1 + n + m, m)
                bias[n, :, pl.ds(m * BLOCK, BLOCK)] = block_bias(
                    start + down, seg_down, block * BLOCK + across, segs_ref[block, 0:1, :]
                )

    fill_bias()
    dk[...] = jnp.zeros_like(dk)
    dv[...] = jnp.zeros_like(dv)
    greet(me)
    mlp = Scatter(
        me, mlp_any, lambda part, at: own_m.at[part, at], near_m, halves_m, blocks_m, second_m, first_m,
        sems_m, BACK_ORDER,
    )
    early = Scatter(
        me, parts, lambda part, at: parts.at[part, core, at], near_e, halves_e, blocks_e, second_e,
        first_e, sems_e, ORDER,
    )
    late = Scatter(
        me, parts, lambda part, at: parts.at[part, core, at], near_l, halves_l, blocks_l, second_l,
        first_l, sems_l, ORDER,
    )
    halo = Copies(sems_h, (gh, stats.at[pl.ds(3, 2)]), partner)
    loads.wait(0)
    for n in range(2):
        block = jnp.where(side == 1, n, 2 - n)
        rows_out = g.at[pl.ds(pl.multiple_of(block * BLOCK, BLOCK), BLOCK)]
        halo.send(0, rows_out, gh.at[pl.ds(n * BLOCK, BLOCK)], partner)
        halo.send(1, stats.at[block], stats.at[3 + n], partner)
    mlp.to_sibling()

    loads.start(5, mlp_any.at[:, core], own_m)
    loads.start(4, qh_any, qh)
    for number, (source, target) in enumerate((
        (dwo_any, dwo_ref), (put_early_any, put_early_ref), (put_late_any, put_late_ref), (short_any, short_ref),
        (short_owner_any, short_owner_ref), (inner_any, inner_ref), (inner_owner_any, inner_owner_ref),
    ), 12):
        loads.start(number, source, target)
    loads.start(6, hidden_any, hidden)
    lane = lax.broadcasted_iota(jnp.int32, (1, 128), 1)
    low = lane < 64
    high_rows = lax.broadcasted_iota(jnp.int32, (128, 1), 0) >= 64
    nothing = jnp.zeros((), BF)

    def one_head(block, e):
        return jnp.where(low if e == 0 else ~low, block, nothing)

    def two_heads(turned):
        return jnp.concatenate(
            [jnp.where(high_rows, nothing, turned), jnp.where(high_rows, turned, nothing)], axis=1
        )

    def stat(block, row):
        return jnp.sum(jnp.where(lane == row, stat_cols[block], 0.0), axis=1, keepdims=True)

    def own_pair(pair, ahead):
        columns = pl.ds(pl.multiple_of(pair * 128, 128), 128)
        here = pl.ds(pl.multiple_of(pair * 128, 128), 128)
        for b in range(3):
            keep_copy(b, pair).wait()
        if ahead:
            for b in range(3):
                keep_copy(b, pair + 1).start()

        def place(b):
            return pl.ds(pl.multiple_of(blocks[b] * BLOCK, BLOCK), BLOCK)

        def products(b):
            values = v[pl.ds(0, 768 + BLOCK * b), columns]
            return [dot(one_head(g[place(b), columns], e), values, NT) for e in range(2)]

        grad_weights = products(0)
        for b in range(3):
            later = products(b + 1) if b < 2 else None
            weights = slots[b].at[pair % 2]
            grad_scores = [
                (
                    weights[pl.ds(BLOCK * e, BLOCK), :].astype(F32)
                    * (grad_weights[e] - stat(blocks[b], 16 + 2 * pair + e))
                ).astype(BF)
                for e in range(2)
            ]
            own = jnp.concatenate([block[:, :768] for block in grad_scores], axis=0)
            dk[here, :] += dot(two_heads(q[place(b), columns].T), own)
            dv[here, :] += dot(two_heads(g[place(b), columns].T), weights[:, pl.ds(0, 768)])
            keys = k[pl.ds(0, 768 + BLOCK * b), columns]
            grad_query = dot(grad_scores[0], one_head(keys, 0)) + dot(grad_scores[1], one_head(keys, 1))
            dq[place(b), columns] = (grad_query * 0.125).astype(BF)
            grad_weights = later

    def own_next(pair, _):
        own_pair(pair, True)
        return 0

    def own_last(pair, _):
        own_pair(pair, False)
        return 0

    def halo_pair(pair, _):
        columns = pl.ds(pl.multiple_of(pair * 128, 128), 128)
        here = pl.ds(pl.multiple_of(pair * 128, 128), 128)
        items = [(n, e) for n in range(2) for e in range(2)]

        def keys_at(n):
            return pl.ds(pl.multiple_of(reach[n][0], BLOCK), reach[n][1])

        def products(n, e):
            those = pl.ds(n * BLOCK, BLOCK)
            scores = dot(one_head(qh[those, columns], e), k[keys_at(n), columns], NT)
            grad_weights = dot(one_head(gh[those, columns], e), v[keys_at(n), columns], NT)
            return scores + bias[n, :, pl.ds(0, reach[n][1])], grad_weights

        ready = [products(*item) for item in items]
        for n in range(2):
            weights, grad_scores = [], []
            for e in range(2):
                scores, grad_weights = ready[2 * n + e]
                raised = jnp.exp(scores - stat(3 + n, 2 * pair + e))
                weights.append(raised.astype(BF))
                grad_scores.append((raised * (grad_weights - stat(3 + n, 16 + 2 * pair + e))).astype(BF))
            those = pl.ds(n * BLOCK, BLOCK)
            dk[here, keys_at(n)] += dot(two_heads(qh[those, columns].T), jnp.concatenate(grad_scores, axis=0))
            dv[here, keys_at(n)] += dot(two_heads(gh[those, columns].T), jnp.concatenate(weights, axis=0))
        grad_k[:, columns] = dk[here, :].T.astype(BF)
        grad_v[:, columns] = dv[here, :].T.astype(BF)
        return 0

    loads.wait(1, 2, 3)
    lax.fori_loop(0, 1, own_next, 0)
    loads.wait(5)
    mlp.opposite()
    lax.fori_loop(1, 3, own_next, 0)
    mlp.nearest()
    lax.fori_loop(3, 4, own_next, 0)
    loads.wait(15, 16, 17, 18)
    rows[...] = jnp.zeros_like(rows)
    for n in range(2, 8):
        spread = dot((short_owner_ref[...] * sums_ref[n : n + 1, :]).astype(BF), short_ref[...], NT)
        rows[...] = jnp.where((lane >= 6 * n) & (lane < 6 * n + 6), spread, rows[...])
    for n in range(4):
        spread = dot((inner_owner_ref[...] * sums_ref[8 + n : 9 + n, :]).astype(BF), inner_ref[...], NT)
        at = pl.ds(32 * n, 32)
        rows[at, :] = jnp.where((lane >= 48) & (lane < 72), spread, rows[at, :])
    mlp.neighbours()
    lax.fori_loop(4, 5, own_next, 0)
    lax.fori_loop(5, 6, own_last, 0)
    halo.finish()
    loads.start(7, x_any, g)
    loads.start(8, wq_any, q)
    loads.wait(7, 12, 13, 14)
    dw[...] = dot(g[...], dq[...], TN).astype(BF)

    def pack_late(group, _):
        at = pl.ds(pl.multiple_of(group * 48, 16), 48)
        for part in range(PARTS):
            columns = pl.ds(part * PART, PART)
            pieces = jnp.concatenate([dw[at, columns], dwo_ref[at, columns]], axis=0)
            placed = dot(put_late_ref[...], pieces).astype(BF)
            for member in range(8):
                parts[slab_index(ORDER, part, slab_place(group, member))] = placed[16 * member : 16 * member + 16]
        return 0

    lax.fori_loop(0, 16, pack_late, 0, unroll=16)
    late.to_sibling()
    halo.arrived(0)
    halo.arrived(1)
    for n in range(2):
        turn(3 + n)
    loads.wait(4)
    lax.fori_loop(0, 2, halo_pair, 0, unroll=2)
    late.opposite()
    late.nearest()
    lax.fori_loop(2, 4, halo_pair, 0, unroll=2)
    mlp.middle()
    late.neighbours()
    lax.fori_loop(4, 6, halo_pair, 0, unroll=2)
    loads.start(9, wk_any, k.at[pl.ds(0, 768)])
    loads.start(10, wv_any, v.at[pl.ds(0, 768)])
    dw[...] = dot(g[...], grad_k[...], TN).astype(BF)
    dwv[...] = dot(g[...], grad_v[...], TN).astype(BF)

    for n, grad in ((0, dq), (1, grad_v)):
        spread = dot((short_owner_ref[...] * row_sum(grad[...].astype(F32))).astype(BF), short_ref[...], NT)
        rows[...] = jnp.where((lane >= 6 * n) & (lane < 6 * n + 6), spread, rows[...])

    def pack_early(group, _):
        at = pl.ds(pl.multiple_of(group * 48, 16), 48)
        vec = rows[pl.ds(pl.multiple_of(group * 8, 8), 8), :]
        vec = jnp.concatenate([vec, jnp.zeros_like(vec)], axis=1)
        vec = jnp.concatenate([vec, jnp.zeros_like(vec)], axis=0).astype(BF)
        for part in range(PARTS):
            columns = pl.ds(part * PART, PART)
            last = vec if part == 0 else jnp.zeros_like(vec)
            pieces = jnp.concatenate([dw[at, columns], dwv[at, columns], last], axis=0)
            placed = dot(put_early_ref[...], pieces).astype(BF)
            for member in range(8):
                parts[slab_index(ORDER, part, slab_place(group, member))] = placed[16 * member : 16 * member + 16]
        return 0

    late.copies.sent(0, 1, 2, 3)
    lax.fori_loop(0, 16, pack_early, 0, unroll=16)
    early.to_sibling()
    loads.wait(6, 8)
    hidden[...] += dot(dq[...], q[...], NT)
    early.opposite()
    early.nearest()
    mlp.final()
    loads.wait(9)
    hidden[...] += dot(grad_k[...], k[pl.ds(0, 768), :], NT)
    late.middle()
    early.neighbours()
    loads.wait(10)
    hidden[...] += dot(grad_v[...], v[pl.ds(0, 768), :], NT)
    loads.start(11, hidden, grad_any)
    early.middle()
    late.final()
    early.final()
    mlp.result(mlp_out)
    late.result(late_out)
    early.result(early_out)
    loads.wait()


def run_backward(q, qh, k, v, g, x, wq, wk, wv, hidden, mlp, kept, top, delta, segs, dwo, sums):
    early, late, _, short, short_owner, inner, inner_owner = tables()
    fixed = (
        jnp.asarray(early.T, BF), jnp.asarray(late.T, BF), jnp.asarray(short, BF),
        jnp.asarray(short_owner), jnp.asarray(inner, BF), jnp.asarray(inner_owner),
    )
    vmem, anywhere = pl.BlockSpec(memory_space=pltpu.VMEM), pl.BlockSpec(memory_space=pl.ANY)
    sems = pltpu.SemaphoreType.DMA

    def steps(parts, rows, width):
        return [
            pltpu.VMEM((parts, *lead, rows, width), BF)
            for lead in ((4, 4, 4), (2, 2, 4), (2, 4, 4), (3, 4), (3,))
        ]

    return pl.pallas_call(
        backward_kernel,
        out_shape=(
            jax.ShapeDtypeStruct((768, 768), F32),
            jax.ShapeDtypeStruct((PARTS, ATTN_ROWS, PART), F32),
            jax.ShapeDtypeStruct((PARTS, ATTN_ROWS, PART), F32),
            jax.ShapeDtypeStruct((WIDES, MLP_ROWS, WIDE), F32),
        ),
        in_specs=[anywhere] * 21 + [vmem] * 4,
        out_specs=(anywhere, vmem, vmem, vmem),
        scratch_shapes=[
            pltpu.VMEM((768, 768), BF), pltpu.VMEM((512, 768), BF),
            pltpu.VMEM((1280, 768), BF), pltpu.VMEM((1280, 768), BF),
            pltpu.VMEM((768, 768), BF), pltpu.VMEM((512, 768), BF),
            pltpu.VMEM((5, 32, BLOCK), F32), pltpu.VMEM((5, BLOCK, 128), F32),
            pltpu.VMEM((WIDES, 4, 4, 4, MLP_ROWS, WIDE), BF),
            *(pltpu.VMEM((2, *one.shape[1:]), BF) for one in kept), pltpu.VMEM((2, BLOCK, 512), F32),
            pltpu.VMEM((768, 768), BF), pltpu.VMEM((768, 768), F32), pltpu.VMEM((768, 768), F32),
            *(pltpu.VMEM((768, 768), BF) for _ in range(4)),
            pltpu.VMEM((128, 128), F32), pltpu.VMEM((768, 768), F32), pltpu.VMEM((768, 768), BF),
            *(pltpu.VMEM(one.shape, one.dtype) for one in fixed),
            pltpu.VMEM((PARTS, 2, 4, 4, 4, ATTN_ROWS, PART), BF),
            *steps(PARTS, ATTN_ROWS, PART), *steps(PARTS, ATTN_ROWS, PART), *steps(WIDES, MLP_ROWS, WIDE),
            sems((19,)), sems((3, 2)), *(sems((2, Scatter.KINDS)) for _ in range(3)), sems((2, 2)),
        ],
        compiler_params=pltpu.CompilerParams(
            collective_id=1, has_side_effects=True, vmem_limit_bytes=VMEM_BYTES
        ),
        name="attend_back_and_scatter",
    )(q, qh, k, v, g, x, wq, wk, wv, hidden, mlp, *kept, dwo, *fixed, top, delta, segs, sums)


def split_kernel(early_any, late_any, mlp_any, grad_any, grad_out, wq, wk, wv, wo, win, wout, inner, *rest):
    short, (early, late, mlp, staged, sums_sem, sems) = rest[:8], rest[8:]
    moves, sums = [], Local(sums_sem)
    for k in range(3):
        at = pl.ds(BLOCK * k, BLOCK)
        moves.append([
            pltpu.make_async_copy(grad_any.at[at], staged.at[at], sems.at[0, k]),
            pltpu.make_async_copy(staged.at[at], grad_out.at[at], sems.at[1, k]),
        ])
        moves[k][0].start()
    for number, (source, target) in enumerate(((early_any, early), (late_any, late), (mlp_any, mlp))):
        sums.start(number, source, target)
    for fetch, put in moves:
        fetch.wait()
        put.start()
    sums.wait()
    for part in range(PARTS):
        columns = pl.ds(PART * part, PART)
        for ref, source, row in ((wk, early, 0), (wv, early, 6), (wq, late, 0), (wo, late, 6)):
            ref[:, columns] = source[part, row : row + 6, :]
    for part in range(WIDES):
        for k in range(4):
            win[:, pl.ds(WIDTH * k + WIDE * part, WIDE)] = mlp[part, 6 * k : 6 * k + 6, :]
        wout[:, pl.ds(WIDE * part, WIDE)] = mlp[part, 24:48, :]
    inner[...] = early[0, 12, 48:72]
    for k in range(8):
        short[k][...] = early[0, 12, 6 * k : 6 * k + 6]
    for fetch, put in moves:
        put.wait()


def split_results(early, late, mlp, grad):
    vmem, anywhere = pl.BlockSpec(memory_space=pltpu.VMEM), pl.BlockSpec(memory_space=pl.ANY)
    shapes = ((768, 768),) + ((6, 768),) * 4 + ((6, 3072), (24, 768), (24,)) + ((6,),) * 8
    return pl.pallas_call(
        split_kernel,
        out_shape=tuple(jax.ShapeDtypeStruct(shape, F32) for shape in shapes),
        in_specs=[anywhere] * 4,
        out_specs=(anywhere,) + (vmem,) * (len(shapes) - 1),
        scratch_shapes=[
            *(pltpu.VMEM(one.shape, F32) for one in (early, late, mlp)), pltpu.VMEM((768, 768), F32),
            pltpu.SemaphoreType.DMA((3,)), pltpu.SemaphoreType.DMA((2, 3)),
        ],
        compiler_params=pltpu.CompilerParams(vmem_limit_bytes=VMEM_BYTES),
        name="split_gradients",
    )(early, late, mlp, grad)


def per_device(
    inputs,
    segments,
    w_query,
    w_key,
    w_value,
    w_output,
    b_query,
    b_value,
    b_output,
    gain_attn,
    bias_attn,
    w_inner,
    b_inner,
    w_outer,
    b_outer,
    gain_out,
    bias_out,
    cotangent,
):
    tokens = inputs.reshape(768, 768)
    short = (b_query, b_value, b_output, gain_attn, bias_attn, b_outer, gain_out, bias_out)
    parts = (w_query, w_key, w_value, w_output, w_inner, w_outer, *short, b_inner)
    wq, wk, wv, wo, win, wout, q, qh, k, v, *kept, mixed, inv, vec, top, segs = run_forward(parts, tokens, segments)
    out, dwo, hidden, gmix, mlp, delta, sums = run_dense(
        tokens, mixed, cotangent.reshape(768, 768), wo, win, wout, inv, vec
    )
    grad_input, early_sum, late_sum, mlp_sum = run_backward(
        q, qh, k, v, gmix, tokens, wq, wk, wv, hidden, mlp, kept, top, delta, segs, dwo, sums
    )
    grad_input, dwq, dwk, dwv, dwo, dwin, dwout, inner, *short = split_results(
        early_sum, late_sum, mlp_sum, grad_input
    )
    return (
        out.reshape(1, 768, 768),
        grad_input.reshape(1, 768, 768),
        dwq,
        dwk,
        dwv,
        dwo,
        *short[:5],
        dwin,
        inner,
        dwout,
        *short[5:],
    )


def solution(mesh):
    return jax.shard_map(
        per_device,
        mesh=mesh,
        in_specs=(
            P("dp", "seq", None),
            P("dp", "seq"),
            P(("seq", "dp"), None),
            P(("seq", "dp"), None),
            P(("seq", "dp"), None),
            P(("seq", "dp"), None),
            P(("seq", "dp")),
            P(("seq", "dp")),
            P(("seq", "dp")),
            P(("seq", "dp")),
            P(("seq", "dp")),
            P(("seq", "dp"), None),
            P(("seq", "dp")),
            P(("seq", "dp"), None),
            P(("seq", "dp")),
            P(("seq", "dp")),
            P(("seq", "dp")),
            P("dp", "seq", None),
        ),
        out_specs=(
            P("dp", "seq", None),
            P("dp", "seq", None),
            P(("seq", "dp"), None),
            P(("seq", "dp"), None),
            P(("seq", "dp"), None),
            P(("seq", "dp"), None),
            P(("seq", "dp")),
            P(("seq", "dp")),
            P(("seq", "dp")),
            P(("seq", "dp")),
            P(("seq", "dp")),
            P(("seq", "dp"), None),
            P(("seq", "dp")),
            P(("seq", "dp"), None),
            P(("seq", "dp")),
            P(("seq", "dp")),
            P(("seq", "dp")),
        ),
        check_vma=False,
    )
```
